512 devices in a mesh: lat: 16 (over x_lo, z), lon: 32 (over x_hi, y, core).
Axes of the slice: x: 4 (x_hi: 2, x_lo: 2; x = x_hi * 2 + x_lo), y: 8, z: 8, core: 2. Of those that a mesh axis runs over, the one named last changes fastest.
Arguments:
- fields: bfloat16 [75, 128, 4096], P(None, 'lat', 'lon'), may hold values from -6 to 6
- mask: int32 [128, 4096], P('lat', 'lon'), may hold values from 0 to 1, as said below
- w1: bfloat16 [9, 48, 75], replicated, may hold values from -0.25 to 0.25
- w2: bfloat16 [9, 48, 48], replicated, may hold values from -0.3125 to 0.3125
- cotangent: bfloat16 [48, 128, 4096], P(None, 'lat', 'lon'), may hold values from -6 to 6
Outputs:
- output: bfloat16 [48, 128, 4096], P(None, 'lat', 'lon')
- dx: bfloat16 [75, 128, 4096], P(None, 'lat', 'lon')
- dw1: float32 [9, 48, 75], replicated
- dw2: float32 [9, 48, 48], replicated
The draws below stay inside these ranges and needn't reach their ends.
Inputs may be any that keep to these rules, and one draw needn't show every extreme that they name: `mask`: rows below 8 are sea. Each aligned block of 8 x 8 grid points is all land or all sea.
All inputs are finite; a program needn't handle non-finite values.
Results may differ from the reference program's by a relative error of at most 0.017.
Values may be sent and summed in bfloat16 or wider, within the bound.
A program may use at most 64 MiB of HBM per device.

```python
import math
import jax
import jax.numpy as jnp

CIN = 75
CH = 48
NY = 128
NX = 4096


def draw_mask(key, part):
    blocks = jax.random.randint(key, (NY // 8, NX // 8), 0, 10)
    sea = (blocks >= 3).astype(jnp.int32)
    sea = jnp.repeat(jnp.repeat(sea, 8, axis=0), 8, axis=1)
    rows_idx = jnp.arange(NY, dtype=jnp.int32)[:, None]
    return jnp.where(rows_idx < 8, 1, sea).astype(jnp.int32)


def block_scale(rng, extent, pieces, low, top_value):
    loudness = 1.0
    for dim, parts in pieces:
        heights = jax.random.uniform(jax.random.fold_in(jax.random.fold_in(rng, 6), dim), (parts,), jnp.float32, low / len(pieces), top_value / len(pieces))
        loudness = loudness * jnp.repeat(jnp.exp(heights), extent[dim] // parts).reshape((-1,) + (1,) * (len(extent) - 1 - dim))
    return loudness


def noise(stream_key, shape, scale, reach, cuts=(), kind=jnp.bfloat16):
    gain = block_scale(stream_key, shape, cuts, -0.22, 0.18) if cuts else 1.0
    values = jax.random.normal(stream_key, shape, jnp.float32) * scale * gain
    return jnp.minimum(jnp.maximum(values, -reach), reach).astype(kind)


def setup_inputs(seed: int = 0) -> dict:
    keys = jax.random.split(jax.random.key(seed), 6)
    return {
        "fields": noise(keys[0], (CIN, NY, NX), 1.0, 6.0, ((1, 16), (2, 32))),
        "mask": draw_mask(jax.random.fold_in(keys[5], 71), 0),
        "w1": noise(keys[2], (9, CH, CIN), (9 * CIN) ** -0.5, 0.25),
        "w2": noise(keys[3], (9, CH, CH), (9 * CH) ** -0.5, 0.3125),
        "cotangent": noise(keys[4], (CH, NY, NX), 1.0, 6.0, ((1, 16), (2, 32))),
    }


def gelu_parts(a):
    coeff = 0.7978845608
    inner = coeff * (a + 0.044715 * a * a * a)
    tval = jnp.tanh(inner)
    value = 0.5 * a * (1.0 + tval)
    slope = 0.5 * (1.0 + tval) + 0.5 * a * (1.0 - tval * tval) * coeff * (1.0 + 0.134145 * a * a)
    return (value, slope)

def extend(field):
    folded = field[:, -1:, ::-1]
    zero_row = jnp.zeros_like(field[:, :1, :])
    rows_ext = jnp.concatenate([zero_row, field, folded], axis=1)
    return jnp.concatenate([rows_ext[:, :, -1:], rows_ext, rows_ext[:, :, :1]], axis=2)

def retract(padded):
    count_x = padded.shape[2] - 2
    inner = padded[:, :, 1:count_x + 1]
    inner = inner.at[:, :, count_x - 1].add(padded[:, :, 0])
    inner = inner.at[:, :, 0].add(padded[:, :, count_x + 1])
    count_y = padded.shape[1] - 2
    result = inner[:, 1:count_y + 1, :]
    return result.at[:, count_y - 1, :].add(inner[:, count_y + 1, ::-1])

def conv(padded, kernel):
    rows_n = padded.shape[1] - 2
    cols_n = padded.shape[2] - 2
    full = padded.astype(jnp.float32)
    kern = kernel.astype(jnp.float32)
    total = jnp.zeros((kernel.shape[1], rows_n, cols_n), jnp.float32)
    for tap in range(9):
        drow, dcol = (tap // 3, tap % 3)
        total = total + jnp.einsum('oi,ihw->ohw', kern[tap], full[:, drow:drow + rows_n, dcol:dcol + cols_n])
    return total

def tconv(grad, kernel):
    rows_n = grad.shape[1]
    cols_n = grad.shape[2]
    wide = jnp.pad(grad.astype(jnp.float32), ((0, 0), (2, 2), (2, 2)))
    kern = kernel.astype(jnp.float32)
    total = jnp.zeros((kernel.shape[2], rows_n + 2, cols_n + 2), jnp.float32)
    for tap in range(9):
        drow, dcol = (tap // 3, tap % 3)
        total = total + jnp.einsum('oi,ohw->ihw', kern[tap], wide[:, 2 - drow:4 - drow + rows_n, 2 - dcol:4 - dcol + cols_n])
    return total

def wgrad(grad, padded):
    rows_n = grad.shape[1]
    cols_n = grad.shape[2]
    gfull = grad.astype(jnp.float32)
    full = padded.astype(jnp.float32)
    terms = []
    for tap in range(9):
        drow, dcol = (tap // 3, tap % 3)
        terms.append(jnp.einsum('ohw,ihw->oi', gfull, full[:, drow:drow + rows_n, dcol:dcol + cols_n]))
    return jnp.stack(terms, 0)

def reference(fields, mask, w1, w2, cotangent):
    sea = mask.astype(jnp.float32)
    x_ext = extend(fields)
    pre = conv(x_ext, w1)
    value, slope = gelu_parts(pre)
    hidden = (value * sea).astype(jnp.bfloat16)
    gate = slope * sea
    h_ext = extend(hidden)
    output = (conv(h_ext, w2) * sea).astype(jnp.bfloat16)
    grad_out = cotangent * mask.astype(jnp.bfloat16)
    grad_w2 = wgrad(grad_out, h_ext)
    grad_h = retract(tconv(grad_out, w2))
    grad_a = (grad_h * gate).astype(jnp.bfloat16)
    grad_w1 = wgrad(grad_a, x_ext)
    dx = retract(tconv(grad_a, w1)).astype(jnp.bfloat16)
    factor = 1.0 / math.sqrt(NY * NX)
    return (output, dx, grad_w1 * factor, grad_w2 * factor)
```

```python
import functools
import math

import jax
import jax.numpy as jnp
from jax import lax
from jax.experimental import pallas as pl
from jax.experimental.pallas import tpu as pltpu
from jax.sharding import PartitionSpec as P

MESH = pl.DeviceIdType.MESH
BF = jnp.bfloat16
F32 = jnp.float32
CIN, CH, KX = 75, 48, 80
ROWS, LANES = 8, 128
EXT = ROWS + 4
RIM = ROWS + 2
TILES = 27


def nn(a, b):
    return lax.dot_general(a, b, (((1,), (0,)), ((), ())), preferred_element_type=F32)


def nt(a, b):
    return lax.dot_general(a, b, (((1,), (1,)), ((), ())), preferred_element_type=F32)


def tn(a, b):
    return lax.dot_general(a, b, (((0,), (0,)), ((), ())), preferred_element_type=F32)


def gelu_parts(a):
    coeff = 0.7978845608
    inner = coeff * (a + 0.044715 * a * a * a)
    tval = jnp.tanh(inner)
    value = 0.5 * a * (1.0 + tval)
    slope = 0.5 * (1.0 + tval) + 0.5 * a * (1.0 - tval * tval) * coeff * (1.0 + 0.134145 * a * a)
    return (value, slope)


def tile(r, count=1):
    return slice(r * LANES, (r + count) * LANES)


def gather_rows(y, rows):
    n = rows * LANES
    c = y.shape[0] // 3
    return y[:c, :n] + y[c : 2 * c, LANES : LANES + n] + y[2 * c :, 2 * LANES : 2 * LANES + n]


def kernel(
    nlat, nlon, per, owners,
    f_ref, wa1, wa1n, wa2, tb2, tb2n, tb1, tb1n,
    out_ref, dx_ref, dw_ref,
    xm, xg, packs, mine, d1m, d1g, d2m, d2g, hd, dad, am, ae, gbuf, rbuf1, rbuf2, obuf,
    send_sem, recv_sem, red_send, red_recv,
):
    lat, lon = lax.axis_index("lat"), lax.axis_index("lon")
    top, bottom = lat == nlat - 1, lat == 0
    east, west = lax.rem(lon + 1, nlon), lax.rem(lon + nlon - 1, nlon)

    barrier = pltpu.get_barrier_semaphore()

    def greet(a, b):
        pl.semaphore_signal(barrier, inc=1, device_id=(a, b), device_id_type=MESH)

    @pl.loop(1, nlon)
    def _(j):
        greet(lat, lax.rem(lon + j, nlon))

    @pl.loop(1, nlat)
    def _(j):
        greet(lax.rem(lat + j, nlat), lon)

    @pl.when(jnp.logical_not(top))
    def _():
        greet(lat + 1, east)
        greet(lat + 1, west)

    @pl.when(jnp.logical_not(bottom))
    def _():
        greet(lat - 1, east)
        greet(lat - 1, west)

    cell = lax.broadcasted_iota(jnp.int32, (32, ROWS * LANES), 0)
    place = lax.broadcasted_iota(jnp.int32, (32, ROWS * LANES), 1)
    want = ((cell % 16) // 2) * LANES + cell % 2 + jnp.where(cell < 16, LANES - 2, 0)
    picked = nt((place == want).astype(F32).astype(BF), f_ref[...]).astype(BF)
    mine[0] = picked[:16]
    mine[1] = picked[16:]

    pl.semaphore_wait(
        barrier,
        nlon - 1 + nlat - 1 + jnp.where(top, 0, 2) + jnp.where(bottom, 0, 2),
    )

    def send(src, dst, slot, a, b):
        return pltpu.make_async_remote_copy(
            src_ref=src, dst_ref=dst, send_sem=send_sem.at[slot], recv_sem=recv_sem.at[slot],
            device_id=(a, b), device_id_type=MESH,
        )

    low, high = f_ref.at[:, tile(0, 2)], f_ref.at[:, tile(ROWS - 2, 2)]
    above, below = xm.at[:, tile(ROWS + 2, 2)], xm.at[:, tile(0, 2)]
    fold_e = lax.rem(2 * nlon - 2 - lon, nlon)
    fold_w = lax.rem(nlon - lon, nlon)

    @pl.when(jnp.logical_not(top))
    def _():
        send(high, below, 7, lat + 1, lon).start()

    @pl.when(top)
    def _():
        send(high, above, 6, lat, nlon - 1 - lon).start()

    @pl.when(jnp.logical_not(bottom))
    def _():
        send(low, above, 8, lat - 1, lon).start()

    send(mine.at[0], packs.at[0], 0, lat, east).start()
    send(mine.at[1], packs.at[1], 1, lat, west).start()

    @pl.when(jnp.logical_not(bottom))
    def _():
        send(mine.at[0], packs.at[2], 2, lat - 1, east).start()
        send(mine.at[1], packs.at[3], 3, lat - 1, west).start()

    @pl.when(jnp.logical_not(top))
    def _():
        send(mine.at[0], packs.at[4], 4, lat + 1, east).start()
        send(mine.at[1], packs.at[5], 5, lat + 1, west).start()

    @pl.when(top)
    def _():
        @pl.when(fold_e != lon)
        def _():
            send(mine.at[0], packs.at[3], 9, lat, fold_e).start()

        @pl.when(fold_w != lon)
        def _():
            send(mine.at[1], packs.at[2], 10, lat, fold_w).start()

        @pl.when(fold_e == lon)
        def _():
            packs[3] = mine[0]

        @pl.when(fold_w == lon)
        def _():
            packs[2] = mine[1]

    @pl.when(bottom)
    def _():
        xm[:, tile(0, 2)] = jnp.zeros((128, 2 * LANES), BF)
        packs[4] = jnp.zeros((16, 128), BF)
        packs[5] = jnp.zeros((16, 128), BF)

    xm[:, tile(2, ROWS)] = f_ref[...]
    zero = jnp.zeros((CH, LANES), BF)
    for dr in range(3):
        at = slice(dr * CH, (dr + 1) * CH)
        ae[at, tile(dr, ROWS)] = f_ref[KX:, :]
        for r in range(RIM):
            if not dr <= r < dr + ROWS:
                am[at, tile(r)] = zero
                ae[at, tile(r)] = zero

    k = lax.broadcasted_iota(jnp.int32, (96, 1), 0)
    slot, row, j = k // 16, (k % 16) // 2, k % 2
    row_to = jnp.where(slot < 2, row + 2, jnp.where(slot < 4, row + 10, row - 6))
    row_to = jnp.where((slot >= 2) & (slot < 4) & top, 17 - row, row_to)
    lane_to = jnp.where(slot % 2 == 0, LANES - 2 + j, j)
    lane_to = jnp.where((slot == 2) & top, LANES - 1 - j, lane_to)
    lane_to = jnp.where((slot == 3) & top, 1 - j, lane_to)
    good = (slot < 2) | ((slot < 4) & (row_to < EXT)) | ((slot >= 4) & (row_to >= 0))
    goal = jnp.where(good, row_to * LANES + lane_to, -1)

    def landed(ref, slot):
        pltpu.make_async_copy(ref, ref, recv_sem.at[slot]).wait()

    landed(packs.at[0], 0)
    landed(packs.at[1], 1)

    @pl.when(jnp.logical_not(top))
    def _():
        landed(above, 8)
        landed(packs.at[2], 2)
        landed(packs.at[3], 3)

    @pl.when(top)
    def _():
        landed(above, 6)

        @pl.when(fold_e != lon)
        def _():
            landed(packs.at[3], 9)

        @pl.when(fold_w != lon)
        def _():
            landed(packs.at[2], 10)

        back = lax.broadcasted_iota(jnp.int32, (LANES, LANES), 0)
        back = back + lax.broadcasted_iota(jnp.int32, (LANES, LANES), 1)
        back = (back == LANES - 1).astype(F32).astype(BF)
        first = nn(xm[:, tile(ROWS + 2)], back).astype(BF)
        second = nn(xm[:, tile(ROWS + 3)], back).astype(BF)
        xm[:, tile(ROWS + 2)] = second
        xm[:, tile(ROWS + 3)] = first

    @pl.when(jnp.logical_not(bottom))
    def _():
        landed(below, 7)
        landed(packs.at[4], 4)
        landed(packs.at[5], 5)

    flat = jnp.concatenate([packs[s] for s in range(6)], axis=0)
    lanes96 = lax.broadcasted_iota(jnp.int32, (96, EXT * LANES), 1)
    xg[...] = tn(flat, (lanes96 == goal).astype(F32).astype(BF)).astype(BF)

    lane = lax.broadcasted_iota(jnp.int32, (1, LANES), 1)

    def shifts(main, ghost):
        main, ghost = main.astype(F32), ghost.astype(F32)
        left = (pltpu.roll(main, 1, 1), pltpu.roll(ghost, 1, 1))
        right = (pltpu.roll(main, LANES - 1, 1), pltpu.roll(ghost, LANES - 1, 1))
        a = jnp.where(lane == 0, left[1], left[0]).astype(BF)
        b = jnp.where(lane == LANES - 1, right[1], right[0]).astype(BF)
        ga = jnp.where(lane == 0, left[0], left[1]).astype(BF)
        gb = jnp.where(lane == LANES - 1, right[0], right[1]).astype(BF)
        return a, b, ga, gb

    for r in range(EXT):
        t = tile(r)
        main, ghost = xm[:, t], xg[:, t]
        a, b, ga, gb = shifts(main, ghost)
        for q, m, g in ((0, a, ga), (1, main, ghost), (2, b, gb)):
            d1m[q * KX : (q + 1) * KX, t] = m[:KX]
            d1g[q * KX : (q + 1) * KX, t] = g[:KX]
            d2m[q * CH : (q + 1) * CH, t] = m[KX:]
            d2g[q * CH : (q + 1) * CH, t] = g[KX:]

    def hidden(d1, d2, field):
        a = gather_rows(nn(wa1[...], d1[...]), RIM)
        last = gather_rows(nn(wa1n[...], d1[:, tile(RIM - 1, 3)]), 1)
        a = jnp.concatenate([a[:, : (RIM - 1) * LANES], last], axis=1)
        value, slope = gelu_parts(a)
        sea = field[CIN : CIN + 1, tile(1, RIM)].astype(F32)
        z = jnp.concatenate(
            [nn(tb2[...], d2[:, tile(0, RIM)]), nn(tb2n[...], d2[:, tile(RIM, 2)])], axis=1
        )
        grad = (gather_rows(z, RIM) * (slope * sea)).astype(BF)
        return (value * sea).astype(BF), grad

    hm, gm = hidden(d1m, d2m, xm)
    hg, gg = hidden(d1g, d2g, xg)
    for dr in range(3):
        am[dr * CH : (dr + 1) * CH, tile(dr, ROWS)] = gm[:, tile(1, ROWS)]
    for r in range(RIM):
        t = tile(r)
        for ref, main, ghost in ((hd, hm[:, t], hg[:, t]), (dad, gm[:, t], gg[:, t])):
            a, b, _, _ = shifts(main, ghost)
            ref[0:CH, t] = a
            ref[CH : 2 * CH, t] = main
            ref[2 * CH :, t] = b

    term2 = nt(ae[...], hd[...])
    term1 = nt(am[...], d1m[:, tile(1, RIM)])
    terms = jnp.concatenate([term1, term2], axis=1).astype(BF)
    for t in range(TILES):
        a, b = t // 3, t % 3
        gbuf[t // per, (t % per) * 16 : (t % per + 1) * 16, :] = terms[16 * a : 16 * a + 16, tile(b)]
    if TILES < per * owners:
        gbuf[owners - 1, (TILES - per * (owners - 1)) * 16 :, :] = jnp.zeros(
            ((per * owners - TILES) * 16, LANES), BF
        )

    def reduce_send(src, dst, phase, a, b):
        return pltpu.make_async_remote_copy(
            src_ref=src, dst_ref=dst, send_sem=red_send.at[phase], recv_sem=red_recv.at[phase],
            device_id=(a, b), device_id_type=MESH,
        )

    @pl.loop(1, nlon)
    def _(j):
        peer = lax.rem(lon + j, nlon)

        @pl.when(peer < owners)
        def _():
            reduce_send(gbuf.at[peer], rbuf1.at[lon], 0, lat, peer).start()

    sea = f_ref[CIN : CIN + 1, :].astype(F32)
    out_ref[...] = (gather_rows(nn(wa2[...], hd[...]), ROWS) * sea).astype(BF)
    v = jnp.concatenate(
        [nn(tb1[...], dad[:, tile(0, RIM - 1)]), nn(tb1n[...], dad[:, tile(RIM - 1)])], axis=1
    )
    dx_ref[...] = gather_rows(v, ROWS).astype(BF)

    owner = lon < owners

    @pl.when(owner)
    def _():
        rbuf1[lon] = gbuf[lon]
        some = rbuf1.at[pl.ds(0, nlon - 1)]
        pltpu.make_async_copy(some, some, red_recv.at[0]).wait()
        rbuf2[lat] = jnp.sum(rbuf1[...].astype(F32), axis=0).astype(BF)

        @pl.loop(1, nlat)
        def _(j):
            peer = lax.rem(lat + j, nlat)
            reduce_send(rbuf2.at[lat], rbuf2.at[lat], 1, peer, lon).start()

        some2 = rbuf2.at[pl.ds(0, nlat - 1)]
        pltpu.make_async_copy(some2, some2, red_recv.at[1]).wait()
        obuf[lon] = jnp.sum(rbuf2[...].astype(F32), axis=0).astype(BF)

        @pl.loop(1, nlon)
        def _(j):
            peer = lax.rem(lon + j, nlon)
            reduce_send(obuf.at[lon], obuf.at[lon], 2, lat, peer).start()

        got = obuf.at[pl.ds(0, owners - 1)]
        pltpu.make_async_copy(got, got, red_recv.at[2]).wait()

    @pl.when(jnp.logical_not(owner))
    def _():
        pltpu.make_async_copy(obuf, obuf, red_recv.at[2]).wait()

    dw_ref[...] = obuf[...]

    def sent(ref, sem):
        pltpu.make_async_copy(ref, ref, sem).wait()

    sent(mine.at[0], send_sem.at[0])
    sent(mine.at[1], send_sem.at[1])

    @pl.when(jnp.logical_not(top))
    def _():
        sent(high, send_sem.at[7])
        sent(mine.at[0], send_sem.at[4])
        sent(mine.at[1], send_sem.at[5])

    @pl.when(top)
    def _():
        sent(high, send_sem.at[6])

        @pl.when(fold_e != lon)
        def _():
            sent(mine.at[0], send_sem.at[9])

        @pl.when(fold_w != lon)
        def _():
            sent(mine.at[1], send_sem.at[10])

    @pl.when(jnp.logical_not(bottom))
    def _():
        sent(low, send_sem.at[8])
        sent(mine.at[0], send_sem.at[2])
        sent(mine.at[1], send_sem.at[3])

    @pl.when(owner)
    def _():
        sent(gbuf.at[pl.ds(0, owners - 1)], red_send.at[0])
        sent(rbuf2.at[pl.ds(0, nlat - 1)], red_send.at[1])
        sent(rbuf1.at[pl.ds(0, nlon - 1)], red_send.at[2])

    @pl.when(jnp.logical_not(owner))
    def _():
        sent(gbuf, red_send.at[0])


def stacked(w, pad):
    w = jnp.pad(w, ((0, 0), (0, 0), (0, 0), (0, pad)))
    return w.transpose(0, 2, 1, 3).reshape(3 * w.shape[2], 3 * w.shape[3])


def body(nlat, nlon, fields, mask, w1, w2, cotangent):
    sea = mask.astype(BF)[None]
    field = jnp.concatenate(
        [fields, sea, jnp.zeros((KX - CIN - 1, ROWS, LANES), BF), cotangent * sea], axis=0
    ).reshape(KX + CH, ROWS * LANES)
    top = lax.axis_index("lat") == nlat - 1
    k1 = w1.reshape(3, 3, CH, CIN)
    k2 = w2.reshape(3, 3, CH, CH)
    k1r, k2r = k1[::-1, ::-1], k2[::-1, ::-1]
    swap = (0, 1, 3, 2)
    rows = ((0, 0), (0, 0), (0, KX - CIN), (0, 0))
    wa1 = stacked(k1, KX - CIN)
    wa1n = stacked(jnp.where(top, k1r, k1), KX - CIN)
    wa2 = stacked(k2, 0)
    tb2 = stacked(k2r.transpose(swap), 0)
    tb2n = stacked(jnp.where(top, k2, k2r).transpose(swap), 0)
    tb1 = stacked(jnp.pad(k1r.transpose(swap), rows), 0)
    tb1n = stacked(jnp.pad(jnp.where(top, k1, k1r).transpose(swap), rows), 0)

    per = -(-TILES // nlon)
    owners = -(-TILES // per)
    chunk = (per * 16, LANES)
    wide, slim = EXT * LANES, RIM * LANES
    vm = pl.BlockSpec(memory_space=pltpu.VMEM)
    out, dx, dw = pl.pallas_call(
        functools.partial(kernel, nlat, nlon, per, owners),
        out_shape=(
            jax.ShapeDtypeStruct((CH, ROWS * LANES), BF),
            jax.ShapeDtypeStruct((KX, ROWS * LANES), BF),
            jax.ShapeDtypeStruct((owners,) + chunk, BF),
        ),
        in_specs=[vm] * 8,
        out_specs=(vm, vm, vm),
        scratch_shapes=[
            pltpu.VMEM((128, wide), BF),
            pltpu.VMEM((128, wide), BF),
            pltpu.VMEM((6, 16, 128), BF),
            pltpu.VMEM((2, 16, 128), BF),
            pltpu.VMEM((3 * KX, wide), BF),
            pltpu.VMEM((3 * KX, wide), BF),
            pltpu.VMEM((3 * CH, wide), BF),
            pltpu.VMEM((3 * CH, wide), BF),
            pltpu.VMEM((3 * CH, slim), BF),
            pltpu.VMEM((3 * CH, slim), BF),
            pltpu.VMEM((3 * CH, slim), BF),
            pltpu.VMEM((3 * CH, slim), BF),
            pltpu.VMEM((owners,) + chunk, BF),
            pltpu.VMEM((nlon,) + chunk, BF),
            pltpu.VMEM((nlat,) + chunk, BF),
            pltpu.VMEM((owners,) + chunk, BF),
            pltpu.SemaphoreType.DMA((11,)),
            pltpu.SemaphoreType.DMA((11,)),
            pltpu.SemaphoreType.DMA((3,)),
            pltpu.SemaphoreType.DMA((3,)),
        ],
        compiler_params=pltpu.CompilerParams(
            collective_id=0, has_side_effects=True, vmem_limit_bytes=40 * 1024 * 1024
        ),
    )(field, wa1, wa1n, wa2, tb2, tb2n, tb1, tb1n)

    factor = 1.0 / math.sqrt(ROWS * LANES * nlat * nlon)
    grads = dw.reshape(-1, 16, LANES)[:TILES].reshape(9, 3, 16, LANES).transpose(0, 2, 1, 3)
    grads = grads.reshape(3 * CH, 3 * LANES).astype(F32) * factor
    dw1 = grads[:, : 3 * KX].reshape(3, CH, 3, KX)[..., :CIN].transpose(0, 2, 1, 3)
    dw2 = grads[:, 3 * KX :].reshape(3, CH, 3, CH).transpose(0, 2, 1, 3)
    return (
        out.reshape(CH, ROWS, LANES),
        dx[:CIN].reshape(CIN, ROWS, LANES),
        dw1.reshape(9, CH, CIN),
        dw2.reshape(9, CH, CH),
    )


def solution(mesh):
    in_specs = (P(None, "lat", "lon"), P("lat", "lon"), P(), P(), P(None, "lat", "lon"))
    out_specs = (P(None, "lat", "lon"), P(None, "lat", "lon"), P(), P())
    run = functools.partial(body, mesh.shape["lat"], mesh.shape["lon"])
    return jax.shard_map(run, mesh=mesh, in_specs=in_specs, out_specs=out_specs, check_vma=False)
```

```python
import functools
import math

import jax
import jax.numpy as jnp
from jax import lax
from jax.experimental import pallas as pl
from jax.experimental.pallas import tpu as pltpu
from jax.sharding import PartitionSpec as P

MESH = pl.DeviceIdType.MESH
BF = jnp.bfloat16
F32 = jnp.float32
CIN, CH, KX = 75, 48, 80
ROWS, LANES = 8, 128
EXT = ROWS + 4
RIM = ROWS + 2
TILES = 27


def nn(a, b):
    return lax.dot_general(a, b, (((1,), (0,)), ((), ())), preferred_element_type=F32)


def nt(a, b):
    return lax.dot_general(a, b, (((1,), (1,)), ((), ())), preferred_element_type=F32)


def tn(a, b):
    return lax.dot_general(a, b, (((0,), (0,)), ((), ())), preferred_element_type=F32)


def gelu_parts(a):
    coeff = 0.7978845608
    inner = coeff * (a + 0.044715 * a * a * a)
    tval = jnp.tanh(inner)
    value = 0.5 * a * (1.0 + tval)
    slope = 0.5 * (1.0 + tval) + 0.5 * a * (1.0 - tval * tval) * coeff * (1.0 + 0.134145 * a * a)
    return (value, slope)


def tile(r, count=1):
    return slice(r * LANES, (r + count) * LANES)


def gather_rows(y, rows):
    n = rows * LANES
    c = y.shape[0] // 3
    return y[:c, :n] + y[c : 2 * c, LANES : LANES + n] + y[2 * c :, 2 * LANES : 2 * LANES + n]


def kernel(
    dims, per,
    x_hbm, m_hbm, w1_hbm, w2_hbm, c_hbm,
    out_ref, dx_ref, dw1_ref, dw2_ref,
    x_in, m_in, w1_in, w2_in, c_in, flip, f_ref,
    wa1, wa1n, wa2, tb2, tb2n, tb1, tb1n,
    xm, xg, packs, mine, d1m, d1g, d2m, d2g, hd, dad, am, ae,
    gbuf, rbuf, za, yb, ya, zb, obuf,
    in_sem, send_sem, recv_sem, red_send, red_recv,
):
    xl_n, z_n, xh_n, y_n, c_n = dims
    nlat, nlon, group = xl_n * z_n, xh_n * y_n * c_n, xl_n * xh_n * c_n
    lat, lon = lax.axis_index("lat"), lax.axis_index("lon")
    xl, z = lat // z_n, lat % z_n
    xh, y, core = lon // (y_n * c_n), (lon // c_n) % y_n, lon % c_n
    me = (xl * xh_n + xh) * c_n + core
    top, bottom = lat == nlat - 1, lat == 0
    east, west = lax.rem(lon + 1, nlon), lax.rem(lon + nlon - 1, nlon)
    mirror = nlon - 1 - lon
    fold_e = lax.rem(2 * nlon - 2 - lon, nlon)
    fold_w = lax.rem(nlon - lon, nlon)

    def at_z(j):
        to = lax.rem(z + j, z_n)
        return xl * z_n + to, lon

    def at_y(j):
        to = lax.rem(y + j, y_n)
        return lat, (xh * y_n + to) * c_n + core

    def at_x(j):
        to = lax.rem(me + j, group)
        a, b, c = to // (xh_n * c_n), (to // c_n) % xh_n, to % c_n
        return to, a * z_n + z, (b * y_n + y) * c_n + c

    barrier = pltpu.get_barrier_semaphore()

    def greet(a, b):
        pl.semaphore_signal(barrier, inc=1, device_id=(a, b), device_id_type=MESH)

    for j in range(1, y_n):
        greet(*at_y(j))
    for j in range(1, z_n):
        greet(*at_z(j))

    @pl.when(top)
    def _():
        greet(lat, mirror)

        @pl.when(fold_e != lon)
        def _():
            greet(lat, fold_e)

        @pl.when(fold_w != lon)
        def _():
            greet(lat, fold_w)

    for j in range(1, group):
        greet(*at_x(j)[1:])

    @pl.when(jnp.logical_not(top))
    def _():
        greet(lat + 1, lon)
        greet(lat + 1, east)
        greet(lat + 1, west)

    @pl.when(jnp.logical_not(bottom))
    def _():
        greet(lat - 1, lon)
        greet(lat - 1, east)
        greet(lat - 1, west)

    greet(lat, east)
    greet(lat, west)

    loads = [
        pltpu.make_async_copy(src, dst, in_sem.at[i])
        for i, (src, dst) in enumerate(
            ((x_hbm, x_in), (m_hbm, m_in), (c_hbm, c_in), (w1_hbm, w1_in), (w2_hbm, w2_in))
        )
    ]
    for load in loads:
        load.start()

    for load in loads[:3]:
        load.wait()
    sea8 = m_in[...].astype(F32)
    flip[: CIN * ROWS, :] = x_in[...].astype(F32).reshape(CIN * ROWS, LANES)
    flip[CIN * ROWS : (CIN + 1) * ROWS, :] = sea8
    flip[(CIN + 1) * ROWS : KX * ROWS, :] = jnp.zeros(((KX - CIN - 1) * ROWS, LANES), F32)
    flip[KX * ROWS :, :] = (c_in[...].astype(F32) * sea8[None]).reshape(CH * ROWS, LANES)
    for r in range(ROWS):
        f_ref[:, tile(r)] = flip[pl.ds(r, KX + CH, stride=ROWS), :].astype(BF)

    cell = lax.broadcasted_iota(jnp.int32, (32, ROWS * LANES), 0)
    place = lax.broadcasted_iota(jnp.int32, (32, ROWS * LANES), 1)
    want = ((cell % 16) // 2) * LANES + cell % 2 + jnp.where(cell < 16, LANES - 2, 0)
    picked = nt((place == want).astype(F32).astype(BF), f_ref[...]).astype(BF)
    mine[0] = picked[:16]
    mine[1] = picked[16:]

    folds = 1 + jnp.where(fold_e != lon, 1, 0) + jnp.where(fold_w != lon, 1, 0)
    pl.semaphore_wait(
        barrier,
        y_n + z_n + group - 3 + 2 + jnp.where(top, folds, 3) + jnp.where(bottom, 0, 3),
    )

    def send(src, dst, slot, a, b):
        return pltpu.make_async_remote_copy(
            src_ref=src, dst_ref=dst, send_sem=send_sem.at[slot], recv_sem=recv_sem.at[slot],
            device_id=(a, b), device_id_type=MESH,
        )

    low, high = f_ref.at[:, tile(0, 2)], f_ref.at[:, tile(ROWS - 2, 2)]
    above, below = xm.at[:, tile(ROWS + 2, 2)], xm.at[:, tile(0, 2)]

    @pl.when(jnp.logical_not(top))
    def _():
        send(high, below, 7, lat + 1, lon).start()

    @pl.when(top)
    def _():
        send(high, above, 6, lat, mirror).start()

    @pl.when(jnp.logical_not(bottom))
    def _():
        send(low, above, 8, lat - 1, lon).start()

    send(mine.at[0], packs.at[0], 0, lat, east).start()
    send(mine.at[1], packs.at[1], 1, lat, west).start()

    @pl.when(jnp.logical_not(bottom))
    def _():
        send(mine.at[0], packs.at[2], 2, lat - 1, east).start()
        send(mine.at[1], packs.at[3], 3, lat - 1, west).start()

    @pl.when(jnp.logical_not(top))
    def _():
        send(mine.at[0], packs.at[4], 4, lat + 1, east).start()
        send(mine.at[1], packs.at[5], 5, lat + 1, west).start()

    @pl.when(top)
    def _():
        @pl.when(fold_e != lon)
        def _():
            send(mine.at[0], packs.at[3], 9, lat, fold_e).start()

        @pl.when(fold_w != lon)
        def _():
            send(mine.at[1], packs.at[2], 10, lat, fold_w).start()

        @pl.when(fold_e == lon)
        def _():
            packs[3] = mine[0]

        @pl.when(fold_w == lon)
        def _():
            packs[2] = mine[1]

    @pl.when(bottom)
    def _():
        xm[:, tile(0, 2)] = jnp.zeros((128, 2 * LANES), BF)
        packs[4] = jnp.zeros((16, 128), BF)
        packs[5] = jnp.zeros((16, 128), BF)

    xm[:, tile(2, ROWS)] = f_ref[...]
    zero = jnp.zeros((CH, LANES), BF)
    for dr in range(3):
        at = slice(dr * CH, (dr + 1) * CH)
        ae[at, tile(dr, ROWS)] = f_ref[KX:, :]
        for r in range(RIM):
            if not dr <= r < dr + ROWS:
                am[at, tile(r)] = zero
                ae[at, tile(r)] = zero

    k = lax.broadcasted_iota(jnp.int32, (96, 1), 0)
    slot, row, j = k // 16, (k % 16) // 2, k % 2
    row_to = jnp.where(slot < 2, row + 2, jnp.where(slot < 4, row + 10, row - 6))
    row_to = jnp.where((slot >= 2) & (slot < 4) & top, 17 - row, row_to)
    lane_to = jnp.where(slot % 2 == 0, LANES - 2 + j, j)
    lane_to = jnp.where((slot == 2) & top, LANES - 1 - j, lane_to)
    lane_to = jnp.where((slot == 3) & top, 1 - j, lane_to)
    good = (slot < 2) | ((slot < 4) & (row_to < EXT)) | ((slot >= 4) & (row_to >= 0))
    goal = jnp.where(good, row_to * LANES + lane_to, -1)

    loads[3].wait()
    loads[4].wait()
    gap = jnp.zeros((CH, KX - CIN), F32)
    k1 = [jnp.concatenate([w1_in[t].astype(F32), gap], axis=1) for t in range(9)]
    k2 = [w2_in[t].astype(F32) for t in range(9)]

    def square(k, pick):
        return jnp.concatenate(
            [jnp.concatenate([k[pick(a, b)] for b in range(3)], axis=1) for a in range(3)], axis=0
        )

    def plain(a, b):
        return 3 * a + b

    def turned(a, b):
        return 8 - 3 * a - b

    def swapped(a, b):
        return 3 * b + a

    def both(a, b):
        return 8 - 3 * b - a

    m = square(k1, plain)
    wa1[...] = m.astype(BF)
    wa1n[...] = jnp.where(top, square(k1, turned), m).astype(BF)
    wa2[...] = square(k2, plain).astype(BF)
    m = square(k2, both)
    tb2[...] = m.T.astype(BF)
    tb2n[...] = jnp.where(top, square(k2, swapped), m).T.astype(BF)
    m = square(k1, both)
    tb1[...] = m.T.astype(BF)
    tb1n[...] = jnp.where(top, square(k1, swapped), m).T.astype(BF)

    def landed(ref, slot):
        pltpu.make_async_copy(ref, ref, recv_sem.at[slot]).wait()

    landed(packs.at[0], 0)
    landed(packs.at[1], 1)

    @pl.when(jnp.logical_not(top))
    def _():
        landed(above, 8)
        landed(packs.at[2], 2)
        landed(packs.at[3], 3)

    @pl.when(top)
    def _():
        landed(above, 6)

        @pl.when(fold_e != lon)
        def _():
            landed(packs.at[3], 9)

        @pl.when(fold_w != lon)
        def _():
            landed(packs.at[2], 10)

        back = lax.broadcasted_iota(jnp.int32, (LANES, LANES), 0)
        back = back + lax.broadcasted_iota(jnp.int32, (LANES, LANES), 1)
        back = (back == LANES - 1).astype(F32).astype(BF)
        first = nn(xm[:, tile(ROWS + 2)], back).astype(BF)
        second = nn(xm[:, tile(ROWS + 3)], back).astype(BF)
        xm[:, tile(ROWS + 2)] = second
        xm[:, tile(ROWS + 3)] = first

    @pl.when(jnp.logical_not(bottom))
    def _():
        landed(below, 7)
        landed(packs.at[4], 4)
        landed(packs.at[5], 5)

    flat = jnp.concatenate([packs[s] for s in range(6)], axis=0)
    lanes96 = lax.broadcasted_iota(jnp.int32, (96, EXT * LANES), 1)
    xg[...] = tn(flat, (lanes96 == goal).astype(F32).astype(BF)).astype(BF)

    lane = lax.broadcasted_iota(jnp.int32, (1, LANES), 1)

    def shifts(main, ghost):
        main, ghost = main.astype(F32), ghost.astype(F32)
        left = (pltpu.roll(main, 1, 1), pltpu.roll(ghost, 1, 1))
        right = (pltpu.roll(main, LANES - 1, 1), pltpu.roll(ghost, LANES - 1, 1))
        a = jnp.where(lane == 0, left[1], left[0]).astype(BF)
        b = jnp.where(lane == LANES - 1, right[1], right[0]).astype(BF)
        ga = jnp.where(lane == 0, left[0], left[1]).astype(BF)
        gb = jnp.where(lane == LANES - 1, right[0], right[1]).astype(BF)
        return a, b, ga, gb

    for r in range(EXT):
        t = tile(r)
        main, ghost = xm[:, t], xg[:, t]
        a, b, ga, gb = shifts(main, ghost)
        for q, m, g in ((0, a, ga), (1, main, ghost), (2, b, gb)):
            d1m[q * KX : (q + 1) * KX, t] = m[:KX]
            d1g[q * KX : (q + 1) * KX, t] = g[:KX]
            d2m[q * CH : (q + 1) * CH, t] = m[KX:]
            d2g[q * CH : (q + 1) * CH, t] = g[KX:]

    def hidden(d1, d2, field):
        a = gather_rows(nn(wa1[...], d1[...]), RIM)
        last = gather_rows(nn(wa1n[...], d1[:, tile(RIM - 1, 3)]), 1)
        a = jnp.concatenate([a[:, : (RIM - 1) * LANES], last], axis=1)
        value, slope = gelu_parts(a)
        sea = field[CIN : CIN + 1, tile(1, RIM)].astype(F32)
        z = jnp.concatenate(
            [nn(tb2[...], d2[:, tile(0, RIM)]), nn(tb2n[...], d2[:, tile(RIM, 2)])], axis=1
        )
        grad = (gather_rows(z, RIM) * (slope * sea)).astype(BF)
        return (value * sea).astype(BF), grad

    hm, gm = hidden(d1m, d2m, xm)
    hg, gg = hidden(d1g, d2g, xg)
    for dr in range(3):
        am[dr * CH : (dr + 1) * CH, tile(dr, ROWS)] = gm[:, tile(1, ROWS)]
    for r in range(RIM):
        t = tile(r)
        for ref, main, ghost in ((hd, hm[:, t], hg[:, t]), (dad, gm[:, t], gg[:, t])):
            a, b, _, _ = shifts(main, ghost)
            ref[0:CH, t] = a
            ref[CH : 2 * CH, t] = main
            ref[2 * CH :, t] = b

    term2 = nt(ae[...], hd[...])
    term1 = nt(am[...], d1m[:, tile(1, RIM)])
    terms = jnp.concatenate([term1, term2], axis=1).astype(BF)
    for t in range(TILES):
        a, b = t // 3, t % 3
        gbuf[t // per, (t % per) * 16 : (t % per + 1) * 16, :] = terms[16 * a : 16 * a + 16, tile(b)]
    blank = jnp.zeros((16, LANES), BF)
    for t in range(TILES, per * group):
        gbuf[t // per, (t % per) * 16 : (t % per + 1) * 16, :] = blank

    def pass_on(src, dst, phase, a, b):
        pltpu.make_async_remote_copy(
            src_ref=src, dst_ref=dst, send_sem=red_send.at[phase], recv_sem=red_recv.at[phase],
            device_id=(a, b), device_id_type=MESH,
        ).start()

    def done(ref, count, sem):
        some = ref.at[pl.ds(0, count)]
        pltpu.make_async_copy(some, some, sem).wait()

    def total(ref):
        return jnp.sum(ref[...].astype(F32), axis=0).astype(BF)

    for j in range(1, group):
        to, a, b = at_x(j)
        pass_on(gbuf.at[to], rbuf.at[me], 0, a, b)
    rbuf[me] = gbuf[me]

    sea = f_ref[CIN : CIN + 1, :].astype(F32)
    res = gather_rows(nn(wa2[...], hd[...]), ROWS) * sea
    for r in range(ROWS):
        flip[pl.ds(r, CH, stride=ROWS), :] = res[:, tile(r)]
    out_ref[...] = flip[: CH * ROWS, :].reshape(CH, ROWS, LANES).astype(BF)
    v = jnp.concatenate(
        [nn(tb1[...], dad[:, tile(0, RIM - 1)]), nn(tb1n[...], dad[:, tile(RIM - 1)])], axis=1
    )
    res = gather_rows(v, ROWS)
    for r in range(ROWS):
        flip[pl.ds(r, KX, stride=ROWS), :] = res[:, tile(r)]
    dx_ref[...] = flip[: CIN * ROWS, :].reshape(CIN, ROWS, LANES).astype(BF)

    half = per * 8
    done(rbuf, group - 1, red_recv.at[0])
    part = total(rbuf)
    za[z] = part[:half]
    yb[y] = part[half:]
    for j in range(1, z_n):
        pass_on(za.at[z], za.at[z], 1, *at_z(j))
    for j in range(1, y_n):
        pass_on(yb.at[y], yb.at[y], 2, *at_y(j))
    done(za, z_n - 1, red_recv.at[1])
    ya[y] = total(za)
    for j in range(1, y_n):
        pass_on(ya.at[y], ya.at[y], 3, *at_y(j))
    done(yb, y_n - 1, red_recv.at[2])
    zb[z] = total(yb)
    for j in range(1, z_n):
        pass_on(zb.at[z], zb.at[z], 4, *at_z(j))
    done(ya, y_n - 1, red_recv.at[3])
    obuf[me, :half] = total(ya)
    done(zb, z_n - 1, red_recv.at[4])
    obuf[me, half:] = total(zb)
    for j in range(1, group):
        _, a, b = at_x(j)
        pass_on(obuf.at[me], obuf.at[me], 5, a, b)
    done(obuf, group - 1, red_recv.at[5])

    factor = 1.0 / math.sqrt(ROWS * LANES * nlat * nlon)
    for dr in range(3):
        rows3 = []
        for a in range(3 * dr, 3 * dr + 3):
            tiles = range(3 * a, 3 * a + 3)
            rows3.append(
                jnp.concatenate(
                    [obuf[t // per, (t % per) * 16 : (t % per + 1) * 16, :] for t in tiles], axis=1
                )
            )
        grads = jnp.concatenate(rows3, axis=0).astype(F32) * factor
        for dc in range(3):
            dw1_ref[3 * dr + dc] = grads[:, dc * KX : dc * KX + CIN]
            dw2_ref[3 * dr + dc] = grads[:, 3 * KX + dc * CH : 3 * KX + (dc + 1) * CH]

    def sent(ref, sem):
        pltpu.make_async_copy(ref, ref, sem).wait()

    sent(mine.at[0], send_sem.at[0])
    sent(mine.at[1], send_sem.at[1])

    @pl.when(jnp.logical_not(top))
    def _():
        sent(high, send_sem.at[7])
        sent(mine.at[0], send_sem.at[4])
        sent(mine.at[1], send_sem.at[5])

    @pl.when(top)
    def _():
        sent(high, send_sem.at[6])

        @pl.when(fold_e != lon)
        def _():
            sent(mine.at[0], send_sem.at[9])

        @pl.when(fold_w != lon)
        def _():
            sent(mine.at[1], send_sem.at[10])

    @pl.when(jnp.logical_not(bottom))
    def _():
        sent(low, send_sem.at[8])
        sent(mine.at[0], send_sem.at[2])
        sent(mine.at[1], send_sem.at[3])

    done(rbuf, group - 1, red_send.at[0])
    done(za, z_n - 1, red_send.at[1])
    done(yb, y_n - 1, red_send.at[2])
    done(ya, y_n - 1, red_send.at[3])
    done(zb, z_n - 1, red_send.at[4])
    done(obuf, group - 1, red_send.at[5])


def body(dims, fields, mask, w1, w2, cotangent):
    xl_n, z_n, xh_n, y_n, c_n = dims
    group = xl_n * xh_n * c_n
    per = -(-TILES // (2 * group)) * 2
    wide, slim = EXT * LANES, RIM * LANES
    vm = pl.BlockSpec(memory_space=pltpu.VMEM)
    hbm = pl.BlockSpec(memory_space=pl.ANY)

    def held(*shape):
        return pltpu.VMEM(shape, BF)

    return pl.pallas_call(
        functools.partial(kernel, dims, per),
        out_shape=(
            jax.ShapeDtypeStruct((CH, ROWS, LANES), BF),
            jax.ShapeDtypeStruct((CIN, ROWS, LANES), BF),
            jax.ShapeDtypeStruct((9, CH, CIN), F32),
            jax.ShapeDtypeStruct((9, CH, CH), F32),
        ),
        in_specs=[hbm] * 5,
        out_specs=(vm,) * 4,
        scratch_shapes=[
            held(CIN, ROWS, LANES), pltpu.VMEM((ROWS, LANES), jnp.int32),
            held(9, CH, CIN), held(9, CH, CH), held(CH, ROWS, LANES),
            pltpu.VMEM(((KX + CH) * ROWS, LANES), F32), held(KX + CH, ROWS * LANES),
            held(3 * CH, 3 * KX), held(3 * CH, 3 * KX), held(3 * CH, 3 * CH),
            held(3 * CH, 3 * CH), held(3 * CH, 3 * CH), held(3 * KX, 3 * CH), held(3 * KX, 3 * CH),
            held(128, wide), held(128, wide), held(6, 16, 128), held(2, 16, 128),
            held(3 * KX, wide), held(3 * KX, wide), held(3 * CH, wide), held(3 * CH, wide),
            held(3 * CH, slim), held(3 * CH, slim), held(3 * CH, slim), held(3 * CH, slim),
            held(group, per * 16, LANES), held(group, per * 16, LANES),
            held(z_n, per * 8, LANES), held(y_n, per * 8, LANES),
            held(y_n, per * 8, LANES), held(z_n, per * 8, LANES),
            held(group, per * 16, LANES),
            pltpu.SemaphoreType.DMA((5,)),
            pltpu.SemaphoreType.DMA((11,)), pltpu.SemaphoreType.DMA((11,)),
            pltpu.SemaphoreType.DMA((6,)), pltpu.SemaphoreType.DMA((6,)),
        ],
        compiler_params=pltpu.CompilerParams(
            collective_id=0, has_side_effects=True, vmem_limit_bytes=56 * 1024 * 1024
        ),
    )(fields, mask, w1, w2, cotangent)


def solution(mesh):
    in_specs = (P(None, "lat", "lon"), P("lat", "lon"), P(), P(), P(None, "lat", "lon"))
    out_specs = (P(None, "lat", "lon"), P(None, "lat", "lon"), P(), P())
    nlat, nlon = mesh.shape["lat"], mesh.shape["lon"]
    x_hi = 2 if nlon > 4 else 1
    dims = (2, nlat // 2, x_hi, nlon // (2 * x_hi), 2)
    run = functools.partial(body, dims)
    return jax.shard_map(run, mesh=mesh, in_specs=in_specs, out_specs=out_specs, check_vma=False)
```

```python
import functools
import math

import jax
import jax.numpy as jnp
from jax import lax
from jax.experimental import pallas as pl
from jax.experimental.pallas import tpu as pltpu
from jax.sharding import PartitionSpec as P

MESH = pl.DeviceIdType.MESH
BF = jnp.bfloat16
F32 = jnp.float32
CIN, CH, KX = 75, 48, 80
ROWS, LANES = 8, 128
EXT = ROWS + 4
RIM = ROWS + 2
TILES = 27


def nn(a, b):
    return lax.dot_general(a, b, (((1,), (0,)), ((), ())), preferred_element_type=F32)


def nt(a, b):
    return lax.dot_general(a, b, (((1,), (1,)), ((), ())), preferred_element_type=F32)


def tn(a, b):
    return lax.dot_general(a, b, (((0,), (0,)), ((), ())), preferred_element_type=F32)


def gelu_parts(a):
    coeff = 0.7978845608
    inner = coeff * (a + 0.044715 * a * a * a)
    tval = jnp.tanh(inner)
    value = 0.5 * a * (1.0 + tval)
    slope = 0.5 * (1.0 + tval) + 0.5 * a * (1.0 - tval * tval) * coeff * (1.0 + 0.134145 * a * a)
    return (value, slope)


def tile(r, count=1):
    return slice(r * LANES, (r + count) * LANES)


def gather_rows(y, rows):
    n = rows * LANES
    c = y.shape[0] // 3
    return y[:c, :n] + y[c : 2 * c, LANES : LANES + n] + y[2 * c :, 2 * LANES : 2 * LANES + n]


def far_first(n):
    return sorted(range(1, n), key=lambda j: -min(j, n - j))


def kernel(
    dims,
    x_hbm, m_hbm, w1_hbm, w2_hbm, c_hbm,
    out_ref, dx_ref, dw_ref,
    x_in, m_in, w1_in, w2_in, c_in, flip, f_ref,
    wa1, wa1n, wa2, tb2, tb2n, tb1, tb1n,
    xm, xg, packs, mine, d1m, d1g, d2m, d2g, hd, dad, am, ae,
    gbuf, rbuf, ex1, ex2, obuf,
    in_sem, out_sem, send_sem, recv_sem, *red,
):
    sem_rs, sem_x1, sem_x2, sem_ag = red[0:2], red[2:4], red[4:6], red[6:8]
    xl_n, z_n, xh_n, y_n, c_n = dims
    nlat, nlon, group = xl_n * z_n, xh_n * y_n * c_n, xl_n * xh_n * c_n
    lat, lon = lax.axis_index("lat"), lax.axis_index("lon")
    xl, z = lat // z_n, lat % z_n
    xh, y, core = lon // (y_n * c_n), (lon // c_n) % y_n, lon % c_n
    me = (xl * xh_n + xh) * c_n + core
    top, bottom = lat == nlat - 1, lat == 0
    east, west = lax.rem(lon + 1, nlon), lax.rem(lon + nlon - 1, nlon)
    mirror = nlon - 1 - lon
    fold_e = lax.rem(2 * nlon - 2 - lon, nlon)
    fold_w = lax.rem(nlon - lon, nlon)

    def at_z(j):
        to = lax.rem(z + j, z_n)
        return xl * z_n + to, lon

    def at_y(j):
        to = lax.rem(y + j, y_n)
        return lat, (xh * y_n + to) * c_n + core

    def at_x(j):
        to = lax.rem(me + j, group)
        a, b, c = to // (xh_n * c_n), (to // c_n) % xh_n, to % c_n
        return to, a * z_n + z, (b * y_n + y) * c_n + c

    loads = [
        pltpu.make_async_copy(src, dst, in_sem.at[i])
        for i, (src, dst) in enumerate(
            ((x_hbm, x_in), (m_hbm, m_in), (c_hbm, c_in), (w1_hbm, w1_in), (w2_hbm, w2_in))
        )
    ]
    for load in loads:
        load.start()

    barrier = pltpu.get_barrier_semaphore()

    def greet(a, b):
        pl.semaphore_signal(barrier, inc=1, device_id=(a, b), device_id_type=MESH)

    @pl.when(top)
    def _():
        greet(lat, mirror)

        @pl.when(fold_e != lon)
        def _():
            greet(lat, fold_e)

        @pl.when(fold_w != lon)
        def _():
            greet(lat, fold_w)

    for j in far_first(y_n):
        greet(*at_y(j))
    for j in far_first(z_n):
        greet(*at_z(j))
    for j in range(1, group):
        greet(*at_x(j)[1:])

    @pl.when(jnp.logical_not(top))
    def _():
        greet(lat + 1, east)
        greet(lat + 1, west)
        greet(lat + 1, lon)

    @pl.when(jnp.logical_not(bottom))
    def _():
        greet(lat - 1, east)
        greet(lat - 1, west)
        greet(lat - 1, lon)

    greet(lat, east)
    greet(lat, west)

    for load in loads[:3]:
        load.wait()
    sea8 = m_in[...].astype(F32)
    flip[: CIN * ROWS, :] = x_in[...].astype(F32).reshape(CIN * ROWS, LANES)
    flip[CIN * ROWS : (CIN + 1) * ROWS, :] = sea8
    flip[(CIN + 1) * ROWS : KX * ROWS, :] = jnp.zeros(((KX - CIN - 1) * ROWS, LANES), F32)
    flip[KX * ROWS :, :] = (c_in[...].astype(F32) * sea8[None]).reshape(CH * ROWS, LANES)
    for r in range(ROWS):
        f_ref[:, tile(r)] = flip[pl.ds(r, KX + CH, stride=ROWS), :].astype(BF)

    cell = lax.broadcasted_iota(jnp.int32, (32, ROWS * LANES), 0)
    place = lax.broadcasted_iota(jnp.int32, (32, ROWS * LANES), 1)
    want = ((cell % 16) // 2) * LANES + cell % 2 + jnp.where(cell < 16, LANES - 2, 0)
    picked = nt((place == want).astype(F32).astype(BF), f_ref[...]).astype(BF)
    mine[0] = picked[:16]
    mine[1] = picked[16:]

    folds = 1 + jnp.where(fold_e != lon, 1, 0) + jnp.where(fold_w != lon, 1, 0)
    pl.semaphore_wait(
        barrier,
        y_n + z_n + group - 3 + 2 + jnp.where(top, folds, 3) + jnp.where(bottom, 0, 3),
    )

    def send(src, dst, slot, a, b):
        return pltpu.make_async_remote_copy(
            src_ref=src, dst_ref=dst, send_sem=send_sem.at[slot], recv_sem=recv_sem.at[slot],
            device_id=(a, b), device_id_type=MESH,
        )

    low, high = f_ref.at[:, tile(0, 2)], f_ref.at[:, tile(ROWS - 2, 2)]
    above, below = xm.at[:, tile(ROWS + 2, 2)], xm.at[:, tile(0, 2)]

    @pl.when(top)
    def _():
        @pl.when(fold_e != lon)
        def _():
            send(mine.at[0], packs.at[3], 9, lat, fold_e).start()

        @pl.when(fold_w != lon)
        def _():
            send(mine.at[1], packs.at[2], 10, lat, fold_w).start()

        send(high, above, 6, lat, mirror).start()

        @pl.when(fold_e == lon)
        def _():
            packs[3] = mine[0]

        @pl.when(fold_w == lon)
        def _():
            packs[2] = mine[1]

    @pl.when(jnp.logical_not(bottom))
    def _():
        send(mine.at[0], packs.at[2], 2, lat - 1, east).start()
        send(mine.at[1], packs.at[3], 3, lat - 1, west).start()

    @pl.when(jnp.logical_not(top))
    def _():
        send(mine.at[0], packs.at[4], 4, lat + 1, east).start()
        send(mine.at[1], packs.at[5], 5, lat + 1, west).start()

    send(mine.at[0], packs.at[0], 0, lat, east).start()
    send(mine.at[1], packs.at[1], 1, lat, west).start()

    @pl.when(jnp.logical_not(top))
    def _():
        send(high, below, 7, lat + 1, lon).start()

    @pl.when(jnp.logical_not(bottom))
    def _():
        send(low, above, 8, lat - 1, lon).start()

    @pl.when(bottom)
    def _():
        xm[:, tile(0, 2)] = jnp.zeros((128, 2 * LANES), BF)
        packs[4] = jnp.zeros((16, 128), BF)
        packs[5] = jnp.zeros((16, 128), BF)

    xm[:, tile(2, ROWS)] = f_ref[...]
    zero = jnp.zeros((CH, LANES), BF)
    for dr in range(3):
        at = slice(dr * CH, (dr + 1) * CH)
        ae[at, tile(dr, ROWS)] = f_ref[KX:, :]
        for r in range(RIM):
            if not dr <= r < dr + ROWS:
                am[at, tile(r)] = zero
                ae[at, tile(r)] = zero

    k = lax.broadcasted_iota(jnp.int32, (96, 1), 0)
    slot, row, j = k // 16, (k % 16) // 2, k % 2
    row_to = jnp.where(slot < 2, row + 2, jnp.where(slot < 4, row + 10, row - 6))
    row_to = jnp.where((slot >= 2) & (slot < 4) & top, 17 - row, row_to)
    lane_to = jnp.where(slot % 2 == 0, LANES - 2 + j, j)
    lane_to = jnp.where((slot == 2) & top, LANES - 1 - j, lane_to)
    lane_to = jnp.where((slot == 3) & top, 1 - j, lane_to)
    good = (slot < 2) | ((slot < 4) & (row_to < EXT)) | ((slot >= 4) & (row_to >= 0))
    goal = jnp.where(good, row_to * LANES + lane_to, -1)

    loads[3].wait()
    loads[4].wait()
    gap = jnp.zeros((CH, KX - CIN), F32)
    k1 = [jnp.concatenate([w1_in[t].astype(F32), gap], axis=1) for t in range(9)]
    k2 = [w2_in[t].astype(F32) for t in range(9)]

    def square(k, pick):
        return jnp.concatenate(
            [jnp.concatenate([k[pick(a, b)] for b in range(3)], axis=1) for a in range(3)], axis=0
        )

    def plain(a, b):
        return 3 * a + b

    def turned(a, b):
        return 8 - 3 * a - b

    def swapped(a, b):
        return 3 * b + a

    def both(a, b):
        return 8 - 3 * b - a

    m = square(k1, plain)
    wa1[...] = m.astype(BF)
    wa1n[...] = jnp.where(top, square(k1, turned), m).astype(BF)
    wa2[...] = square(k2, plain).astype(BF)
    m = square(k2, both)
    tb2[...] = m.T.astype(BF)
    tb2n[...] = jnp.where(top, square(k2, swapped), m).T.astype(BF)
    m = square(k1, both)
    tb1[...] = m.T.astype(BF)
    tb1n[...] = jnp.where(top, square(k1, swapped), m).T.astype(BF)

    def landed(ref, slot):
        pltpu.make_async_copy(ref, ref, recv_sem.at[slot]).wait()

    landed(packs.at[0], 0)
    landed(packs.at[1], 1)

    @pl.when(jnp.logical_not(top))
    def _():
        landed(above, 8)
        landed(packs.at[2], 2)
        landed(packs.at[3], 3)

    @pl.when(top)
    def _():
        landed(above, 6)

        @pl.when(fold_e != lon)
        def _():
            landed(packs.at[3], 9)

        @pl.when(fold_w != lon)
        def _():
            landed(packs.at[2], 10)

        back = lax.broadcasted_iota(jnp.int32, (LANES, LANES), 0)
        back = back + lax.broadcasted_iota(jnp.int32, (LANES, LANES), 1)
        back = (back == LANES - 1).astype(F32).astype(BF)
        first = nn(xm[:, tile(ROWS + 2)], back).astype(BF)
        second = nn(xm[:, tile(ROWS + 3)], back).astype(BF)
        xm[:, tile(ROWS + 2)] = second
        xm[:, tile(ROWS + 3)] = first

    @pl.when(jnp.logical_not(bottom))
    def _():
        landed(below, 7)
        landed(packs.at[4], 4)
        landed(packs.at[5], 5)

    flat = jnp.concatenate([packs[s] for s in range(6)], axis=0)
    lanes96 = lax.broadcasted_iota(jnp.int32, (96, EXT * LANES), 1)
    xg[...] = tn(flat, (lanes96 == goal).astype(F32).astype(BF)).astype(BF)

    lane = lax.broadcasted_iota(jnp.int32, (1, LANES), 1)

    def shifts(main, ghost):
        main, ghost = main.astype(F32), ghost.astype(F32)
        left = (pltpu.roll(main, 1, 1), pltpu.roll(ghost, 1, 1))
        right = (pltpu.roll(main, LANES - 1, 1), pltpu.roll(ghost, LANES - 1, 1))
        a = jnp.where(lane == 0, left[1], left[0]).astype(BF)
        b = jnp.where(lane == LANES - 1, right[1], right[0]).astype(BF)
        ga = jnp.where(lane == 0, left[0], left[1]).astype(BF)
        gb = jnp.where(lane == LANES - 1, right[0], right[1]).astype(BF)
        return a, b, ga, gb

    for r in range(EXT):
        t = tile(r)
        main, ghost = xm[:, t], xg[:, t]
        a, b, ga, gb = shifts(main, ghost)
        for q, m, g in ((0, a, ga), (1, main, ghost), (2, b, gb)):
            d1m[q * KX : (q + 1) * KX, t] = m[:KX]
            d1g[q * KX : (q + 1) * KX, t] = g[:KX]
            d2m[q * CH : (q + 1) * CH, t] = m[KX:]
            d2g[q * CH : (q + 1) * CH, t] = g[KX:]

    def hidden(d1, d2, field):
        a = gather_rows(nn(wa1[...], d1[...]), RIM)
        last = gather_rows(nn(wa1n[...], d1[:, tile(RIM - 1, 3)]), 1)
        a = jnp.concatenate([a[:, : (RIM - 1) * LANES], last], axis=1)
        value, slope = gelu_parts(a)
        sea = field[CIN : CIN + 1, tile(1, RIM)].astype(F32)
        z = jnp.concatenate(
            [nn(tb2[...], d2[:, tile(0, RIM)]), nn(tb2n[...], d2[:, tile(RIM, 2)])], axis=1
        )
        grad = (gather_rows(z, RIM) * (slope * sea)).astype(BF)
        return (value * sea).astype(BF), grad

    hm, gm = hidden(d1m, d2m, xm)
    hg, gg = hidden(d1g, d2g, xg)
    for dr in range(3):
        am[dr * CH : (dr + 1) * CH, tile(dr, ROWS)] = gm[:, tile(1, ROWS)]
    for r in range(RIM):
        t = tile(r)
        for ref, main, ghost in ((hd, hm[:, t], hg[:, t]), (dad, gm[:, t], gg[:, t])):
            a, b, _, _ = shifts(main, ghost)
            ref[0:CH, t] = a
            ref[CH : 2 * CH, t] = main
            ref[2 * CH :, t] = b

    term2 = nt(ae[...], hd[...])
    term1 = nt(am[...], d1m[:, tile(1, RIM)])
    terms = jnp.concatenate([term1, term2], axis=1).astype(BF)
    for t in range(TILES):
        a, b = t // 3, t % 3
        gbuf[t // group, t % group] = terms[16 * a : 16 * a + 16, tile(b)]

    def pass_on(src, dst, sems, p, a, b):
        pltpu.make_async_remote_copy(
            src_ref=src, dst_ref=dst, send_sem=sems[0].at[p], recv_sem=sems[1].at[p],
            device_id=(a, b), device_id_type=MESH,
        ).start()

    def done(ref, count, sem):
        some = ref.at[pl.ds(0, count)]
        pltpu.make_async_copy(some, some, sem).wait()

    def total(ref, p, count):
        acc = ref[p, 0].astype(F32)
        for i in range(1, count):
            acc = acc + ref[p, i].astype(F32)
        return acc.astype(BF)

    def only(test, always, f):
        if always:
            f()
        else:
            pl.when(test)(f)

    parts = -(-TILES // group)
    count = [min(group, TILES - p * group) for p in range(parts)]
    first = [(z_n, z, at_z) if p % 2 == 0 else (y_n, y, at_y) for p in range(parts)]
    second = [(y_n, y, at_y) if p % 2 == 0 else (z_n, z, at_z) for p in range(parts)]

    for p in range(parts):
        for j in range(1, group):
            to, a, b = at_x(j)
            only(
                to < count[p], count[p] == group,
                functools.partial(pass_on, gbuf.at[p, to], rbuf.at[p, me], sem_rs, p, a, b),
            )

    sea = f_ref[CIN : CIN + 1, :].astype(F32)
    res = gather_rows(nn(wa2[...], hd[...]), ROWS) * sea
    for r in range(ROWS):
        flip[pl.ds(r, CH, stride=ROWS), :] = res[:, tile(r)]
    c_in[...] = flip[: CH * ROWS, :].reshape(CH, ROWS, LANES).astype(BF)
    stores = [pltpu.make_async_copy(c_in, out_ref, in_sem.at[0])]
    stores[0].start()
    v = jnp.concatenate(
        [nn(tb1[...], dad[:, tile(0, RIM - 1)]), nn(tb1n[...], dad[:, tile(RIM - 1)])], axis=1
    )
    res = gather_rows(v, ROWS)
    for r in range(ROWS):
        flip[pl.ds(r, KX, stride=ROWS), :] = res[:, tile(r)]
    x_in[...] = flip[: CIN * ROWS, :].reshape(CIN, ROWS, LANES).astype(BF)
    stores.append(pltpu.make_async_copy(x_in, dx_ref, in_sem.at[1]))
    stores[1].start()

    def hop(p, source, arrived, sem, held_as, axis, sems):
        length, at, peer = axis

        def go():
            done(source.at[p], arrived - 1, sem.at[p])
            held_as[p, at] = total(source, p, arrived)
            for j in far_first(length):
                pass_on(held_as.at[p, at], held_as.at[p, at], sems, p, *peer(j))

        only(me < count[p], count[p] == group, go)

    for p in range(parts):
        def own(p=p):
            rbuf[p, me] = gbuf[p, me]

        only(me < count[p], count[p] == group, own)
        hop(p, rbuf, group, sem_rs[1], ex1, first[p], sem_x1)
    for p in range(parts):
        hop(p, ex1, first[p][0], sem_x1[1], ex2, second[p], sem_x2)
    everyone = (group, me, lambda j: at_x(j)[1:])
    for p in range(parts):
        hop(p, ex2, second[p][0], sem_x2[1], obuf, everyone, sem_ag)
    for p in range(parts):
        if count[p] == group:
            done(obuf.at[p], group - 1, sem_ag[1].at[p])
        else:
            pl.when(me < count[p])(
                functools.partial(done, obuf.at[p], count[p] - 1, sem_ag[1].at[p])
            )
            pl.when(me >= count[p])(
                functools.partial(done, obuf.at[p], count[p], sem_ag[1].at[p])
            )
        n = count[p]
        move = pltpu.make_async_copy(obuf.at[p, pl.ds(0, n)], dw_ref.at[p, pl.ds(0, n)], out_sem.at[p])
        move.start()
        stores.append(move)

    def sent(ref, sem):
        pltpu.make_async_copy(ref, ref, sem).wait()

    sent(mine.at[0], send_sem.at[0])
    sent(mine.at[1], send_sem.at[1])

    @pl.when(jnp.logical_not(top))
    def _():
        sent(high, send_sem.at[7])
        sent(mine.at[0], send_sem.at[4])
        sent(mine.at[1], send_sem.at[5])

    @pl.when(top)
    def _():
        sent(high, send_sem.at[6])

        @pl.when(fold_e != lon)
        def _():
            sent(mine.at[0], send_sem.at[9])

        @pl.when(fold_w != lon)
        def _():
            sent(mine.at[1], send_sem.at[10])

    @pl.when(jnp.logical_not(bottom))
    def _():
        sent(low, send_sem.at[8])
        sent(mine.at[0], send_sem.at[2])
        sent(mine.at[1], send_sem.at[3])

    for p in range(parts):
        n = count[p]
        if n == group:
            done(gbuf.at[p], group - 1, sem_rs[0].at[p])
        else:
            pl.when(me < n)(functools.partial(done, gbuf.at[p], n - 1, sem_rs[0].at[p]))
            pl.when(me >= n)(functools.partial(done, gbuf.at[p], n, sem_rs[0].at[p]))

        def drain(p=p):
            done(ex1.at[p], first[p][0] - 1, sem_x1[0].at[p])
            done(ex2.at[p], second[p][0] - 1, sem_x2[0].at[p])
            done(rbuf.at[p], group - 1, sem_ag[0].at[p])

        only(me < n, n == group, drain)
    for store in stores:
        store.wait()


def finish(
    factor, parts, group,
    out_hbm, dx_hbm, dw_hbm, out_ref, dx_ref, dw1_ref, dw2_ref, tiles, dw1, dw2, sem
):
    get = pltpu.make_async_copy(dw_hbm, tiles, sem.at[0])
    get.start()
    moves = [
        pltpu.make_async_copy(src, dst, sem.at[i])
        for i, (src, dst) in enumerate(
            ((out_hbm, out_ref), (dx_hbm, dx_ref), (dw1, dw1_ref), (dw2, dw2_ref)), 1
        )
    ]
    moves[0].start()
    moves[1].start()
    get.wait()
    for dr in range(3):
        grads = jnp.concatenate(
            [
                jnp.concatenate(
                    [tiles[t // group, t % group] for t in range(3 * a, 3 * a + 3)], axis=1
                )
                for a in range(3 * dr, 3 * dr + 3)
            ],
            axis=0,
        ).astype(F32) * factor
        for dc in range(3):
            dw1[3 * dr + dc] = grads[:, dc * KX : dc * KX + CIN]
            dw2[3 * dr + dc] = grads[:, 3 * KX + dc * CH : 3 * KX + (dc + 1) * CH]
    moves[2].start()
    moves[3].start()
    for move in moves:
        move.wait()


def body(dims, fields, mask, w1, w2, cotangent):
    xl_n, z_n, xh_n, y_n, c_n = dims
    group = xl_n * xh_n * c_n
    parts = -(-TILES // group)
    wide, slim, ring = EXT * LANES, RIM * LANES, max(y_n, z_n)
    hbm = pl.BlockSpec(memory_space=pl.ANY)

    def held(*shape):
        return pltpu.VMEM(shape, BF)

    fields_like = (
        jax.ShapeDtypeStruct((CH, ROWS, LANES), BF),
        jax.ShapeDtypeStruct((CIN, ROWS, LANES), BF),
    )
    out, dx, dw = pl.pallas_call(
        functools.partial(kernel, dims),
        out_shape=fields_like + (jax.ShapeDtypeStruct((parts, group, 16, LANES), BF),),
        in_specs=[hbm] * 5,
        out_specs=(hbm,) * 3,
        scratch_shapes=[
            held(CIN, ROWS, LANES), pltpu.VMEM((ROWS, LANES), jnp.int32),
            held(9, CH, CIN), held(9, CH, CH), held(CH, ROWS, LANES),
            pltpu.VMEM(((KX + CH) * ROWS, LANES), F32), held(KX + CH, ROWS * LANES),
            held(3 * CH, 3 * KX), held(3 * CH, 3 * KX), held(3 * CH, 3 * CH),
            held(3 * CH, 3 * CH), held(3 * CH, 3 * CH), held(3 * KX, 3 * CH), held(3 * KX, 3 * CH),
            held(128, wide), held(128, wide), held(6, 16, 128), held(2, 16, 128),
            held(3 * KX, wide), held(3 * KX, wide), held(3 * CH, wide), held(3 * CH, wide),
            held(3 * CH, slim), held(3 * CH, slim), held(3 * CH, slim), held(3 * CH, slim),
            held(parts, group, 16, LANES), held(parts, group, 16, LANES),
            held(parts, ring, 16, LANES), held(parts, ring, 16, LANES),
            held(parts, group, 16, LANES),
            pltpu.SemaphoreType.DMA((5,)), pltpu.SemaphoreType.DMA((parts,)),
            pltpu.SemaphoreType.DMA((11,)), pltpu.SemaphoreType.DMA((11,)),
        ] + [pltpu.SemaphoreType.DMA((parts,))] * 8,
        compiler_params=pltpu.CompilerParams(
            collective_id=0, has_side_effects=True, vmem_limit_bytes=56 * 1024 * 1024
        ),
    )(fields, mask, w1, w2, cotangent)
    factor = 1.0 / math.sqrt(ROWS * LANES * xl_n * z_n * xh_n * y_n * c_n)
    return pl.pallas_call(
        functools.partial(finish, factor, parts, group),
        out_shape=fields_like + (
            jax.ShapeDtypeStruct((9, CH, CIN), F32),
            jax.ShapeDtypeStruct((9, CH, CH), F32),
        ),
        in_specs=[hbm] * 3,
        out_specs=(hbm,) * 4,
        scratch_shapes=[
            held(parts, group, 16, LANES),
            pltpu.VMEM((9, CH, CIN), F32), pltpu.VMEM((9, CH, CH), F32),
            pltpu.SemaphoreType.DMA((5,)),
        ],
        compiler_params=pltpu.CompilerParams(vmem_limit_bytes=56 * 1024 * 1024),
    )(out, dx, dw)


def solution(mesh):
    in_specs = (P(None, "lat", "lon"), P("lat", "lon"), P(), P(), P(None, "lat", "lon"))
    out_specs = (P(None, "lat", "lon"), P(None, "lat", "lon"), P(), P())
    nlat, nlon = mesh.shape["lat"], mesh.shape["lon"]
    x_hi = 2 if nlon > 4 else 1
    dims = (2, nlat // 2, x_hi, nlon // (2 * x_hi), 2)
    run = functools.partial(body, dims)
    return jax.shard_map(run, mesh=mesh, in_specs=in_specs, out_specs=out_specs, check_vma=False)
```

```python
import functools
import math

import jax
import jax.numpy as jnp
from jax import lax
from jax.experimental import pallas as pl
from jax.experimental.pallas import tpu as pltpu
from jax.sharding import PartitionSpec as P

MESH = pl.DeviceIdType.MESH
BF = jnp.bfloat16
F32 = jnp.float32
CIN, CH, KX = 75, 48, 80
ROWS, LANES = 8, 128
EXT = ROWS + 4
RIM = ROWS + 2
TILES = 27


def nn(a, b):
    return lax.dot_general(a, b, (((1,), (0,)), ((), ())), preferred_element_type=F32)


def nt(a, b):
    return lax.dot_general(a, b, (((1,), (1,)), ((), ())), preferred_element_type=F32)


def tn(a, b):
    return lax.dot_general(a, b, (((0,), (0,)), ((), ())), preferred_element_type=F32)


def gelu_parts(a):
    coeff = 0.7978845608
    inner = coeff * (a + 0.044715 * a * a * a)
    tval = jnp.tanh(inner)
    value = 0.5 * a * (1.0 + tval)
    slope = 0.5 * (1.0 + tval) + 0.5 * a * (1.0 - tval * tval) * coeff * (1.0 + 0.134145 * a * a)
    return (value, slope)


def tile(r, count=1):
    return slice(r * LANES, (r + count) * LANES)


def gather_rows(y, rows):
    n = rows * LANES
    c = y.shape[0] // 3
    return y[:c, :n] + y[c : 2 * c, LANES : LANES + n] + y[2 * c :, 2 * LANES : 2 * LANES + n]


def far_first(n):
    return sorted(range(1, n), key=lambda j: -min(j, n - j))


def kernel(
    dims,
    x_hbm, m_hbm, w1_hbm, w2_hbm, c_hbm,
    out_ref, dx_ref, dw_ref,
    x_in, m_in, w1_in, w2_in, c_in, flip, f_ref,
    wa1, wa1n, wa2, tb2, tb2n, tb1, tb1n,
    xm, xg, packs, mine, d1m, d1g, d2m, d2g, hd, dad, am, ae,
    gbuf, rbuf, ex1, ex2, obuf,
    in_sem, out_sem, send_sem, recv_sem, *red,
):
    sem_rs, sem_x1, sem_x2, sem_ag = red[0:2], red[2:4], red[4:6], red[6:8]
    xl_n, z_n, xh_n, y_n, c_n = dims
    nlat, nlon, group = xl_n * z_n, xh_n * y_n * c_n, xl_n * xh_n * c_n
    lat, lon = lax.axis_index("lat"), lax.axis_index("lon")
    xl, z = lat // z_n, lat % z_n
    xh, y, core = lon // (y_n * c_n), (lon // c_n) % y_n, lon % c_n
    me = (xl * xh_n + xh) * c_n + core
    top, bottom = lat == nlat - 1, lat == 0
    east, west = lax.rem(lon + 1, nlon), lax.rem(lon + nlon - 1, nlon)
    mirror = nlon - 1 - lon
    fold_e = lax.rem(2 * nlon - 2 - lon, nlon)
    fold_w = lax.rem(nlon - lon, nlon)

    def at_z(j):
        to = lax.rem(z + j, z_n)
        return xl * z_n + to, lon

    def at_y(j):
        to = lax.rem(y + j, y_n)
        return lat, (xh * y_n + to) * c_n + core

    def at_x(j):
        to = lax.rem(me + j, group)
        a, b, c = to // (xh_n * c_n), (to // c_n) % xh_n, to % c_n
        return to, a * z_n + z, (b * y_n + y) * c_n + c

    loads = [
        pltpu.make_async_copy(src, dst, in_sem.at[i])
        for i, (src, dst) in enumerate(
            ((x_hbm, x_in), (m_hbm, m_in), (c_hbm, c_in), (w1_hbm, w1_in), (w2_hbm, w2_in))
        )
    ]
    for load in loads:
        load.start()

    barrier = pltpu.get_barrier_semaphore()

    def greet(a, b):
        pl.semaphore_signal(barrier, inc=1, device_id=(a, b), device_id_type=MESH)

    @pl.when(top)
    def _():
        greet(lat, mirror)

        @pl.when(fold_e != lon)
        def _():
            greet(lat, fold_e)

        @pl.when(fold_w != lon)
        def _():
            greet(lat, fold_w)

    for j in far_first(y_n):
        greet(*at_y(j))
    for j in far_first(z_n):
        greet(*at_z(j))
    for j in range(1, group):
        greet(*at_x(j)[1:])

    @pl.when(jnp.logical_not(top))
    def _():
        greet(lat + 1, east)
        greet(lat + 1, west)
        greet(lat + 1, lon)

    @pl.when(jnp.logical_not(bottom))
    def _():
        greet(lat - 1, east)
        greet(lat - 1, west)
        greet(lat - 1, lon)

    greet(lat, east)
    greet(lat, west)

    for load in loads[:3]:
        load.wait()
    sea8 = m_in[...].astype(F32)
    flip[: CIN * ROWS, :] = x_in[...].astype(F32).reshape(CIN * ROWS, LANES)
    flip[CIN * ROWS : (CIN + 1) * ROWS, :] = sea8
    flip[(CIN + 1) * ROWS : KX * ROWS, :] = jnp.zeros(((KX - CIN - 1) * ROWS, LANES), F32)
    flip[KX * ROWS :, :] = (c_in[...].astype(F32) * sea8[None]).reshape(CH * ROWS, LANES)
    for r in range(ROWS):
        f_ref[:, tile(r)] = flip[pl.ds(r, KX + CH, stride=ROWS), :].astype(BF)

    cell = lax.broadcasted_iota(jnp.int32, (32, ROWS * LANES), 0)
    place = lax.broadcasted_iota(jnp.int32, (32, ROWS * LANES), 1)
    want = ((cell % 16) // 2) * LANES + cell % 2 + jnp.where(cell < 16, LANES - 2, 0)
    picked = nt((place == want).astype(F32).astype(BF), f_ref[...]).astype(BF)
    mine[0] = picked[:16]
    mine[1] = picked[16:]

    folds = 1 + jnp.where(fold_e != lon, 1, 0) + jnp.where(fold_w != lon, 1, 0)
    pl.semaphore_wait(
        barrier,
        y_n + z_n + group - 3 + 2 + jnp.where(top, folds, 3) + jnp.where(bottom, 0, 3),
    )

    def send(src, dst, slot, a, b):
        return pltpu.make_async_remote_copy(
            src_ref=src, dst_ref=dst, send_sem=send_sem.at[slot], recv_sem=recv_sem.at[slot],
            device_id=(a, b), device_id_type=MESH,
        )

    low, high = f_ref.at[:, tile(0, 2)], f_ref.at[:, tile(ROWS - 2, 2)]
    above, below = xm.at[:, tile(ROWS + 2, 2)], xm.at[:, tile(0, 2)]

    @pl.when(top)
    def _():
        @pl.when(fold_e != lon)
        def _():
            send(mine.at[0], packs.at[3], 9, lat, fold_e).start()

        @pl.when(fold_w != lon)
        def _():
            send(mine.at[1], packs.at[2], 10, lat, fold_w).start()

        send(high, above, 6, lat, mirror).start()

        @pl.when(fold_e == lon)
        def _():
            packs[3] = mine[0]

        @pl.when(fold_w == lon)
        def _():
            packs[2] = mine[1]

    @pl.when(jnp.logical_not(bottom))
    def _():
        send(mine.at[0], packs.at[2], 2, lat - 1, east).start()
        send(mine.at[1], packs.at[3], 3, lat - 1, west).start()

    @pl.when(jnp.logical_not(top))
    def _():
        send(mine.at[0], packs.at[4], 4, lat + 1, east).start()
        send(mine.at[1], packs.at[5], 5, lat + 1, west).start()

    send(mine.at[0], packs.at[0], 0, lat, east).start()
    send(mine.at[1], packs.at[1], 1, lat, west).start()

    @pl.when(jnp.logical_not(top))
    def _():
        send(high, below, 7, lat + 1, lon).start()

    @pl.when(jnp.logical_not(bottom))
    def _():
        send(low, above, 8, lat - 1, lon).start()

    @pl.when(bottom)
    def _():
        xm[:, tile(0, 2)] = jnp.zeros((128, 2 * LANES), BF)
        packs[4] = jnp.zeros((16, 128), BF)
        packs[5] = jnp.zeros((16, 128), BF)

    xm[:, tile(2, ROWS)] = f_ref[...]
    zero = jnp.zeros((CH, LANES), BF)
    for dr in range(3):
        at = slice(dr * CH, (dr + 1) * CH)
        ae[at, tile(dr, ROWS)] = f_ref[KX:, :]
        for r in range(RIM):
            if not dr <= r < dr + ROWS:
                am[at, tile(r)] = zero
                ae[at, tile(r)] = zero

    k = lax.broadcasted_iota(jnp.int32, (96, 1), 0)
    slot, row, j = k // 16, (k % 16) // 2, k % 2
    row_to = jnp.where(slot < 2, row + 2, jnp.where(slot < 4, row + 10, row - 6))
    row_to = jnp.where((slot >= 2) & (slot < 4) & top, 17 - row, row_to)
    lane_to = jnp.where(slot % 2 == 0, LANES - 2 + j, j)
    lane_to = jnp.where((slot == 2) & top, LANES - 1 - j, lane_to)
    lane_to = jnp.where((slot == 3) & top, 1 - j, lane_to)
    good = (slot < 2) | ((slot < 4) & (row_to < EXT)) | ((slot >= 4) & (row_to >= 0))
    goal = jnp.where(good, row_to * LANES + lane_to, -1)

    loads[3].wait()
    loads[4].wait()
    gap = jnp.zeros((CH, KX - CIN), F32)
    k1 = [jnp.concatenate([w1_in[t].astype(F32), gap], axis=1) for t in range(9)]
    k2 = [w2_in[t].astype(F32) for t in range(9)]

    def square(k, pick):
        return jnp.concatenate(
            [jnp.concatenate([k[pick(a, b)] for b in range(3)], axis=1) for a in range(3)], axis=0
        )

    def plain(a, b):
        return 3 * a + b

    def turned(a, b):
        return 8 - 3 * a - b

    def swapped(a, b):
        return 3 * b + a

    def both(a, b):
        return 8 - 3 * b - a

    m = square(k1, plain)
    wa1[...] = m.astype(BF)
    wa1n[...] = jnp.where(top, square(k1, turned), m).astype(BF)
    wa2[...] = square(k2, plain).astype(BF)
    m = square(k2, both)
    tb2[...] = m.T.astype(BF)
    tb2n[...] = jnp.where(top, square(k2, swapped), m).T.astype(BF)
    m = square(k1, both)
    tb1[...] = m.T.astype(BF)
    tb1n[...] = jnp.where(top, square(k1, swapped), m).T.astype(BF)

    def landed(ref, slot):
        pltpu.make_async_copy(ref, ref, recv_sem.at[slot]).wait()

    landed(packs.at[0], 0)
    landed(packs.at[1], 1)

    @pl.when(jnp.logical_not(top))
    def _():
        landed(above, 8)
        landed(packs.at[2], 2)
        landed(packs.at[3], 3)

    @pl.when(top)
    def _():
        landed(above, 6)

        @pl.when(fold_e != lon)
        def _():
            landed(packs.at[3], 9)

        @pl.when(fold_w != lon)
        def _():
            landed(packs.at[2], 10)

        back = lax.broadcasted_iota(jnp.int32, (LANES, LANES), 0)
        back = back + lax.broadcasted_iota(jnp.int32, (LANES, LANES), 1)
        back = (back == LANES - 1).astype(F32).astype(BF)
        first = nn(xm[:, tile(ROWS + 2)], back).astype(BF)
        second = nn(xm[:, tile(ROWS + 3)], back).astype(BF)
        xm[:, tile(ROWS + 2)] = second
        xm[:, tile(ROWS + 3)] = first

    @pl.when(jnp.logical_not(bottom))
    def _():
        landed(below, 7)
        landed(packs.at[4], 4)
        landed(packs.at[5], 5)

    flat = jnp.concatenate([packs[s] for s in range(6)], axis=0)
    lanes96 = lax.broadcasted_iota(jnp.int32, (96, EXT * LANES), 1)
    xg[...] = tn(flat, (lanes96 == goal).astype(F32).astype(BF)).astype(BF)

    lane = lax.broadcasted_iota(jnp.int32, (1, LANES), 1)

    def shifts(main, ghost):
        main, ghost = main.astype(F32), ghost.astype(F32)
        left = (pltpu.roll(main, 1, 1), pltpu.roll(ghost, 1, 1))
        right = (pltpu.roll(main, LANES - 1, 1), pltpu.roll(ghost, LANES - 1, 1))
        a = jnp.where(lane == 0, left[1], left[0]).astype(BF)
        b = jnp.where(lane == LANES - 1, right[1], right[0]).astype(BF)
        ga = jnp.where(lane == 0, left[0], left[1]).astype(BF)
        gb = jnp.where(lane == LANES - 1, right[0], right[1]).astype(BF)
        return a, b, ga, gb

    for r in range(EXT):
        t = tile(r)
        main, ghost = xm[:, t], xg[:, t]
        a, b, ga, gb = shifts(main, ghost)
        for q, m, g in ((0, a, ga), (1, main, ghost), (2, b, gb)):
            d1m[q * KX : (q + 1) * KX, t] = m[:KX]
            d1g[q * KX : (q + 1) * KX, t] = g[:KX]
            d2m[q * CH : (q + 1) * CH, t] = m[KX:]
            d2g[q * CH : (q + 1) * CH, t] = g[KX:]

    def hidden(d1, d2, field):
        a = gather_rows(nn(wa1[...], d1[...]), RIM)
        last = gather_rows(nn(wa1n[...], d1[:, tile(RIM - 1, 3)]), 1)
        a = jnp.concatenate([a[:, : (RIM - 1) * LANES], last], axis=1)
        value, slope = gelu_parts(a)
        sea = field[CIN : CIN + 1, tile(1, RIM)].astype(F32)
        z = jnp.concatenate(
            [nn(tb2[...], d2[:, tile(0, RIM)]), nn(tb2n[...], d2[:, tile(RIM, 2)])], axis=1
        )
        grad = (gather_rows(z, RIM) * (slope * sea)).astype(BF)
        return (value * sea).astype(BF), grad

    hm, gm = hidden(d1m, d2m, xm)
    hg, gg = hidden(d1g, d2g, xg)
    for dr in range(3):
        am[dr * CH : (dr + 1) * CH, tile(dr, ROWS)] = gm[:, tile(1, ROWS)]
    for r in range(RIM):
        t = tile(r)
        for ref, main, ghost in ((hd, hm[:, t], hg[:, t]), (dad, gm[:, t], gg[:, t])):
            a, b, _, _ = shifts(main, ghost)
            ref[0:CH, t] = a
            ref[CH : 2 * CH, t] = main
            ref[2 * CH :, t] = b

    term2 = nt(ae[...], hd[...])
    term1 = nt(am[...], d1m[:, tile(1, RIM)])
    terms = jnp.concatenate([term1, term2], axis=1).astype(BF)
    for t in range(TILES):
        a, b = t // 3, t % 3
        gbuf[t // group, t % group] = terms[16 * a : 16 * a + 16, tile(b)]

    def pass_on(src, dst, sems, p, a, b):
        pltpu.make_async_remote_copy(
            src_ref=src, dst_ref=dst, send_sem=sems[0].at[p], recv_sem=sems[1].at[p],
            device_id=(a, b), device_id_type=MESH,
        ).start()

    def done(ref, count, sem):
        some = ref.at[pl.ds(0, count)]
        pltpu.make_async_copy(some, some, sem).wait()

    def total(ref, p, count):
        acc = ref[p, 0].astype(F32)
        for i in range(1, count):
            acc = acc + ref[p, i].astype(F32)
        return acc.astype(BF)

    def only(test, always, f):
        if always:
            f()
        else:
            pl.when(test)(f)

    parts = -(-TILES // group)
    count = [min(group, TILES - p * group) for p in range(parts)]
    first = [(z_n, z, at_z) if p % 2 == 0 else (y_n, y, at_y) for p in range(parts)]
    second = [(y_n, y, at_y) if p % 2 == 0 else (z_n, z, at_z) for p in range(parts)]

    for p in range(parts):
        for j in range(1, group):
            to, a, b = at_x(j)
            only(
                to < count[p], count[p] == group,
                functools.partial(pass_on, gbuf.at[p, to], rbuf.at[p, me], sem_rs, p, a, b),
            )

    sea = f_ref[CIN : CIN + 1, :].astype(F32)
    res = gather_rows(nn(wa2[...], hd[...]), ROWS) * sea
    for r in range(ROWS):
        flip[pl.ds(r, CH, stride=ROWS), :] = res[:, tile(r)]
    c_in[...] = flip[: CH * ROWS, :].reshape(CH, ROWS, LANES).astype(BF)
    stores = [pltpu.make_async_copy(c_in, out_ref, in_sem.at[0])]
    stores[0].start()
    v = jnp.concatenate(
        [nn(tb1[...], dad[:, tile(0, RIM - 1)]), nn(tb1n[...], dad[:, tile(RIM - 1)])], axis=1
    )
    res = gather_rows(v, ROWS)
    for r in range(ROWS):
        flip[pl.ds(r, KX, stride=ROWS), :] = res[:, tile(r)]
    x_in[...] = flip[: CIN * ROWS, :].reshape(CIN, ROWS, LANES).astype(BF)
    stores.append(pltpu.make_async_copy(x_in, dx_ref, in_sem.at[1]))
    stores[1].start()

    def hop(p, source, arrived, sem, held_as, axis, sems):
        length, at, peer = axis

        def go():
            done(source.at[p], arrived - 1, sem.at[p])
            held_as[p, at] = total(source, p, arrived)
            for j in far_first(length):
                pass_on(held_as.at[p, at], held_as.at[p, at], sems, p, *peer(j))

        only(me < count[p], count[p] == group, go)

    for p in range(parts):
        def own(p=p):
            rbuf[p, me] = gbuf[p, me]

        only(me < count[p], count[p] == group, own)
        hop(p, rbuf, group, sem_rs[1], ex1, first[p], sem_x1)
    for p in range(parts):
        hop(p, ex1, first[p][0], sem_x1[1], ex2, second[p], sem_x2)
    everyone = (group, me, lambda j: at_x(j)[1:])
    for p in range(parts):
        hop(p, ex2, second[p][0], sem_x2[1], obuf, everyone, sem_ag)
    for p in range(parts):
        if count[p] == group:
            done(obuf.at[p], group - 1, sem_ag[1].at[p])
        else:
            pl.when(me < count[p])(
                functools.partial(done, obuf.at[p], count[p] - 1, sem_ag[1].at[p])
            )
            pl.when(me >= count[p])(
                functools.partial(done, obuf.at[p], count[p], sem_ag[1].at[p])
            )
        n = count[p]
        move = pltpu.make_async_copy(obuf.at[p, pl.ds(0, n)], dw_ref.at[p, pl.ds(0, n)], out_sem.at[p])
        move.start()
        stores.append(move)

    def sent(ref, sem):
        pltpu.make_async_copy(ref, ref, sem).wait()

    sent(mine.at[0], send_sem.at[0])
    sent(mine.at[1], send_sem.at[1])

    @pl.when(jnp.logical_not(top))
    def _():
        sent(high, send_sem.at[7])
        sent(mine.at[0], send_sem.at[4])
        sent(mine.at[1], send_sem.at[5])

    @pl.when(top)
    def _():
        sent(high, send_sem.at[6])

        @pl.when(fold_e != lon)
        def _():
            sent(mine.at[0], send_sem.at[9])

        @pl.when(fold_w != lon)
        def _():
            sent(mine.at[1], send_sem.at[10])

    @pl.when(jnp.logical_not(bottom))
    def _():
        sent(low, send_sem.at[8])
        sent(mine.at[0], send_sem.at[2])
        sent(mine.at[1], send_sem.at[3])

    for p in range(parts):
        n = count[p]
        if n == group:
            done(gbuf.at[p], group - 1, sem_rs[0].at[p])
        else:
            pl.when(me < n)(functools.partial(done, gbuf.at[p], n - 1, sem_rs[0].at[p]))
            pl.when(me >= n)(functools.partial(done, gbuf.at[p], n, sem_rs[0].at[p]))

        def drain(p=p):
            done(ex1.at[p], first[p][0] - 1, sem_x1[0].at[p])
            done(ex2.at[p], second[p][0] - 1, sem_x2[0].at[p])
            done(rbuf.at[p], group - 1, sem_ag[0].at[p])

        only(me < n, n == group, drain)
    for store in stores:
        store.wait()


def finish(
    factor, parts, group,
    out_in, dx_in, dw_in, out_ref, dx_ref, dw1_ref, dw2_ref,
    tiles, dw1, dw2, get_sem, put_sem,
):
    get = pltpu.make_async_copy(dw_in, tiles, get_sem)
    puts = [
        pltpu.make_async_copy(src, dst, put_sem.at[i])
        for i, (src, dst) in enumerate(
            ((dw1, dw1_ref), (dw2, dw2_ref), (out_in, out_ref), (dx_in, dx_ref))
        )
    ]
    get.start()
    puts[2].start()
    puts[3].start()
    get.wait()
    for dr in range(3):
        grads = jnp.concatenate(
            [
                jnp.concatenate(
                    [tiles[t // group, t % group] for t in range(3 * a, 3 * a + 3)], axis=1
                )
                for a in range(3 * dr, 3 * dr + 3)
            ],
            axis=0,
        ).astype(F32) * factor
        for dc in range(3):
            dw1[3 * dr + dc] = grads[:, dc * KX : dc * KX + CIN]
            dw2[3 * dr + dc] = grads[:, 3 * KX + dc * CH : 3 * KX + (dc + 1) * CH]
    puts[0].start()
    puts[1].start()
    for put in puts:
        put.wait()


def body(dims, *inputs):
    xl_n, z_n, xh_n, y_n, c_n = dims
    group = xl_n * xh_n * c_n
    parts = -(-TILES // group)
    wide, slim, ring = EXT * LANES, RIM * LANES, max(y_n, z_n)
    anywhere = pl.BlockSpec(memory_space=pl.ANY)
    hbm = pl.BlockSpec(memory_space=pltpu.HBM)

    def held(*shape):
        return pltpu.VMEM(shape, BF)

    fields_like = (
        jax.ShapeDtypeStruct((CH, ROWS, LANES), BF),
        jax.ShapeDtypeStruct((CIN, ROWS, LANES), BF),
    )
    out, dx, dw = pl.pallas_call(
        functools.partial(kernel, dims),
        out_shape=fields_like + (jax.ShapeDtypeStruct((parts, group, 16, LANES), BF),),
        in_specs=[hbm] * 5,
        out_specs=(anywhere,) * 3,
        scratch_shapes=[
            held(CIN, ROWS, LANES), pltpu.VMEM((ROWS, LANES), jnp.int32),
            held(9, CH, CIN), held(9, CH, CH), held(CH, ROWS, LANES),
            pltpu.VMEM(((KX + CH) * ROWS, LANES), F32), held(KX + CH, ROWS * LANES),
            held(3 * CH, 3 * KX), held(3 * CH, 3 * KX), held(3 * CH, 3 * CH),
            held(3 * CH, 3 * CH), held(3 * CH, 3 * CH), held(3 * KX, 3 * CH), held(3 * KX, 3 * CH),
            held(128, wide), held(128, wide), held(6, 16, 128), held(2, 16, 128),
            held(3 * KX, wide), held(3 * KX, wide), held(3 * CH, wide), held(3 * CH, wide),
            held(3 * CH, slim), held(3 * CH, slim), held(3 * CH, slim), held(3 * CH, slim),
            held(parts, group, 16, LANES), held(parts, group, 16, LANES),
            held(parts, ring, 16, LANES), held(parts, ring, 16, LANES),
            held(parts, group, 16, LANES),
            pltpu.SemaphoreType.DMA((5,)), pltpu.SemaphoreType.DMA((parts,)),
            pltpu.SemaphoreType.DMA((11,)), pltpu.SemaphoreType.DMA((11,)),
        ] + [pltpu.SemaphoreType.DMA((parts,))] * 8,
        compiler_params=pltpu.CompilerParams(
            collective_id=0, has_side_effects=True, vmem_limit_bytes=24 * 1024 * 1024
        ),
    )(*(pltpu.with_memory_space_constraint(v, pltpu.HBM) for v in inputs))
    factor = 1.0 / math.sqrt(ROWS * LANES * xl_n * z_n * xh_n * y_n * c_n)
    return pl.pallas_call(
        functools.partial(finish, factor, parts, group),
        out_shape=fields_like + (
            jax.ShapeDtypeStruct((9, CH, CIN), F32),
            jax.ShapeDtypeStruct((9, CH, CH), F32),
        ),
        in_specs=[anywhere] * 3,
        out_specs=(hbm,) * 4,
        scratch_shapes=[
            held(parts, group, 16, LANES),
            pltpu.VMEM((9, CH, CIN), F32), pltpu.VMEM((9, CH, CH), F32),
            pltpu.SemaphoreType.DMA, pltpu.SemaphoreType.DMA((4,)),
        ],
        compiler_params=pltpu.CompilerParams(vmem_limit_bytes=8 * 1024 * 1024),
    )(out, dx, dw)


def solution(mesh):
    in_specs = (P(None, "lat", "lon"), P("lat", "lon"), P(), P(), P(None, "lat", "lon"))
    out_specs = (P(None, "lat", "lon"), P(None, "lat", "lon"), P(), P())
    nlat, nlon = mesh.shape["lat"], mesh.shape["lon"]
    x_hi = 2 if nlon > 4 else 1
    dims = (2, nlat // 2, x_hi, nlon // (2 * x_hi), 2)
    run = functools.partial(body, dims)
    return jax.shard_map(run, mesh=mesh, in_specs=in_specs, out_specs=out_specs, check_vma=False)
```

```python
import functools
import math

import jax
import jax.numpy as jnp
from jax import lax
from jax.experimental import pallas as pl
from jax.experimental.pallas import tpu as pltpu
from jax.sharding import PartitionSpec as P

MESH = pl.DeviceIdType.MESH
BF = jnp.bfloat16
F32 = jnp.float32
CIN, CH, KX = 75, 48, 80
ROWS, LANES = 8, 128
EXT = ROWS + 4
RIM = ROWS + 2
TILES = 27


def nn(a, b):
    return lax.dot_general(a, b, (((1,), (0,)), ((), ())), preferred_element_type=F32)


def nt(a, b):
    return lax.dot_general(a, b, (((1,), (1,)), ((), ())), preferred_element_type=F32)


def tn(a, b):
    return lax.dot_general(a, b, (((0,), (0,)), ((), ())), preferred_element_type=F32)


def gelu_parts(a):
    coeff = 0.7978845608
    inner = coeff * (a + 0.044715 * a * a * a)
    tval = jnp.tanh(inner)
    value = 0.5 * a * (1.0 + tval)
    slope = 0.5 * (1.0 + tval) + 0.5 * a * (1.0 - tval * tval) * coeff * (1.0 + 0.134145 * a * a)
    return (value, slope)


def tile(r, count=1):
    return slice(r * LANES, (r + count) * LANES)


def gather_rows(y, rows):
    n = rows * LANES
    c = y.shape[0] // 3
    return y[:c, :n] + y[c : 2 * c, LANES : LANES + n] + y[2 * c :, 2 * LANES : 2 * LANES + n]


def far_first(n):
    return sorted(range(1, n), key=lambda j: -min(j, n - j))


def kernel(
    dims,
    x_hbm, m_hbm, w1_hbm, w2_hbm, c_hbm,
    out_ref, dx_ref, dw_ref,
    x_in, m_in, w1_in, w2_in, c_in, flip, f_ref,
    wa1, wa1n, wa2, tb2, tb2n, tb1, tb1n,
    xm, xg, packs, mine, d1m, d1g, d2m, d2g, hd, dad, am, ae,
    gbuf, rbuf, ex1, ex2, obuf,
    in_sem, out_sem, send_sem, recv_sem, *red,
):
    sem_rs, sem_x1, sem_x2, sem_ag = red[0:2], red[2:4], red[4:6], red[6:8]
    xl_n, z_n, xh_n, y_n, c_n = dims
    nlat, nlon, group = xl_n * z_n, xh_n * y_n * c_n, xl_n * xh_n * c_n
    lat, lon = lax.axis_index("lat"), lax.axis_index("lon")
    xl, z = lat // z_n, lat % z_n
    xh, y, core = lon // (y_n * c_n), (lon // c_n) % y_n, lon % c_n
    me = (xl * xh_n + xh) * c_n + core
    top, bottom = lat == nlat - 1, lat == 0
    east, west = lax.rem(lon + 1, nlon), lax.rem(lon + nlon - 1, nlon)
    mirror = nlon - 1 - lon
    fold_e = lax.rem(2 * nlon - 2 - lon, nlon)
    fold_w = lax.rem(nlon - lon, nlon)

    def at_z(j):
        to = lax.rem(z + j, z_n)
        return xl * z_n + to, lon

    def at_y(j):
        to = lax.rem(y + j, y_n)
        return lat, (xh * y_n + to) * c_n + core

    def at_x(j):
        to = lax.rem(me + j, group)
        a, b, c = to // (xh_n * c_n), (to // c_n) % xh_n, to % c_n
        return to, a * z_n + z, (b * y_n + y) * c_n + c

    loads = [
        pltpu.make_async_copy(src, dst, in_sem.at[i])
        for i, (src, dst) in enumerate(
            ((x_hbm, x_in), (m_hbm, m_in), (c_hbm, c_in), (w1_hbm, w1_in), (w2_hbm, w2_in))
        )
    ]
    for load in loads:
        load.start()

    barrier = pltpu.get_barrier_semaphore()

    def greet(a, b):
        pl.semaphore_signal(barrier, inc=1, device_id=(a, b), device_id_type=MESH)

    @pl.when(top)
    def _():
        greet(lat, mirror)

        @pl.when(fold_e != lon)
        def _():
            greet(lat, fold_e)

        @pl.when(fold_w != lon)
        def _():
            greet(lat, fold_w)

    for j in far_first(y_n):
        greet(*at_y(j))
    for j in far_first(z_n):
        greet(*at_z(j))
    for j in range(1, group):
        greet(*at_x(j)[1:])

    @pl.when(jnp.logical_not(top))
    def _():
        greet(lat + 1, east)
        greet(lat + 1, west)
        greet(lat + 1, lon)

    @pl.when(jnp.logical_not(bottom))
    def _():
        greet(lat - 1, east)
        greet(lat - 1, west)
        greet(lat - 1, lon)

    greet(lat, east)
    greet(lat, west)

    for load in loads[:3]:
        load.wait()
    sea8 = m_in[...].astype(F32)
    flip[: CIN * ROWS, :] = x_in[...].astype(F32).reshape(CIN * ROWS, LANES)
    flip[CIN * ROWS : (CIN + 1) * ROWS, :] = sea8
    flip[(CIN + 1) * ROWS : KX * ROWS, :] = jnp.zeros(((KX - CIN - 1) * ROWS, LANES), F32)
    flip[KX * ROWS :, :] = (c_in[...].astype(F32) * sea8[None]).reshape(CH * ROWS, LANES)
    for r in range(ROWS):
        f_ref[:, tile(r)] = flip[pl.ds(r, KX + CH, stride=ROWS), :].astype(BF)

    cell = lax.broadcasted_iota(jnp.int32, (32, ROWS * LANES), 0)
    place = lax.broadcasted_iota(jnp.int32, (32, ROWS * LANES), 1)
    want = ((cell % 16) // 2) * LANES + cell % 2 + jnp.where(cell < 16, LANES - 2, 0)
    picked = nt((place == want).astype(F32).astype(BF), f_ref[...]).astype(BF)
    mine[0] = picked[:16]
    mine[1] = picked[16:]

    folds = 1 + jnp.where(fold_e != lon, 1, 0) + jnp.where(fold_w != lon, 1, 0)
    pl.semaphore_wait(
        barrier,
        y_n + z_n + group - 3 + 2 + jnp.where(top, folds, 3) + jnp.where(bottom, 0, 3),
    )

    def send(src, dst, slot, a, b):
        return pltpu.make_async_remote_copy(
            src_ref=src, dst_ref=dst, send_sem=send_sem.at[slot], recv_sem=recv_sem.at[slot],
            device_id=(a, b), device_id_type=MESH,
        )

    low, high = f_ref.at[:, tile(0, 2)], f_ref.at[:, tile(ROWS - 2, 2)]
    above, below = xm.at[:, tile(ROWS + 2, 2)], xm.at[:, tile(0, 2)]

    @pl.when(top)
    def _():
        @pl.when(fold_e != lon)
        def _():
            send(mine.at[0], packs.at[3], 9, lat, fold_e).start()

        @pl.when(fold_w != lon)
        def _():
            send(mine.at[1], packs.at[2], 10, lat, fold_w).start()

        @pl.when(fold_e == lon)
        def _():
            packs[3] = mine[0]

        @pl.when(fold_w == lon)
        def _():
            packs[2] = mine[1]

    @pl.when(jnp.logical_not(bottom))
    def _():
        send(mine.at[0], packs.at[2], 2, lat - 1, east).start()
        send(mine.at[1], packs.at[3], 3, lat - 1, west).start()

    @pl.when(jnp.logical_not(top))
    def _():
        send(mine.at[0], packs.at[4], 4, lat + 1, east).start()
        send(mine.at[1], packs.at[5], 5, lat + 1, west).start()

    send(mine.at[0], packs.at[0], 0, lat, east).start()
    send(mine.at[1], packs.at[1], 1, lat, west).start()

    @pl.when(jnp.logical_not(top))
    def _():
        send(high, below, 7, lat + 1, lon).start()

    @pl.when(jnp.logical_not(bottom))
    def _():
        send(low, above, 8, lat - 1, lon).start()

    @pl.when(top)
    def _():
        send(high, above, 6, lat, mirror).start()

    @pl.when(bottom)
    def _():
        xm[:, tile(0, 2)] = jnp.zeros((128, 2 * LANES), BF)
        packs[4] = jnp.zeros((16, 128), BF)
        packs[5] = jnp.zeros((16, 128), BF)

    xm[:, tile(2, ROWS)] = f_ref[...]
    zero = jnp.zeros((CH, LANES), BF)
    for dr in range(3):
        at = slice(dr * CH, (dr + 1) * CH)
        ae[at, tile(dr, ROWS)] = f_ref[KX:, :]
        for r in range(RIM):
            if not dr <= r < dr + ROWS:
                am[at, tile(r)] = zero
                ae[at, tile(r)] = zero

    k = lax.broadcasted_iota(jnp.int32, (96, 1), 0)
    slot, row, j = k // 16, (k % 16) // 2, k % 2
    row_to = jnp.where(slot < 2, row + 2, jnp.where(slot < 4, row + 10, row - 6))
    row_to = jnp.where((slot >= 2) & (slot < 4) & top, 17 - row, row_to)
    lane_to = jnp.where(slot % 2 == 0, LANES - 2 + j, j)
    lane_to = jnp.where((slot == 2) & top, LANES - 1 - j, lane_to)
    lane_to = jnp.where((slot == 3) & top, 1 - j, lane_to)
    good = (slot < 2) | ((slot < 4) & (row_to < EXT)) | ((slot >= 4) & (row_to >= 0))
    goal = jnp.where(good, row_to * LANES + lane_to, -1)

    loads[3].wait()
    loads[4].wait()
    gap = jnp.zeros((CH, KX - CIN), F32)
    k1 = [jnp.concatenate([w1_in[t].astype(F32), gap], axis=1) for t in range(9)]
    k2 = [w2_in[t].astype(F32) for t in range(9)]

    def square(k, pick):
        return jnp.concatenate(
            [jnp.concatenate([k[pick(a, b)] for b in range(3)], axis=1) for a in range(3)], axis=0
        )

    def plain(a, b):
        return 3 * a + b

    def turned(a, b):
        return 8 - 3 * a - b

    def swapped(a, b):
        return 3 * b + a

    def both(a, b):
        return 8 - 3 * b - a

    m = square(k1, plain)
    wa1[...] = m.astype(BF)
    wa1n[...] = jnp.where(top, square(k1, turned), m).astype(BF)
    wa2[...] = square(k2, plain).astype(BF)
    m = square(k2, both)
    tb2[...] = m.T.astype(BF)
    tb2n[...] = jnp.where(top, square(k2, swapped), m).T.astype(BF)
    m = square(k1, both)
    tb1[...] = m.T.astype(BF)
    tb1n[...] = jnp.where(top, square(k1, swapped), m).T.astype(BF)

    def landed(ref, slot):
        pltpu.make_async_copy(ref, ref, recv_sem.at[slot]).wait()

    landed(packs.at[0], 0)
    landed(packs.at[1], 1)

    @pl.when(jnp.logical_not(top))
    def _():
        landed(above, 8)
        landed(packs.at[2], 2)
        landed(packs.at[3], 3)

    @pl.when(top)
    def _():
        landed(above, 6)

        @pl.when(fold_e != lon)
        def _():
            landed(packs.at[3], 9)

        @pl.when(fold_w != lon)
        def _():
            landed(packs.at[2], 10)

        back = lax.broadcasted_iota(jnp.int32, (LANES, LANES), 0)
        back = back + lax.broadcasted_iota(jnp.int32, (LANES, LANES), 1)
        back = (back == LANES - 1).astype(F32).astype(BF)
        first = nn(xm[:, tile(ROWS + 2)], back).astype(BF)
        second = nn(xm[:, tile(ROWS + 3)], back).astype(BF)
        xm[:, tile(ROWS + 2)] = second
        xm[:, tile(ROWS + 3)] = first

    @pl.when(jnp.logical_not(bottom))
    def _():
        landed(below, 7)
        landed(packs.at[4], 4)
        landed(packs.at[5], 5)

    flat = jnp.concatenate([packs[s] for s in range(6)], axis=0)
    lanes96 = lax.broadcasted_iota(jnp.int32, (96, EXT * LANES), 1)
    xg[...] = tn(flat, (lanes96 == goal).astype(F32).astype(BF)).astype(BF)

    lane = lax.broadcasted_iota(jnp.int32, (1, LANES), 1)

    def shifts(main, ghost):
        main, ghost = main.astype(F32), ghost.astype(F32)
        left = (pltpu.roll(main, 1, 1), pltpu.roll(ghost, 1, 1))
        right = (pltpu.roll(main, LANES - 1, 1), pltpu.roll(ghost, LANES - 1, 1))
        a = jnp.where(lane == 0, left[1], left[0]).astype(BF)
        b = jnp.where(lane == LANES - 1, right[1], right[0]).astype(BF)
        ga = jnp.where(lane == 0, left[0], left[1]).astype(BF)
        gb = jnp.where(lane == LANES - 1, right[0], right[1]).astype(BF)
        return a, b, ga, gb

    for r in range(EXT):
        t = tile(r)
        main, ghost = xm[:, t], xg[:, t]
        a, b, ga, gb = shifts(main, ghost)
        for q, m, g in ((0, a, ga), (1, main, ghost), (2, b, gb)):
            d1m[q * KX : (q + 1) * KX, t] = m[:KX]
            d1g[q * KX : (q + 1) * KX, t] = g[:KX]
            d2m[q * CH : (q + 1) * CH, t] = m[KX:]
            d2g[q * CH : (q + 1) * CH, t] = g[KX:]

    def hidden(d1, d2, field):
        a = gather_rows(nn(wa1[...], d1[...]), RIM)
        last = gather_rows(nn(wa1n[...], d1[:, tile(RIM - 1, 3)]), 1)
        a = jnp.concatenate([a[:, : (RIM - 1) * LANES], last], axis=1)
        value, slope = gelu_parts(a)
        sea = field[CIN : CIN + 1, tile(1, RIM)].astype(F32)
        z = jnp.concatenate(
            [nn(tb2[...], d2[:, tile(0, RIM)]), nn(tb2n[...], d2[:, tile(RIM, 2)])], axis=1
        )
        grad = (gather_rows(z, RIM) * (slope * sea)).astype(BF)
        return (value * sea).astype(BF), grad

    hm, gm = hidden(d1m, d2m, xm)
    hg, gg = hidden(d1g, d2g, xg)
    for dr in range(3):
        am[dr * CH : (dr + 1) * CH, tile(dr, ROWS)] = gm[:, tile(1, ROWS)]
    for r in range(RIM):
        t = tile(r)
        for ref, main, ghost in ((hd, hm[:, t], hg[:, t]), (dad, gm[:, t], gg[:, t])):
            a, b, _, _ = shifts(main, ghost)
            ref[0:CH, t] = a
            ref[CH : 2 * CH, t] = main
            ref[2 * CH :, t] = b

    term2 = nt(ae[...], hd[...])
    term1 = nt(am[...], d1m[:, tile(1, RIM)])
    terms = jnp.concatenate([term1, term2], axis=1).astype(BF)
    for t in range(TILES):
        a, b = t // 3, t % 3
        gbuf[t // group, t % group] = terms[16 * a : 16 * a + 16, tile(b)]

    def pass_on(src, dst, sems, p, a, b):
        pltpu.make_async_remote_copy(
            src_ref=src, dst_ref=dst, send_sem=sems[0].at[p], recv_sem=sems[1].at[p],
            device_id=(a, b), device_id_type=MESH,
        ).start()

    def done(ref, count, sem):
        some = ref.at[pl.ds(0, count)]
        pltpu.make_async_copy(some, some, sem).wait()

    def total(ref, p, count):
        acc = ref[p, 0].astype(F32)
        for i in range(1, count):
            acc = acc + ref[p, i].astype(F32)
        return acc.astype(BF)

    def only(test, always, f):
        if always:
            f()
        else:
            pl.when(test)(f)

    parts = -(-TILES // group)
    count = [min(group, TILES - p * group) for p in range(parts)]
    by_z = {j: at_z(j) for j in range(1, z_n)}
    by_y = {j: at_y(j) for j in range(1, y_n)}
    axes = ((z_n, z, by_z.get), (y_n, y, by_y.get))
    first = [axes[p % 2] for p in range(parts)]
    second = [axes[1 - p % 2] for p in range(parts)]

    by_x = {j: at_x(j) for j in range(1, group)}
    for p in range(parts):
        for j in range(1, group):
            to, a, b = by_x[j]
            only(
                to < count[p], count[p] == group,
                functools.partial(pass_on, gbuf.at[p, to], rbuf.at[p, me], sem_rs, p, a, b),
            )

    def hop(p, source, arrived, sem, held_as, axis, sems):
        length, at, peer = axis

        def go():
            done(source.at[p], arrived - 1, sem.at[p])
            held_as[p, at] = total(source, p, arrived)
            for j in far_first(length):
                pass_on(held_as.at[p, at], held_as.at[p, at], sems, p, *peer(j))

        only(me < count[p], count[p] == group, go)

    for p in range(parts):
        def own(p=p):
            rbuf[p, me] = gbuf[p, me]

        only(me < count[p], count[p] == group, own)
        hop(p, rbuf, group, sem_rs[1], ex1, first[p], sem_x1)
    sea = f_ref[CIN : CIN + 1, :].astype(F32)
    res = gather_rows(nn(wa2[...], hd[...]), ROWS) * sea
    for r in range(ROWS):
        flip[pl.ds(r, CH, stride=ROWS), :] = res[:, tile(r)]
    c_in[...] = flip[: CH * ROWS, :].reshape(CH, ROWS, LANES).astype(BF)
    stores = [pltpu.make_async_copy(c_in, out_ref, in_sem.at[0])]
    stores[0].start()

    for p in range(parts):
        hop(p, ex1, first[p][0], sem_x1[1], ex2, second[p], sem_x2)

    v = jnp.concatenate(
        [nn(tb1[...], dad[:, tile(0, RIM - 1)]), nn(tb1n[...], dad[:, tile(RIM - 1)])], axis=1
    )
    res = gather_rows(v, ROWS)
    for r in range(ROWS):
        flip[pl.ds(r, KX, stride=ROWS), :] = res[:, tile(r)]
    x_in[...] = flip[: CIN * ROWS, :].reshape(CIN, ROWS, LANES).astype(BF)
    stores.append(pltpu.make_async_copy(x_in, dx_ref, in_sem.at[1]))
    stores[1].start()

    everyone = (group, me, lambda j: by_x[j][1:])
    for p in range(parts):
        hop(p, ex2, second[p][0], sem_x2[1], obuf, everyone, sem_ag)
    for p in range(parts):
        if count[p] == group:
            done(obuf.at[p], group - 1, sem_ag[1].at[p])
        else:
            pl.when(me < count[p])(
                functools.partial(done, obuf.at[p], count[p] - 1, sem_ag[1].at[p])
            )
            pl.when(me >= count[p])(
                functools.partial(done, obuf.at[p], count[p], sem_ag[1].at[p])
            )
        n = count[p]
        move = pltpu.make_async_copy(obuf.at[p, pl.ds(0, n)], dw_ref.at[p, pl.ds(0, n)], out_sem.at[p])
        move.start()
        stores.append(move)

    def sent(ref, sem):
        pltpu.make_async_copy(ref, ref, sem).wait()

    sent(mine.at[0], send_sem.at[0])
    sent(mine.at[1], send_sem.at[1])

    @pl.when(jnp.logical_not(top))
    def _():
        sent(high, send_sem.at[7])
        sent(mine.at[0], send_sem.at[4])
        sent(mine.at[1], send_sem.at[5])

    @pl.when(top)
    def _():
        sent(high, send_sem.at[6])

        @pl.when(fold_e != lon)
        def _():
            sent(mine.at[0], send_sem.at[9])

        @pl.when(fold_w != lon)
        def _():
            sent(mine.at[1], send_sem.at[10])

    @pl.when(jnp.logical_not(bottom))
    def _():
        sent(low, send_sem.at[8])
        sent(mine.at[0], send_sem.at[2])
        sent(mine.at[1], send_sem.at[3])

    for p in range(parts):
        n = count[p]
        if n == group:
            done(gbuf.at[p], group - 1, sem_rs[0].at[p])
        else:
            pl.when(me < n)(functools.partial(done, gbuf.at[p], n - 1, sem_rs[0].at[p]))
            pl.when(me >= n)(functools.partial(done, gbuf.at[p], n, sem_rs[0].at[p]))

        def drain(p=p):
            done(ex1.at[p], first[p][0] - 1, sem_x1[0].at[p])
            done(ex2.at[p], second[p][0] - 1, sem_x2[0].at[p])
            done(rbuf.at[p], group - 1, sem_ag[0].at[p])

        only(me < n, n == group, drain)
    for store in stores:
        store.wait()


def finish(
    factor, parts, group,
    out_in, dx_in, dw_in, out_ref, dx_ref, dw1_ref, dw2_ref,
    tiles, dw1, dw2, get_sem, put_sem,
):
    get = pltpu.make_async_copy(dw_in, tiles, get_sem)
    puts = [
        pltpu.make_async_copy(src, dst, put_sem.at[i])
        for i, (src, dst) in enumerate(
            ((dw1, dw1_ref), (dw2, dw2_ref), (out_in, out_ref), (dx_in, dx_ref))
        )
    ]
    get.start()
    puts[2].start()
    puts[3].start()
    get.wait()
    for dr in range(3):
        grads = jnp.concatenate(
            [
                jnp.concatenate(
                    [tiles[t // group, t % group] for t in range(3 * a, 3 * a + 3)], axis=1
                )
                for a in range(3 * dr, 3 * dr + 3)
            ],
            axis=0,
        ).astype(F32) * factor
        for dc in range(3):
            dw1[3 * dr + dc] = grads[:, dc * KX : dc * KX + CIN]
            dw2[3 * dr + dc] = grads[:, 3 * KX + dc * CH : 3 * KX + (dc + 1) * CH]
    puts[0].start()
    puts[1].start()
    for put in puts:
        put.wait()


def body(dims, *inputs):
    xl_n, z_n, xh_n, y_n, c_n = dims
    group = xl_n * xh_n * c_n
    parts = -(-TILES // group)
    wide, slim, ring = EXT * LANES, RIM * LANES, max(y_n, z_n)
    anywhere = pl.BlockSpec(memory_space=pl.ANY)
    hbm = pl.BlockSpec(memory_space=pltpu.HBM)

    def held(*shape):
        return pltpu.VMEM(shape, BF)

    fields_like = (
        jax.ShapeDtypeStruct((CH, ROWS, LANES), BF),
        jax.ShapeDtypeStruct((CIN, ROWS, LANES), BF),
    )
    out, dx, dw = pl.pallas_call(
        functools.partial(kernel, dims),
        out_shape=fields_like + (jax.ShapeDtypeStruct((parts, group, 16, LANES), BF),),
        in_specs=[hbm] * 5,
        out_specs=(anywhere,) * 3,
        scratch_shapes=[
            held(CIN, ROWS, LANES), pltpu.VMEM((ROWS, LANES), jnp.int32),
            held(9, CH, CIN), held(9, CH, CH), held(CH, ROWS, LANES),
            pltpu.VMEM(((KX + CH) * ROWS, LANES), F32), held(KX + CH, ROWS * LANES),
            held(3 * CH, 3 * KX), held(3 * CH, 3 * KX), held(3 * CH, 3 * CH),
            held(3 * CH, 3 * CH), held(3 * CH, 3 * CH), held(3 * KX, 3 * CH), held(3 * KX, 3 * CH),
            held(128, wide), held(128, wide), held(6, 16, 128), held(2, 16, 128),
            held(3 * KX, wide), held(3 * KX, wide), held(3 * CH, wide), held(3 * CH, wide),
            held(3 * CH, slim), held(3 * CH, slim), held(3 * CH, slim), held(3 * CH, slim),
            held(parts, group, 16, LANES), held(parts, group, 16, LANES),
            held(parts, ring, 16, LANES), held(parts, ring, 16, LANES),
            held(parts, group, 16, LANES),
            pltpu.SemaphoreType.DMA((5,)), pltpu.SemaphoreType.DMA((parts,)),
            pltpu.SemaphoreType.DMA((11,)), pltpu.SemaphoreType.DMA((11,)),
        ] + [pltpu.SemaphoreType.DMA((parts,))] * 8,
        compiler_params=pltpu.CompilerParams(
            collective_id=0, has_side_effects=True, vmem_limit_bytes=24 * 1024 * 1024
        ),
    )(*(pltpu.with_memory_space_constraint(v, pltpu.HBM) for v in inputs))
    factor = 1.0 / math.sqrt(ROWS * LANES * xl_n * z_n * xh_n * y_n * c_n)
    return pl.pallas_call(
        functools.partial(finish, factor, parts, group),
        out_shape=fields_like + (
            jax.ShapeDtypeStruct((9, CH, CIN), F32),
            jax.ShapeDtypeStruct((9, CH, CH), F32),
        ),
        in_specs=[anywhere] * 3,
        out_specs=(hbm,) * 4,
        scratch_shapes=[
            held(parts, group, 16, LANES),
            pltpu.VMEM((9, CH, CIN), F32), pltpu.VMEM((9, CH, CH), F32),
            pltpu.SemaphoreType.DMA, pltpu.SemaphoreType.DMA((4,)),
        ],
        compiler_params=pltpu.CompilerParams(vmem_limit_bytes=8 * 1024 * 1024),
    )(out, dx, dw)


def solution(mesh):
    in_specs = (P(None, "lat", "lon"), P("lat", "lon"), P(), P(), P(None, "lat", "lon"))
    out_specs = (P(None, "lat", "lon"), P(None, "lat", "lon"), P(), P())
    nlat, nlon = mesh.shape["lat"], mesh.shape["lon"]
    x_hi = 2 if nlon > 4 else 1
    dims = (2, nlat // 2, x_hi, nlon // (2 * x_hi), 2)
    run = functools.partial(body, dims)
    return jax.shard_map(run, mesh=mesh, in_specs=in_specs, out_specs=out_specs, check_vma=False)
```

```python
import functools
import math

import jax
import jax.numpy as jnp
from jax import lax
from jax.experimental import pallas as pl
from jax.experimental.pallas import tpu as pltpu
from jax.sharding import PartitionSpec as P

MESH = pl.DeviceIdType.MESH
BF = jnp.bfloat16
F32 = jnp.float32
CIN, CH, KX = 75, 48, 80
ROWS, LANES = 8, 128
EXT = ROWS + 4
RIM = ROWS + 2
TILES = 27


def nn(a, b):
    return lax.dot_general(a, b, (((1,), (0,)), ((), ())), preferred_element_type=F32)


def nt(a, b):
    return lax.dot_general(a, b, (((1,), (1,)), ((), ())), preferred_element_type=F32)


def tn(a, b):
    return lax.dot_general(a, b, (((0,), (0,)), ((), ())), preferred_element_type=F32)


def gelu_parts(a):
    coeff = 0.7978845608
    inner = coeff * (a + 0.044715 * a * a * a)
    tval = jnp.tanh(inner)
    value = 0.5 * a * (1.0 + tval)
    slope = 0.5 * (1.0 + tval) + 0.5 * a * (1.0 - tval * tval) * coeff * (1.0 + 0.134145 * a * a)
    return (value, slope)


def tile(r, count=1):
    return slice(r * LANES, (r + count) * LANES)


def gather_rows(y, rows):
    n = rows * LANES
    c = y.shape[0] // 3
    return y[:c, :n] + y[c : 2 * c, LANES : LANES + n] + y[2 * c :, 2 * LANES : 2 * LANES + n]


def far_first(n):
    return sorted(range(1, n), key=lambda j: -min(j, n - j))


def kernel(
    dims,
    x_hbm, m_hbm, w1_hbm, w2_hbm, c_hbm,
    out_ref, dx_ref, dw_ref,
    x_in, m_in, w1_in, w2_in, c_in, flip, f_ref,
    wa1, wa1n, wa2, tb2, tb2n, tb1, tb1n,
    xm, xg, packs, mine, d1m, d1g, d2m, d2g, hd, dad, am, ae,
    gbuf, rbuf, ex1, ex2, obuf,
    in_sem, out_sem, send_sem, recv_sem, *red,
):
    sem_rs, sem_x1, sem_x2, sem_ag = red[0:2], red[2:4], red[4:6], red[6:8]
    xl_n, z_n, xh_n, y_n, c_n = dims
    nlat, nlon, group = xl_n * z_n, xh_n * y_n * c_n, xl_n * xh_n * c_n
    lat, lon = lax.axis_index("lat"), lax.axis_index("lon")
    xl, z = lat // z_n, lat % z_n
    xh, y, core = lon // (y_n * c_n), (lon // c_n) % y_n, lon % c_n
    me = (xl * xh_n + xh) * c_n + core
    top, bottom = lat == nlat - 1, lat == 0
    east, west = lax.rem(lon + 1, nlon), lax.rem(lon + nlon - 1, nlon)
    mirror = nlon - 1 - lon
    fold_e = lax.rem(2 * nlon - 2 - lon, nlon)
    fold_w = lax.rem(nlon - lon, nlon)

    def at_z(j):
        to = lax.rem(z + j, z_n)
        return xl * z_n + to, lon

    def at_y(j):
        to = lax.rem(y + j, y_n)
        return lat, (xh * y_n + to) * c_n + core

    def at_x(j):
        to = lax.rem(me + j, group)
        a, b, c = to // (xh_n * c_n), (to // c_n) % xh_n, to % c_n
        return to, a * z_n + z, (b * y_n + y) * c_n + c

    loads = [
        pltpu.make_async_copy(src, dst, in_sem.at[i])
        for i, (src, dst) in enumerate(
            ((x_hbm, x_in), (m_hbm, m_in), (c_hbm, c_in), (w1_hbm, w1_in), (w2_hbm, w2_in))
        )
    ]
    for load in loads:
        load.start()

    barrier = pltpu.get_barrier_semaphore()

    def greet(a, b):
        pl.semaphore_signal(barrier, inc=1, device_id=(a, b), device_id_type=MESH)

    @pl.when(top)
    def _():
        greet(lat, mirror)

        @pl.when(fold_e != lon)
        def _():
            greet(lat, fold_e)

        @pl.when(fold_w != lon)
        def _():
            greet(lat, fold_w)

    for j in far_first(y_n):
        greet(*at_y(j))
    for j in far_first(z_n):
        greet(*at_z(j))
    for j in range(1, group):
        greet(*at_x(j)[1:])

    @pl.when(jnp.logical_not(top))
    def _():
        greet(lat + 1, east)
        greet(lat + 1, west)
        greet(lat + 1, lon)

    @pl.when(jnp.logical_not(bottom))
    def _():
        greet(lat - 1, east)
        greet(lat - 1, west)
        greet(lat - 1, lon)

    greet(lat, east)
    greet(lat, west)

    for load in loads[:3]:
        load.wait()
    sea8 = m_in[...].astype(F32)
    flip[: CIN * ROWS, :] = x_in[...].astype(F32).reshape(CIN * ROWS, LANES)
    flip[CIN * ROWS : (CIN + 1) * ROWS, :] = sea8
    flip[(CIN + 1) * ROWS : KX * ROWS, :] = jnp.zeros(((KX - CIN - 1) * ROWS, LANES), F32)
    flip[KX * ROWS :, :] = (c_in[...].astype(F32) * sea8[None]).reshape(CH * ROWS, LANES)
    for r in range(ROWS):
        f_ref[:, tile(r)] = flip[pl.ds(r, KX + CH, stride=ROWS), :].astype(BF)

    cell = lax.broadcasted_iota(jnp.int32, (32, ROWS * LANES), 0)
    place = lax.broadcasted_iota(jnp.int32, (32, ROWS * LANES), 1)
    want = ((cell % 16) // 2) * LANES + cell % 2 + jnp.where(cell < 16, LANES - 2, 0)
    picked = nt((place == want).astype(F32).astype(BF), f_ref[...]).astype(BF)
    mine[0] = picked[:16]
    mine[1] = picked[16:]

    folds = 1 + jnp.where(fold_e != lon, 1, 0) + jnp.where(fold_w != lon, 1, 0)
    pl.semaphore_wait(
        barrier,
        y_n + z_n + group - 3 + 2 + jnp.where(top, folds, 3) + jnp.where(bottom, 0, 3),
    )

    def send(src, dst, slot, a, b):
        return pltpu.make_async_remote_copy(
            src_ref=src, dst_ref=dst, send_sem=send_sem.at[slot], recv_sem=recv_sem.at[slot],
            device_id=(a, b), device_id_type=MESH,
        )

    low, high = f_ref.at[:, tile(0, 2)], f_ref.at[:, tile(ROWS - 2, 2)]
    above, below = xm.at[:, tile(ROWS + 2, 2)], xm.at[:, tile(0, 2)]

    @pl.when(top)
    def _():
        @pl.when(fold_e != lon)
        def _():
            send(mine.at[0], packs.at[3], 9, lat, fold_e).start()

        @pl.when(fold_w != lon)
        def _():
            send(mine.at[1], packs.at[2], 10, lat, fold_w).start()

        @pl.when(fold_e == lon)
        def _():
            packs[3] = mine[0]

        @pl.when(fold_w == lon)
        def _():
            packs[2] = mine[1]

    @pl.when(jnp.logical_not(bottom))
    def _():
        send(mine.at[0], packs.at[2], 2, lat - 1, east).start()
        send(mine.at[1], packs.at[3], 3, lat - 1, west).start()

    @pl.when(jnp.logical_not(top))
    def _():
        send(mine.at[0], packs.at[4], 4, lat + 1, east).start()
        send(mine.at[1], packs.at[5], 5, lat + 1, west).start()

    send(mine.at[0], packs.at[0], 0, lat, east).start()
    send(mine.at[1], packs.at[1], 1, lat, west).start()

    @pl.when(jnp.logical_not(top))
    def _():
        send(high, below, 7, lat + 1, lon).start()

    @pl.when(jnp.logical_not(bottom))
    def _():
        send(low, above, 8, lat - 1, lon).start()

    @pl.when(top)
    def _():
        send(high, above, 6, lat, mirror).start()

    @pl.when(bottom)
    def _():
        xm[:, tile(0, 2)] = jnp.zeros((128, 2 * LANES), BF)
        packs[4] = jnp.zeros((16, 128), BF)
        packs[5] = jnp.zeros((16, 128), BF)

    xm[:, tile(2, ROWS)] = f_ref[...]
    zero = jnp.zeros((CH, LANES), BF)
    for dr in range(3):
        at = slice(dr * CH, (dr + 1) * CH)
        ae[at, tile(dr, ROWS)] = f_ref[KX:, :]
        for r in range(RIM):
            if not dr <= r < dr + ROWS:
                am[at, tile(r)] = zero
                ae[at, tile(r)] = zero

    def select(cells, slot, tiles, base):
        k = lax.broadcasted_iota(jnp.int32, (cells, 1), 0)
        slot, row, j = slot(k // 16), (k % 16) // 2, k % 2
        row_to = jnp.where(slot < 2, row + 2, jnp.where(slot < 4, row + 10, row - 6))
        row_to = jnp.where((slot >= 2) & (slot < 4) & top, 17 - row, row_to)
        lane_to = jnp.where(slot % 2 == 0, LANES - 2 + j, j)
        lane_to = jnp.where((slot == 2) & top, LANES - 1 - j, lane_to)
        lane_to = jnp.where((slot == 3) & top, 1 - j, lane_to)
        good = (slot < 2) | ((slot < 4) & (row_to < EXT)) | ((slot >= 4) & (row_to >= 0))
        goal = jnp.where(good, (row_to - base) * LANES + lane_to, -1)
        place = lax.broadcasted_iota(jnp.int32, (cells, tiles * LANES), 1)
        return (place == goal).astype(F32).astype(BF)

    loads[3].wait()
    loads[4].wait()
    gap = jnp.zeros((CH, KX - CIN), F32)
    k1 = [jnp.concatenate([w1_in[t].astype(F32), gap], axis=1) for t in range(9)]
    k2 = [w2_in[t].astype(F32) for t in range(9)]

    def square(k, pick):
        return jnp.concatenate(
            [jnp.concatenate([k[pick(a, b)] for b in range(3)], axis=1) for a in range(3)], axis=0
        )

    def plain(a, b):
        return 3 * a + b

    def turned(a, b):
        return 8 - 3 * a - b

    def swapped(a, b):
        return 3 * b + a

    def both(a, b):
        return 8 - 3 * b - a

    m = square(k1, plain)
    wa1[...] = m.astype(BF)
    wa1n[...] = jnp.where(top, square(k1, turned), m).astype(BF)
    wa2[...] = square(k2, plain).astype(BF)
    m = square(k2, both)
    tb2[...] = m.T.astype(BF)
    tb2n[...] = jnp.where(top, square(k2, swapped), m).T.astype(BF)
    m = square(k1, both)
    tb1[...] = m.T.astype(BF)
    tb1n[...] = jnp.where(top, square(k1, swapped), m).T.astype(BF)

    def landed(ref, slot):
        pltpu.make_async_copy(ref, ref, recv_sem.at[slot]).wait()

    lane = lax.broadcasted_iota(jnp.int32, (1, LANES), 1)

    def shifts(main, ghost):
        main, ghost = main.astype(F32), ghost.astype(F32)
        left = (pltpu.roll(main, 1, 1), pltpu.roll(ghost, 1, 1))
        right = (pltpu.roll(main, LANES - 1, 1), pltpu.roll(ghost, LANES - 1, 1))
        a = jnp.where(lane == 0, left[1], left[0]).astype(BF)
        b = jnp.where(lane == LANES - 1, right[1], right[0]).astype(BF)
        ga = jnp.where(lane == 0, left[0], left[1]).astype(BF)
        gb = jnp.where(lane == LANES - 1, right[0], right[1]).astype(BF)
        return a, b, ga, gb

    def spread(rows):
        for r in rows:
            t = tile(r)
            main, ghost = xm[:, t], xg[:, t]
            a, b, ga, gb = shifts(main, ghost)
            for q, m, g in ((0, a, ga), (1, main, ghost), (2, b, gb)):
                d1m[q * KX : (q + 1) * KX, t] = m[:KX]
                d1g[q * KX : (q + 1) * KX, t] = g[:KX]
                d2m[q * CH : (q + 1) * CH, t] = m[KX:]
                d2g[q * CH : (q + 1) * CH, t] = g[KX:]

    def spread_results(h, g, base):
        for r in range(h[0].shape[1] // LANES):
            t, to = tile(r), tile(base + r)
            for ref, (main, ghost) in ((hd, h), (dad, g)):
                main = main[:, t]
                a, b, _, _ = shifts(main, ghost[:, t])
                ref[0:CH, to] = a
                ref[CH : 2 * CH, to] = main
                ref[2 * CH :, to] = b

    def gated(a, grad, field, t):
        value, slope = gelu_parts(a)
        sea = field[CIN : CIN + 1, t].astype(F32)
        return (value * sea).astype(BF), (grad * (slope * sea)).astype(BF)

    inner = RIM - 2

    def lower(d1, d2, field):
        y = nn(wa1[...], d1[:, tile(0, RIM)])
        v = nn(tb2[...], d2[:, tile(0, RIM)])
        left = tuple(
            u[:CH, tile(inner)] + u[CH : 2 * CH, tile(inner + 1)] for u in (y, v)
        ) + (v[:CH, tile(inner + 1)],)
        h, g = gated(gather_rows(y, inner), gather_rows(v, inner), field, tile(1, inner))
        return h, g, left

    def upper(d1, d2, field, left):
        y = nn(wa1[...], d1[:, tile(RIM)])
        yn = nn(wa1n[...], d1[:, tile(RIM - 1, 3)])
        v = nn(tb2n[...], d2[:, tile(RIM, 2)])
        a = jnp.concatenate([left[0] + y[2 * CH :], gather_rows(yn, 1)], axis=1)
        grad = jnp.concatenate(
            [
                left[1] + v[2 * CH :, tile(0)],
                left[2] + v[CH : 2 * CH, tile(0)] + v[2 * CH :, tile(1)],
            ],
            axis=1,
        )
        return gated(a, grad, field, tile(RIM - 1, 2))

    pick_low = select(64, lambda s: jnp.where(s < 2, s, s + 2), RIM, 0)
    pick_high = select(32, lambda s: s + 2, 2, RIM)

    landed(packs.at[0], 0)
    landed(packs.at[1], 1)

    @pl.when(jnp.logical_not(bottom))
    def _():
        landed(below, 7)
        landed(packs.at[4], 4)
        landed(packs.at[5], 5)

    flat = jnp.concatenate([packs[s] for s in (0, 1, 4, 5)], axis=0)
    xg[:, tile(0, RIM)] = tn(flat, pick_low).astype(BF)
    spread(range(RIM))
    hm, gm, left_m = lower(d1m, d2m, xm)
    hg, gg, left_g = lower(d1g, d2g, xg)
    for dr in range(3):
        am[dr * CH : (dr + 1) * CH, tile(dr, ROWS - 1)] = gm[:, tile(1, ROWS - 1)]
    spread_results((hm, hg), (gm, gg), 0)
    term2 = nt(ae[:, tile(0, inner)], hd[:, tile(0, inner)])
    term1 = nt(am[:, tile(0, inner - 1)], d1m[:, tile(1, inner - 1)])

    @pl.when(jnp.logical_not(top))
    def _():
        landed(above, 8)
        landed(packs.at[2], 2)
        landed(packs.at[3], 3)

    @pl.when(top)
    def _():
        landed(above, 6)

        @pl.when(fold_e != lon)
        def _():
            landed(packs.at[3], 9)

        @pl.when(fold_w != lon)
        def _():
            landed(packs.at[2], 10)

        back = lax.broadcasted_iota(jnp.int32, (LANES, LANES), 0)
        back = back + lax.broadcasted_iota(jnp.int32, (LANES, LANES), 1)
        back = (back == LANES - 1).astype(F32).astype(BF)
        first = nn(xm[:, tile(ROWS + 2)], back).astype(BF)
        second = nn(xm[:, tile(ROWS + 3)], back).astype(BF)
        xm[:, tile(ROWS + 2)] = second
        xm[:, tile(ROWS + 3)] = first

    flat = jnp.concatenate([packs[s] for s in (2, 3)], axis=0)
    xg[:, tile(RIM, 2)] = tn(flat, pick_high).astype(BF)
    spread((RIM, RIM + 1))
    hm, gm = upper(d1m, d2m, xm, left_m)
    hg, gg = upper(d1g, d2g, xg, left_g)
    for dr in range(3):
        am[dr * CH : (dr + 1) * CH, tile(dr + ROWS - 1)] = gm[:, tile(0)]
    spread_results((hm, hg), (gm, gg), inner)
    term2 = term2 + nt(ae[:, tile(inner, 2)], hd[:, tile(inner, 2)])
    term1 = term1 + nt(am[:, tile(inner - 1, 3)], d1m[:, tile(inner, 3)])
    terms = jnp.concatenate([term1, term2], axis=1).astype(BF)
    for t in range(TILES):
        a, b = t // 3, t % 3
        gbuf[t // group, t % group] = terms[16 * a : 16 * a + 16, tile(b)]

    def pass_on(src, dst, sems, p, a, b):
        pltpu.make_async_remote_copy(
            src_ref=src, dst_ref=dst, send_sem=sems[0].at[p], recv_sem=sems[1].at[p],
            device_id=(a, b), device_id_type=MESH,
        ).start()

    def done(ref, count, sem):
        some = ref.at[pl.ds(0, count)]
        pltpu.make_async_copy(some, some, sem).wait()

    def total(ref, p, count):
        acc = ref[p, 0].astype(F32)
        for i in range(1, count):
            acc = acc + ref[p, i].astype(F32)
        return acc.astype(BF)

    def only(test, always, f):
        if always:
            f()
        else:
            pl.when(test)(f)

    parts = -(-TILES // group)
    count = [min(group, TILES - p * group) for p in range(parts)]
    by_z = {j: at_z(j) for j in range(1, z_n)}
    by_y = {j: at_y(j) for j in range(1, y_n)}
    axes = ((z_n, z, by_z.get), (y_n, y, by_y.get))
    first = [axes[p % 2] for p in range(parts)]
    second = [axes[1 - p % 2] for p in range(parts)]

    by_x = {j: at_x(j) for j in range(1, group)}
    for p in range(parts):
        for j in range(1, group):
            to, a, b = by_x[j]
            only(
                to < count[p], count[p] == group,
                functools.partial(pass_on, gbuf.at[p, to], rbuf.at[p, me], sem_rs, p, a, b),
            )

    def hop(p, source, arrived, sem, held_as, axis, sems):
        length, at, peer = axis

        def go():
            done(source.at[p], arrived - 1, sem.at[p])
            held_as[p, at] = total(source, p, arrived)
            for j in far_first(length):
                pass_on(held_as.at[p, at], held_as.at[p, at], sems, p, *peer(j))

        only(me < count[p], count[p] == group, go)

    for p in range(parts):
        def own(p=p):
            rbuf[p, me] = gbuf[p, me]

        only(me < count[p], count[p] == group, own)
        hop(p, rbuf, group, sem_rs[1], ex1, first[p], sem_x1)
    sea = f_ref[CIN : CIN + 1, :].astype(F32)
    res = gather_rows(nn(wa2[...], hd[...]), ROWS) * sea
    for r in range(ROWS):
        flip[pl.ds(r, CH, stride=ROWS), :] = res[:, tile(r)]
    c_in[...] = flip[: CH * ROWS, :].reshape(CH, ROWS, LANES).astype(BF)
    stores = [pltpu.make_async_copy(c_in, out_ref, in_sem.at[0])]
    stores[0].start()

    for p in range(parts):
        hop(p, ex1, first[p][0], sem_x1[1], ex2, second[p], sem_x2)

    v = jnp.concatenate(
        [nn(tb1[...], dad[:, tile(0, RIM - 1)]), nn(tb1n[...], dad[:, tile(RIM - 1)])], axis=1
    )
    res = gather_rows(v, ROWS)
    for r in range(ROWS):
        flip[pl.ds(r, KX, stride=ROWS), :] = res[:, tile(r)]
    x_in[...] = flip[: CIN * ROWS, :].reshape(CIN, ROWS, LANES).astype(BF)
    stores.append(pltpu.make_async_copy(x_in, dx_ref, in_sem.at[1]))
    stores[1].start()

    everyone = (group, me, lambda j: by_x[j][1:])
    for p in range(parts):
        hop(p, ex2, second[p][0], sem_x2[1], obuf, everyone, sem_ag)
    for p in range(parts):
        if count[p] == group:
            done(obuf.at[p], group - 1, sem_ag[1].at[p])
        else:
            pl.when(me < count[p])(
                functools.partial(done, obuf.at[p], count[p] - 1, sem_ag[1].at[p])
            )
            pl.when(me >= count[p])(
                functools.partial(done, obuf.at[p], count[p], sem_ag[1].at[p])
            )
        n = count[p]
        move = pltpu.make_async_copy(obuf.at[p, pl.ds(0, n)], dw_ref.at[p, pl.ds(0, n)], out_sem.at[p])
        move.start()
        stores.append(move)

    def sent(ref, sem):
        pltpu.make_async_copy(ref, ref, sem).wait()

    sent(mine.at[0], send_sem.at[0])
    sent(mine.at[1], send_sem.at[1])

    @pl.when(jnp.logical_not(top))
    def _():
        sent(high, send_sem.at[7])
        sent(mine.at[0], send_sem.at[4])
        sent(mine.at[1], send_sem.at[5])

    @pl.when(top)
    def _():
        sent(high, send_sem.at[6])

        @pl.when(fold_e != lon)
        def _():
            sent(mine.at[0], send_sem.at[9])

        @pl.when(fold_w != lon)
        def _():
            sent(mine.at[1], send_sem.at[10])

    @pl.when(jnp.logical_not(bottom))
    def _():
        sent(low, send_sem.at[8])
        sent(mine.at[0], send_sem.at[2])
        sent(mine.at[1], send_sem.at[3])

    for p in range(parts):
        n = count[p]
        if n == group:
            done(gbuf.at[p], group - 1, sem_rs[0].at[p])
        else:
            pl.when(me < n)(functools.partial(done, gbuf.at[p], n - 1, sem_rs[0].at[p]))
            pl.when(me >= n)(functools.partial(done, gbuf.at[p], n, sem_rs[0].at[p]))

        def drain(p=p):
            done(ex1.at[p], first[p][0] - 1, sem_x1[0].at[p])
            done(ex2.at[p], second[p][0] - 1, sem_x2[0].at[p])
            done(rbuf.at[p], group - 1, sem_ag[0].at[p])

        only(me < n, n == group, drain)
    for store in stores:
        store.wait()


def finish(
    factor, parts, group,
    out_in, dx_in, dw_in, out_ref, dx_ref, dw1_ref, dw2_ref,
    tiles, dw1, dw2, get_sem, put_sem,
):
    get = pltpu.make_async_copy(dw_in, tiles, get_sem)
    puts = [
        pltpu.make_async_copy(src, dst, put_sem.at[i])
        for i, (src, dst) in enumerate(
            ((dw1, dw1_ref), (dw2, dw2_ref), (out_in, out_ref), (dx_in, dx_ref))
        )
    ]
    get.start()
    puts[2].start()
    puts[3].start()
    get.wait()
    for dr in range(3):
        grads = jnp.concatenate(
            [
                jnp.concatenate(
                    [tiles[t // group, t % group] for t in range(3 * a, 3 * a + 3)], axis=1
                )
                for a in range(3 * dr, 3 * dr + 3)
            ],
            axis=0,
        ).astype(F32) * factor
        for dc in range(3):
            dw1[3 * dr + dc] = grads[:, dc * KX : dc * KX + CIN]
            dw2[3 * dr + dc] = grads[:, 3 * KX + dc * CH : 3 * KX + (dc + 1) * CH]
    puts[0].start()
    puts[1].start()
    for put in puts:
        put.wait()


def body(dims, *inputs):
    xl_n, z_n, xh_n, y_n, c_n = dims
    group = xl_n * xh_n * c_n
    parts = -(-TILES // group)
    wide, slim, ring = EXT * LANES, RIM * LANES, max(y_n, z_n)
    anywhere = pl.BlockSpec(memory_space=pl.ANY)
    hbm = pl.BlockSpec(memory_space=pltpu.HBM)

    def held(*shape):
        return pltpu.VMEM(shape, BF)

    fields_like = (
        jax.ShapeDtypeStruct((CH, ROWS, LANES), BF),
        jax.ShapeDtypeStruct((CIN, ROWS, LANES), BF),
    )
    out, dx, dw = pl.pallas_call(
        functools.partial(kernel, dims),
        out_shape=fields_like + (jax.ShapeDtypeStruct((parts, group, 16, LANES), BF),),
        in_specs=[hbm] * 5,
        out_specs=(anywhere,) * 3,
        scratch_shapes=[
            held(CIN, ROWS, LANES), pltpu.VMEM((ROWS, LANES), jnp.int32),
            held(9, CH, CIN), held(9, CH, CH), held(CH, ROWS, LANES),
            pltpu.VMEM(((KX + CH) * ROWS, LANES), F32), held(KX + CH, ROWS * LANES),
            held(3 * CH, 3 * KX), held(3 * CH, 3 * KX), held(3 * CH, 3 * CH),
            held(3 * CH, 3 * CH), held(3 * CH, 3 * CH), held(3 * KX, 3 * CH), held(3 * KX, 3 * CH),
            held(128, wide), held(128, wide), held(6, 16, 128), held(2, 16, 128),
            held(3 * KX, wide), held(3 * KX, wide), held(3 * CH, wide), held(3 * CH, wide),
            held(3 * CH, slim), held(3 * CH, slim), held(3 * CH, slim), held(3 * CH, slim),
            held(parts, group, 16, LANES), held(parts, group, 16, LANES),
            held(parts, ring, 16, LANES), held(parts, ring, 16, LANES),
            held(parts, group, 16, LANES),
            pltpu.SemaphoreType.DMA((5,)), pltpu.SemaphoreType.DMA((parts,)),
            pltpu.SemaphoreType.DMA((11,)), pltpu.SemaphoreType.DMA((11,)),
        ] + [pltpu.SemaphoreType.DMA((parts,))] * 8,
        compiler_params=pltpu.CompilerParams(
            collective_id=0, has_side_effects=True, vmem_limit_bytes=24 * 1024 * 1024
        ),
    )(*(pltpu.with_memory_space_constraint(v, pltpu.HBM) for v in inputs))
    factor = 1.0 / math.sqrt(ROWS * LANES * xl_n * z_n * xh_n * y_n * c_n)
    return pl.pallas_call(
        functools.partial(finish, factor, parts, group),
        out_shape=fields_like + (
            jax.ShapeDtypeStruct((9, CH, CIN), F32),
            jax.ShapeDtypeStruct((9, CH, CH), F32),
        ),
        in_specs=[anywhere] * 3,
        out_specs=(hbm,) * 4,
        scratch_shapes=[
            held(parts, group, 16, LANES),
            pltpu.VMEM((9, CH, CIN), F32), pltpu.VMEM((9, CH, CH), F32),
            pltpu.SemaphoreType.DMA, pltpu.SemaphoreType.DMA((4,)),
        ],
        compiler_params=pltpu.CompilerParams(vmem_limit_bytes=8 * 1024 * 1024),
    )(out, dx, dw)


def solution(mesh):
    in_specs = (P(None, "lat", "lon"), P("lat", "lon"), P(), P(), P(None, "lat", "lon"))
    out_specs = (P(None, "lat", "lon"), P(None, "lat", "lon"), P(), P())
    nlat, nlon = mesh.shape["lat"], mesh.shape["lon"]
    x_hi = 2 if nlon > 4 else 1
    dims = (2, nlat // 2, x_hi, nlon // (2 * x_hi), 2)
    run = functools.partial(body, dims)
    return jax.shard_map(run, mesh=mesh, in_specs=in_specs, out_specs=out_specs, check_vma=False)
```

```python
import functools
import math

import jax
import jax.numpy as jnp
from jax import lax
from jax.experimental import pallas as pl
from jax.experimental.pallas import tpu as pltpu
from jax.sharding import PartitionSpec as P

MESH = pl.DeviceIdType.MESH
BF = jnp.bfloat16
F32 = jnp.float32
CIN, CH, KX = 75, 48, 80
ROWS, LANES = 8, 128
EXT = ROWS + 4
RIM = ROWS + 2
TILES = 27
UNIT = 2
CHUNKS = -(-TILES // UNIT)
TALL = 16 * UNIT


def nn(a, b):
    return lax.dot_general(a, b, (((1,), (0,)), ((), ())), preferred_element_type=F32)


def nt(a, b):
    return lax.dot_general(a, b, (((1,), (1,)), ((), ())), preferred_element_type=F32)


def tn(a, b):
    return lax.dot_general(a, b, (((0,), (0,)), ((), ())), preferred_element_type=F32)


def gelu_parts(a):
    coeff = 0.7978845608
    inner = coeff * (a + 0.044715 * a * a * a)
    tval = jnp.tanh(inner)
    value = 0.5 * a * (1.0 + tval)
    slope = 0.5 * (1.0 + tval) + 0.5 * a * (1.0 - tval * tval) * coeff * (1.0 + 0.134145 * a * a)
    return (value, slope)


def tile(r, count=1):
    return slice(r * LANES, (r + count) * LANES)


def gather_rows(y, rows):
    n = rows * LANES
    c = y.shape[0] // 3
    return y[:c, :n] + y[c : 2 * c, LANES : LANES + n] + y[2 * c :, 2 * LANES : 2 * LANES + n]


def chunk_of(t, group):
    c, row = t // UNIT, t % UNIT * 16
    return c // group, c % group, slice(row, row + 16)


def far_first(n):
    return sorted(range(1, n), key=lambda j: -min(j, n - j))


def kernel(
    dims,
    x_hbm, m_hbm, w1_hbm, w2_hbm, c_hbm,
    out_ref, dx_ref, dw1_ref, dw2_ref,
    x_in, m_in, w1_in, w2_in, c_in, flip, f_ref,
    wa1, wa1n, wa2, tb2, tb2n, tb1, tb1n,
    xm, xg, packs, mine, d1m, d1g, d2m, d2g, hd, dad, am, ae,
    gbuf, rbuf, ex1, ex2, obuf, dw1, dw2,
    in_sem, out_sem, send_sem, recv_sem, *red,
):
    sem_rs, sem_x1, sem_x2, sem_ag = red[0:2], red[2:4], red[4:6], red[6:8]
    xl_n, z_n, xh_n, y_n, c_n = dims
    nlat, nlon, group = xl_n * z_n, xh_n * y_n * c_n, xl_n * xh_n * c_n
    lat, lon = lax.axis_index("lat"), lax.axis_index("lon")
    xl, z = lat // z_n, lat % z_n
    xh, y, core = lon // (y_n * c_n), (lon // c_n) % y_n, lon % c_n
    me = (xl * xh_n + xh) * c_n + core
    top, bottom = lat == nlat - 1, lat == 0
    east, west = lax.rem(lon + 1, nlon), lax.rem(lon + nlon - 1, nlon)
    mirror = nlon - 1 - lon
    fold_e = lax.rem(2 * nlon - 2 - lon, nlon)
    fold_w = lax.rem(nlon - lon, nlon)

    def at_z(j):
        to = lax.rem(z + j, z_n)
        return xl * z_n + to, lon

    def at_y(j):
        to = lax.rem(y + j, y_n)
        return lat, (xh * y_n + to) * c_n + core

    def at_x(d):
        a, b, c = lax.rem(xl + d[0], xl_n), lax.rem(xh + d[1], xh_n), lax.rem(core + d[2], c_n)
        return (a * xh_n + b) * c_n + c, a * z_n + z, (b * y_n + y) * c_n + c

    others = [
        (a, b, c) for a in range(xl_n) for b in range(xh_n) for c in range(c_n) if a or b or c
    ]
    others.sort(key=lambda d: 0 if d[1] and not d[0] else 1 if d[0] else 2)

    loads = [
        pltpu.make_async_copy(src, dst, in_sem.at[i])
        for i, (src, dst) in enumerate(
            ((x_hbm, x_in), (m_hbm, m_in), (c_hbm, c_in), (w1_hbm, w1_in), (w2_hbm, w2_in))
        )
    ]
    for load in loads:
        load.start()

    barrier = pltpu.get_barrier_semaphore()

    def greet(a, b):
        pl.semaphore_signal(barrier, inc=1, device_id=(a, b), device_id_type=MESH)

    @pl.when(top)
    def _():
        greet(lat, mirror)

        @pl.when(fold_e != lon)
        def _():
            greet(lat, fold_e)

        @pl.when(fold_w != lon)
        def _():
            greet(lat, fold_w)

    for j in far_first(y_n):
        greet(*at_y(j))
    for j in far_first(z_n):
        greet(*at_z(j))
    for d in others:
        greet(*at_x(d)[1:])

    @pl.when(jnp.logical_not(top))
    def _():
        greet(lat + 1, east)
        greet(lat + 1, west)
        greet(lat + 1, lon)

    @pl.when(jnp.logical_not(bottom))
    def _():
        greet(lat - 1, east)
        greet(lat - 1, west)
        greet(lat - 1, lon)

    greet(lat, east)
    greet(lat, west)

    for load in loads[:3]:
        load.wait()
    sea8 = m_in[...].astype(F32)
    flip[: CIN * ROWS, :] = x_in[...].astype(F32).reshape(CIN * ROWS, LANES)
    flip[CIN * ROWS : (CIN + 1) * ROWS, :] = sea8
    flip[(CIN + 1) * ROWS : KX * ROWS, :] = jnp.zeros(((KX - CIN - 1) * ROWS, LANES), F32)
    flip[KX * ROWS :, :] = (c_in[...].astype(F32) * sea8[None]).reshape(CH * ROWS, LANES)
    for r in range(ROWS):
        f_ref[:, tile(r)] = flip[pl.ds(r, KX + CH, stride=ROWS), :].astype(BF)

    cell = lax.broadcasted_iota(jnp.int32, (32, ROWS * LANES), 0)
    place = lax.broadcasted_iota(jnp.int32, (32, ROWS * LANES), 1)
    want = ((cell % 16) // 2) * LANES + cell % 2 + jnp.where(cell < 16, LANES - 2, 0)
    picked = nt((place == want).astype(F32).astype(BF), f_ref[...]).astype(BF)
    mine[0] = picked[:16]
    mine[1] = picked[16:]

    folds = 1 + jnp.where(fold_e != lon, 1, 0) + jnp.where(fold_w != lon, 1, 0)
    pl.semaphore_wait(
        barrier,
        y_n + z_n + group - 3 + 2 + jnp.where(top, folds, 3) + jnp.where(bottom, 0, 3),
    )

    def send(src, dst, slot, a, b):
        return pltpu.make_async_remote_copy(
            src_ref=src, dst_ref=dst, send_sem=send_sem.at[slot], recv_sem=recv_sem.at[slot],
            device_id=(a, b), device_id_type=MESH,
        )

    low, high = f_ref.at[:, tile(0, 2)], f_ref.at[:, tile(ROWS - 2, 2)]
    above, below = xm.at[:, tile(ROWS + 2, 2)], xm.at[:, tile(0, 2)]

    @pl.when(top)
    def _():
        @pl.when(fold_e != lon)
        def _():
            send(mine.at[0], packs.at[3], 9, lat, fold_e).start()

        @pl.when(fold_w != lon)
        def _():
            send(mine.at[1], packs.at[2], 10, lat, fold_w).start()

        @pl.when(fold_e == lon)
        def _():
            packs[3] = mine[0]

        @pl.when(fold_w == lon)
        def _():
            packs[2] = mine[1]

    @pl.when(jnp.logical_not(bottom))
    def _():
        send(mine.at[0], packs.at[2], 2, lat - 1, east).start()
        send(mine.at[1], packs.at[3], 3, lat - 1, west).start()

    @pl.when(jnp.logical_not(top))
    def _():
        send(mine.at[0], packs.at[4], 4, lat + 1, east).start()
        send(mine.at[1], packs.at[5], 5, lat + 1, west).start()

    send(mine.at[0], packs.at[0], 0, lat, east).start()
    send(mine.at[1], packs.at[1], 1, lat, west).start()

    @pl.when(jnp.logical_not(top))
    def _():
        send(high, below, 7, lat + 1, lon).start()

    @pl.when(jnp.logical_not(bottom))
    def _():
        send(low, above, 8, lat - 1, lon).start()

    @pl.when(top)
    def _():
        send(high, above, 6, lat, mirror).start()

    @pl.when(bottom)
    def _():
        xm[:, tile(0, 2)] = jnp.zeros((128, 2 * LANES), BF)
        packs[4] = jnp.zeros((16, 128), BF)
        packs[5] = jnp.zeros((16, 128), BF)

    xm[:, tile(2, ROWS)] = f_ref[...]
    zero = jnp.zeros((CH, LANES), BF)
    for dr in range(3):
        at = slice(dr * CH, (dr + 1) * CH)
        ae[at, tile(dr, ROWS)] = f_ref[KX:, :]
        for r in range(RIM):
            if not dr <= r < dr + ROWS:
                am[at, tile(r)] = zero
                ae[at, tile(r)] = zero

    def select(cells, slot, tiles, base):
        k = lax.broadcasted_iota(jnp.int32, (cells, 1), 0)
        slot, row, j = slot(k // 16), (k % 16) // 2, k % 2
        row_to = jnp.where(slot < 2, row + 2, jnp.where(slot < 4, row + 10, row - 6))
        row_to = jnp.where((slot >= 2) & (slot < 4) & top, 17 - row, row_to)
        lane_to = jnp.where(slot % 2 == 0, LANES - 2 + j, j)
        lane_to = jnp.where((slot == 2) & top, LANES - 1 - j, lane_to)
        lane_to = jnp.where((slot == 3) & top, 1 - j, lane_to)
        good = (slot < 2) | ((slot < 4) & (row_to < EXT)) | ((slot >= 4) & (row_to >= 0))
        goal = jnp.where(good, (row_to - base) * LANES + lane_to, -1)
        place = lax.broadcasted_iota(jnp.int32, (cells, tiles * LANES), 1)
        return (place == goal).astype(F32).astype(BF)

    loads[3].wait()
    loads[4].wait()
    gap = jnp.zeros((CH, KX - CIN), F32)
    k1 = [jnp.concatenate([w1_in[t].astype(F32), gap], axis=1) for t in range(9)]
    k2 = [w2_in[t].astype(F32) for t in range(9)]

    def square(k, pick):
        return jnp.concatenate(
            [jnp.concatenate([k[pick(a, b)] for b in range(3)], axis=1) for a in range(3)], axis=0
        )

    def plain(a, b):
        return 3 * a + b

    def turned(a, b):
        return 8 - 3 * a - b

    def swapped(a, b):
        return 3 * b + a

    def both(a, b):
        return 8 - 3 * b - a

    m = square(k1, plain)
    wa1[...] = m.astype(BF)
    wa1n[...] = jnp.where(top, square(k1, turned), m).astype(BF)
    wa2[...] = square(k2, plain).astype(BF)
    m = square(k2, both)
    tb2[...] = m.T.astype(BF)
    tb2n[...] = jnp.where(top, square(k2, swapped), m).T.astype(BF)
    m = square(k1, both)
    tb1[...] = m.T.astype(BF)
    tb1n[...] = jnp.where(top, square(k1, swapped), m).T.astype(BF)

    def landed(ref, slot):
        pltpu.make_async_copy(ref, ref, recv_sem.at[slot]).wait()

    lane = lax.broadcasted_iota(jnp.int32, (1, LANES), 1)

    def shifts(main, ghost):
        main, ghost = main.astype(F32), ghost.astype(F32)
        left = (pltpu.roll(main, 1, 1), pltpu.roll(ghost, 1, 1))
        right = (pltpu.roll(main, LANES - 1, 1), pltpu.roll(ghost, LANES - 1, 1))
        a = jnp.where(lane == 0, left[1], left[0]).astype(BF)
        b = jnp.where(lane == LANES - 1, right[1], right[0]).astype(BF)
        ga = jnp.where(lane == 0, left[0], left[1]).astype(BF)
        gb = jnp.where(lane == LANES - 1, right[0], right[1]).astype(BF)
        return a, b, ga, gb

    def spread(rows):
        for r in rows:
            t = tile(r)
            main, ghost = xm[:, t], xg[:, t]
            a, b, ga, gb = shifts(main, ghost)
            for q, m, g in ((0, a, ga), (1, main, ghost), (2, b, gb)):
                d1m[q * KX : (q + 1) * KX, t] = m[:KX]
                d1g[q * KX : (q + 1) * KX, t] = g[:KX]
                d2m[q * CH : (q + 1) * CH, t] = m[KX:]
                d2g[q * CH : (q + 1) * CH, t] = g[KX:]

    def spread_results(h, g, base):
        for r in range(h[0].shape[1] // LANES):
            t, to = tile(r), tile(base + r)
            for ref, (main, ghost) in ((hd, h), (dad, g)):
                main = main[:, t]
                a, b, _, _ = shifts(main, ghost[:, t])
                ref[0:CH, to] = a
                ref[CH : 2 * CH, to] = main
                ref[2 * CH :, to] = b

    def gated(a, grad, field, t):
        value, slope = gelu_parts(a)
        sea = field[CIN : CIN + 1, t].astype(F32)
        return (value * sea).astype(BF), (grad * (slope * sea)).astype(BF)

    inner = RIM - 2

    def lower(d1, d2, field):
        y = nn(wa1[...], d1[:, tile(0, RIM)])
        v = nn(tb2[...], d2[:, tile(0, RIM)])
        left = tuple(
            u[:CH, tile(inner)] + u[CH : 2 * CH, tile(inner + 1)] for u in (y, v)
        ) + (v[:CH, tile(inner + 1)],)
        h, g = gated(gather_rows(y, inner), gather_rows(v, inner), field, tile(1, inner))
        return h, g, left

    def upper(d1, d2, field, left):
        y = nn(wa1[...], d1[:, tile(RIM)])
        yn = nn(wa1n[...], d1[:, tile(RIM - 1, 3)])
        v = nn(tb2n[...], d2[:, tile(RIM, 2)])
        a = jnp.concatenate([left[0] + y[2 * CH :], gather_rows(yn, 1)], axis=1)
        grad = jnp.concatenate(
            [
                left[1] + v[2 * CH :, tile(0)],
                left[2] + v[CH : 2 * CH, tile(0)] + v[2 * CH :, tile(1)],
            ],
            axis=1,
        )
        return gated(a, grad, field, tile(RIM - 1, 2))

    pick_low = select(64, lambda s: jnp.where(s < 2, s, s + 2), RIM, 0)
    pick_high = select(32, lambda s: s + 2, 2, RIM)

    landed(packs.at[0], 0)
    landed(packs.at[1], 1)

    @pl.when(jnp.logical_not(bottom))
    def _():
        landed(below, 7)
        landed(packs.at[4], 4)
        landed(packs.at[5], 5)

    flat = jnp.concatenate([packs[s] for s in (0, 1, 4, 5)], axis=0)
    xg[:, tile(0, RIM)] = tn(flat, pick_low).astype(BF)
    spread(range(RIM))
    hm, gm, left_m = lower(d1m, d2m, xm)
    hg, gg, left_g = lower(d1g, d2g, xg)
    for dr in range(3):
        am[dr * CH : (dr + 1) * CH, tile(dr, ROWS - 1)] = gm[:, tile(1, ROWS - 1)]
    spread_results((hm, hg), (gm, gg), 0)
    term2 = nt(ae[:, tile(0, inner)], hd[:, tile(0, inner)])
    term1 = nt(am[:, tile(0, inner - 1)], d1m[:, tile(1, inner - 1)])

    @pl.when(jnp.logical_not(top))
    def _():
        landed(above, 8)
        landed(packs.at[2], 2)
        landed(packs.at[3], 3)

    @pl.when(top)
    def _():
        landed(above, 6)

        @pl.when(fold_e != lon)
        def _():
            landed(packs.at[3], 9)

        @pl.when(fold_w != lon)
        def _():
            landed(packs.at[2], 10)

        back = lax.broadcasted_iota(jnp.int32, (LANES, LANES), 0)
        back = back + lax.broadcasted_iota(jnp.int32, (LANES, LANES), 1)
        back = (back == LANES - 1).astype(F32).astype(BF)
        first = nn(xm[:, tile(ROWS + 2)], back).astype(BF)
        second = nn(xm[:, tile(ROWS + 3)], back).astype(BF)
        xm[:, tile(ROWS + 2)] = second
        xm[:, tile(ROWS + 3)] = first

    flat = jnp.concatenate([packs[s] for s in (2, 3)], axis=0)
    xg[:, tile(RIM, 2)] = tn(flat, pick_high).astype(BF)
    spread((RIM, RIM + 1))
    hm, gm = upper(d1m, d2m, xm, left_m)
    hg, gg = upper(d1g, d2g, xg, left_g)
    for dr in range(3):
        am[dr * CH : (dr + 1) * CH, tile(dr + ROWS - 1)] = gm[:, tile(0)]
    spread_results((hm, hg), (gm, gg), inner)
    term2 = term2 + nt(ae[:, tile(inner, 2)], hd[:, tile(inner, 2)])
    term1 = term1 + nt(am[:, tile(inner - 1, 3)], d1m[:, tile(inner, 3)])
    terms = jnp.concatenate([term1, term2], axis=1).astype(BF)
    for t in range(TILES):
        a, b = t // 3, t % 3
        gbuf[chunk_of(t, group)] = terms[16 * a : 16 * a + 16, tile(b)]
    for t in range(TILES, CHUNKS * UNIT):
        gbuf[chunk_of(t, group)] = jnp.zeros((16, LANES), BF)

    def pass_on(src, dst, sems, p, a, b):
        pltpu.make_async_remote_copy(
            src_ref=src, dst_ref=dst, send_sem=sems[0].at[p], recv_sem=sems[1].at[p],
            device_id=(a, b), device_id_type=MESH,
        ).start()

    def done(ref, count, sem):
        some = ref.at[pl.ds(0, count)]
        pltpu.make_async_copy(some, some, sem).wait()

    def total(ref, p, count):
        acc = ref[p, 0].astype(F32)
        for i in range(1, count):
            acc = acc + ref[p, i].astype(F32)
        return acc.astype(BF)

    def only(test, always, f):
        if always:
            f()
        else:
            pl.when(test)(f)

    parts = -(-CHUNKS // group)
    count = [min(group, CHUNKS - p * group) for p in range(parts)]
    by_z = {j: at_z(j) for j in range(1, z_n)}
    by_y = {j: at_y(j) for j in range(1, y_n)}
    axes = ((z_n, z, far_first(z_n), by_z.get), (y_n, y, far_first(y_n), by_y.get))
    first = [axes[p % 2] for p in range(parts)]
    second = [axes[1 - p % 2] for p in range(parts)]

    by_x = {d: at_x(d) for d in others}
    for p in range(parts):
        for d in others:
            to, a, b = by_x[d]
            only(
                to < count[p], count[p] == group,
                functools.partial(pass_on, gbuf.at[p, to], rbuf.at[p, me], sem_rs, p, a, b),
            )

    def hop(p, source, arrived, sem, held_as, axis, sems):
        _, at, order, peer = axis

        def go():
            done(source.at[p], arrived - 1, sem.at[p])
            held_as[p, at] = total(source, p, arrived)
            for j in order:
                pass_on(held_as.at[p, at], held_as.at[p, at], sems, p, *peer(j))

        only(me < count[p], count[p] == group, go)

    for p in range(parts):
        def own(p=p):
            rbuf[p, me] = gbuf[p, me]

        only(me < count[p], count[p] == group, own)
        hop(p, rbuf, group, sem_rs[1], ex1, first[p], sem_x1)
    sea = f_ref[CIN : CIN + 1, :].astype(F32)
    res = gather_rows(nn(wa2[...], hd[...]), ROWS) * sea
    for r in range(ROWS):
        flip[pl.ds(r, CH, stride=ROWS), :] = res[:, tile(r)]
    c_in[...] = flip[: CH * ROWS, :].reshape(CH, ROWS, LANES).astype(BF)
    stores = [pltpu.make_async_copy(c_in, out_ref, in_sem.at[0])]
    stores[0].start()

    for p in range(parts):
        hop(p, ex1, first[p][0], sem_x1[1], ex2, second[p], sem_x2)

    v = jnp.concatenate(
        [nn(tb1[...], dad[:, tile(0, RIM - 1)]), nn(tb1n[...], dad[:, tile(RIM - 1)])], axis=1
    )
    res = gather_rows(v, ROWS)
    for r in range(ROWS):
        flip[pl.ds(r, KX, stride=ROWS), :] = res[:, tile(r)]
    x_in[...] = flip[: CIN * ROWS, :].reshape(CIN, ROWS, LANES).astype(BF)
    stores.append(pltpu.make_async_copy(x_in, dx_ref, in_sem.at[1]))
    stores[1].start()

    everyone = (group, me, others, lambda d: by_x[d][1:])
    for p in range(parts):
        hop(p, ex2, second[p][0], sem_x2[1], obuf, everyone, sem_ag)
    for p in range(parts):
        if count[p] == group:
            done(obuf.at[p], group - 1, sem_ag[1].at[p])
        else:
            pl.when(me < count[p])(
                functools.partial(done, obuf.at[p], count[p] - 1, sem_ag[1].at[p])
            )
            pl.when(me >= count[p])(
                functools.partial(done, obuf.at[p], count[p], sem_ag[1].at[p])
            )

    for dr in range(3):
        grads = jnp.concatenate(
            [
                jnp.concatenate(
                    [obuf[chunk_of(t, group)] for t in range(3 * a, 3 * a + 3)], axis=1
                )
                for a in range(3 * dr, 3 * dr + 3)
            ],
            axis=0,
        ).astype(F32) * (1.0 / math.sqrt(ROWS * LANES * nlat * nlon))
        for dc in range(3):
            dw1[3 * dr + dc] = grads[:, dc * KX : dc * KX + CIN]
            dw2[3 * dr + dc] = grads[:, 3 * KX + dc * CH : 3 * KX + (dc + 1) * CH]
    for i, (src, dst) in enumerate(((dw1, dw1_ref), (dw2, dw2_ref))):
        stores.append(pltpu.make_async_copy(src, dst, out_sem.at[i]))
        stores[-1].start()

    def sent(ref, sem):
        pltpu.make_async_copy(ref, ref, sem).wait()

    sent(mine.at[0], send_sem.at[0])
    sent(mine.at[1], send_sem.at[1])

    @pl.when(jnp.logical_not(top))
    def _():
        sent(high, send_sem.at[7])
        sent(mine.at[0], send_sem.at[4])
        sent(mine.at[1], send_sem.at[5])

    @pl.when(top)
    def _():
        sent(high, send_sem.at[6])

        @pl.when(fold_e != lon)
        def _():
            sent(mine.at[0], send_sem.at[9])

        @pl.when(fold_w != lon)
        def _():
            sent(mine.at[1], send_sem.at[10])

    @pl.when(jnp.logical_not(bottom))
    def _():
        sent(low, send_sem.at[8])
        sent(mine.at[0], send_sem.at[2])
        sent(mine.at[1], send_sem.at[3])

    for p in range(parts):
        n = count[p]
        if n == group:
            done(gbuf.at[p], group - 1, sem_rs[0].at[p])
        else:
            pl.when(me < n)(functools.partial(done, gbuf.at[p], n - 1, sem_rs[0].at[p]))
            pl.when(me >= n)(functools.partial(done, gbuf.at[p], n, sem_rs[0].at[p]))

        def drain(p=p):
            done(ex1.at[p], first[p][0] - 1, sem_x1[0].at[p])
            done(ex2.at[p], second[p][0] - 1, sem_x2[0].at[p])
            done(rbuf.at[p], group - 1, sem_ag[0].at[p])

        only(me < n, n == group, drain)
    for store in stores:
        store.wait()


def finish(*refs):
    moves = [
        pltpu.make_async_copy(src, dst, refs[8].at[i])
        for i, (src, dst) in enumerate(zip(refs[:4], refs[4:8]))
    ]
    for move in moves:
        move.start()
    for move in moves:
        move.wait()


def body(dims, *inputs):
    xl_n, z_n, xh_n, y_n, c_n = dims
    group = xl_n * xh_n * c_n
    parts = -(-CHUNKS // group)
    wide, slim, ring = EXT * LANES, RIM * LANES, max(y_n, z_n)
    anywhere = pl.BlockSpec(memory_space=pl.ANY)
    hbm = pl.BlockSpec(memory_space=pltpu.HBM)

    def held(*shape):
        return pltpu.VMEM(shape, BF)

    results = (
        jax.ShapeDtypeStruct((CH, ROWS, LANES), BF),
        jax.ShapeDtypeStruct((CIN, ROWS, LANES), BF),
        jax.ShapeDtypeStruct((9, CH, CIN), F32),
        jax.ShapeDtypeStruct((9, CH, CH), F32),
    )
    held_results = pl.pallas_call(
        functools.partial(kernel, dims),
        out_shape=results,
        in_specs=[hbm] * 5,
        out_specs=(anywhere,) * 4,
        scratch_shapes=[
            held(CIN, ROWS, LANES), pltpu.VMEM((ROWS, LANES), jnp.int32),
            held(9, CH, CIN), held(9, CH, CH), held(CH, ROWS, LANES),
            pltpu.VMEM(((KX + CH) * ROWS, LANES), F32), held(KX + CH, ROWS * LANES),
            held(3 * CH, 3 * KX), held(3 * CH, 3 * KX), held(3 * CH, 3 * CH),
            held(3 * CH, 3 * CH), held(3 * CH, 3 * CH), held(3 * KX, 3 * CH), held(3 * KX, 3 * CH),
            held(128, wide), held(128, wide), held(6, 16, 128), held(2, 16, 128),
            held(3 * KX, wide), held(3 * KX, wide), held(3 * CH, wide), held(3 * CH, wide),
            held(3 * CH, slim), held(3 * CH, slim), held(3 * CH, slim), held(3 * CH, slim),
            held(parts, group, TALL, LANES), held(parts, group, TALL, LANES),
            held(parts, ring, TALL, LANES), held(parts, ring, TALL, LANES),
            held(parts, group, TALL, LANES),
            pltpu.VMEM((9, CH, CIN), F32), pltpu.VMEM((9, CH, CH), F32),
            pltpu.SemaphoreType.DMA((5,)), pltpu.SemaphoreType.DMA((2,)),
            pltpu.SemaphoreType.DMA((11,)), pltpu.SemaphoreType.DMA((11,)),
        ] + [pltpu.SemaphoreType.DMA((parts,))] * 8,
        compiler_params=pltpu.CompilerParams(
            collective_id=0, has_side_effects=True, vmem_limit_bytes=24 * 1024 * 1024
        ),
    )(*(pltpu.with_memory_space_constraint(v, pltpu.HBM) for v in inputs))
    return pl.pallas_call(
        finish,
        out_shape=results,
        in_specs=[anywhere] * 4,
        out_specs=(hbm,) * 4,
        scratch_shapes=[pltpu.SemaphoreType.DMA((4,))],
        compiler_params=pltpu.CompilerParams(vmem_limit_bytes=8 * 1024 * 1024),
    )(*held_results)


def solution(mesh):
    in_specs = (P(None, "lat", "lon"), P("lat", "lon"), P(), P(), P(None, "lat", "lon"))
    out_specs = (P(None, "lat", "lon"), P(None, "lat", "lon"), P(), P())
    nlat, nlon = mesh.shape["lat"], mesh.shape["lon"]
    x_hi = 2 if nlon > 4 else 1
    dims = (2, nlat // 2, x_hi, nlon // (2 * x_hi), 2)
    run = functools.partial(body, dims)
    return jax.shard_map(run, mesh=mesh, in_specs=in_specs, out_specs=out_specs, check_vma=False)
```

```python
import functools
import math

import jax
import jax.numpy as jnp
from jax import lax
from jax.experimental import pallas as pl
from jax.experimental.pallas import tpu as pltpu
from jax.sharding import PartitionSpec as P

MESH = pl.DeviceIdType.MESH
BF = jnp.bfloat16
F32 = jnp.float32
CIN, CH, KX = 75, 48, 80
ROWS, LANES = 8, 128
EXT = ROWS + 4
RIM = ROWS + 2
TILES = 27
UNIT = 2
CHUNKS = -(-TILES // UNIT)
TALL = 16 * UNIT


def nn(a, b):
    return lax.dot_general(a, b, (((1,), (0,)), ((), ())), preferred_element_type=F32)


def nt(a, b):
    return lax.dot_general(a, b, (((1,), (1,)), ((), ())), preferred_element_type=F32)


def tn(a, b):
    return lax.dot_general(a, b, (((0,), (0,)), ((), ())), preferred_element_type=F32)


def gelu_parts(a):
    coeff = 0.7978845608
    inner = coeff * (a + 0.044715 * a * a * a)
    tval = jnp.tanh(inner)
    value = 0.5 * a * (1.0 + tval)
    slope = 0.5 * (1.0 + tval) + 0.5 * a * (1.0 - tval * tval) * coeff * (1.0 + 0.134145 * a * a)
    return (value, slope)


def tile(r, count=1):
    return slice(r * LANES, (r + count) * LANES)


def gather_rows(y, rows):
    n = rows * LANES
    c = y.shape[0] // 3
    return y[:c, :n] + y[c : 2 * c, LANES : LANES + n] + y[2 * c :, 2 * LANES : 2 * LANES + n]


def chunk_of(t, group):
    c, row = t // UNIT, t % UNIT * 16
    return c // group, c % group, slice(row, row + 16)


def far_first(n):
    return sorted(range(1, n), key=lambda j: -min(j, n - j))


def kernel(
    dims,
    x_hbm, m_hbm, w1_hbm, w2_hbm, c_hbm,
    out_ref, dx_ref, dw_ref,
    x_in, m_in, w1_in, w2_in, c_in, flip, f_ref,
    wa1, wa1n, wa2, tb2, tb2n, tb1, tb1n,
    xm, xg, xo, packs, mine, d1m, d1g, d2m, d2g, hd, dad, am, ae,
    gbuf, rbuf, ex1, ex2, obuf,
    in_sem, out_sem, send_sem, recv_sem, *red,
):
    sem_rs, sem_x1, sem_x2, sem_ag = red[0:2], red[2:4], red[4:6], red[6:8]
    xl_n, z_n, xh_n, y_n, c_n = dims
    nlat, nlon, group = xl_n * z_n, xh_n * y_n * c_n, xl_n * xh_n * c_n
    lat, lon = lax.axis_index("lat"), lax.axis_index("lon")
    xl, z = lat // z_n, lat % z_n
    xh, y, core = lon // (y_n * c_n), (lon // c_n) % y_n, lon % c_n
    me = (xl * xh_n + xh) * c_n + core
    top, bottom = lat == nlat - 1, lat == 0
    east, west = lax.rem(lon + 1, nlon), lax.rem(lon + nlon - 1, nlon)
    mirror = nlon - 1 - lon
    fold_e = lax.rem(2 * nlon - 2 - lon, nlon)
    fold_w = lax.rem(nlon - lon, nlon)

    def at_z(j):
        to = lax.rem(z + j, z_n)
        return xl * z_n + to, lon

    def at_y(j):
        to = lax.rem(y + j, y_n)
        return lat, (xh * y_n + to) * c_n + core

    def at_x(j):
        to = lax.rem(me + j, group)
        a, b, c = to // (xh_n * c_n), (to // c_n) % xh_n, to % c_n
        return to, a * z_n + z, (b * y_n + y) * c_n + c

    loads = [
        pltpu.make_async_copy(src, dst, in_sem.at[i])
        for i, (src, dst) in enumerate(
            ((x_hbm, x_in), (m_hbm, m_in), (c_hbm, c_in), (w1_hbm, w1_in), (w2_hbm, w2_in))
        )
    ]
    for load in loads:
        load.start()

    barrier = pltpu.get_barrier_semaphore()

    def greet(a, b):
        pl.semaphore_signal(barrier, inc=1, device_id=(a, b), device_id_type=MESH)

    @pl.when(top)
    def _():
        greet(lat, mirror)

        @pl.when(fold_e != lon)
        def _():
            greet(lat, fold_e)

        @pl.when(fold_w != lon)
        def _():
            greet(lat, fold_w)

    @pl.when(jnp.logical_not(top))
    def _():
        greet(lat + 1, east)
        greet(lat + 1, west)
        greet(lat + 1, lon)

    @pl.when(jnp.logical_not(bottom))
    def _():
        greet(lat - 1, east)
        greet(lat - 1, west)
        greet(lat - 1, lon)

    greet(lat, east)
    greet(lat, west)

    for j in far_first(y_n):
        greet(*at_y(j))
    for j in far_first(z_n):
        greet(*at_z(j))
    for j in range(1, group):
        greet(*at_x(j)[1:])

    for load in loads[:3]:
        load.wait()
    sea8 = m_in[...].astype(F32)
    flip[: CIN * ROWS, :] = x_in[...].astype(F32).reshape(CIN * ROWS, LANES)
    flip[CIN * ROWS : (CIN + 1) * ROWS, :] = sea8
    flip[(CIN + 1) * ROWS : KX * ROWS, :] = jnp.zeros(((KX - CIN - 1) * ROWS, LANES), F32)
    flip[KX * ROWS :, :] = (c_in[...].astype(F32) * sea8[None]).reshape(CH * ROWS, LANES)
    for r in range(ROWS):
        f_ref[:, tile(r)] = flip[pl.ds(r, KX + CH, stride=ROWS), :].astype(BF)

    cell = lax.broadcasted_iota(jnp.int32, (32, ROWS * LANES), 0)
    place = lax.broadcasted_iota(jnp.int32, (32, ROWS * LANES), 1)
    want = ((cell % 16) // 2) * LANES + cell % 2 + jnp.where(cell < 16, LANES - 2, 0)
    picked = nt((place == want).astype(F32).astype(BF), f_ref[...]).astype(BF)
    mine[0] = picked[:16]
    mine[1] = picked[16:]

    folds = 1 + jnp.where(fold_e != lon, 1, 0) + jnp.where(fold_w != lon, 1, 0)
    pl.semaphore_wait(
        barrier,
        y_n + z_n + group - 3 + 2 + jnp.where(top, folds, 3) + jnp.where(bottom, 0, 3),
    )

    def send(src, dst, slot, a, b):
        return pltpu.make_async_remote_copy(
            src_ref=src, dst_ref=dst, send_sem=send_sem.at[slot], recv_sem=recv_sem.at[slot],
            device_id=(a, b), device_id_type=MESH,
        )

    low, high = f_ref.at[:, tile(0, 2)], f_ref.at[:, tile(ROWS - 2, 2)]
    above, below = xm.at[:, tile(ROWS + 2, 2)], xm.at[:, tile(0, 2)]

    @pl.when(top)
    def _():
        @pl.when(fold_e != lon)
        def _():
            send(mine.at[0], packs.at[3], 9, lat, fold_e).start()

        @pl.when(fold_w != lon)
        def _():
            send(mine.at[1], packs.at[2], 10, lat, fold_w).start()

        @pl.when(fold_e == lon)
        def _():
            packs[3] = mine[0]

        @pl.when(fold_w == lon)
        def _():
            packs[2] = mine[1]

    @pl.when(jnp.logical_not(bottom))
    def _():
        send(mine.at[0], packs.at[2], 2, lat - 1, east).start()
        send(mine.at[1], packs.at[3], 3, lat - 1, west).start()

    @pl.when(jnp.logical_not(top))
    def _():
        send(mine.at[0], packs.at[4], 4, lat + 1, east).start()
        send(mine.at[1], packs.at[5], 5, lat + 1, west).start()

    send(mine.at[0], packs.at[0], 0, lat, east).start()
    send(mine.at[1], packs.at[1], 1, lat, west).start()

    @pl.when(jnp.logical_not(top))
    def _():
        send(high, below, 7, lat + 1, lon).start()

    @pl.when(jnp.logical_not(bottom))
    def _():
        send(low, above, 8, lat - 1, lon).start()

    @pl.when(top)
    def _():
        send(high, above, 6, lat, mirror).start()

    @pl.when(bottom)
    def _():
        xm[:, tile(0, 2)] = jnp.zeros((128, 2 * LANES), BF)
        packs[4] = jnp.zeros((16, 128), BF)
        packs[5] = jnp.zeros((16, 128), BF)

    xm[:, tile(2, ROWS)] = f_ref[...]
    zero = jnp.zeros((CH, LANES), BF)
    for dr in range(3):
        at = slice(dr * CH, (dr + 1) * CH)
        ae[at, tile(dr, ROWS)] = f_ref[KX:, :]
        for r in range(RIM):
            if not dr <= r < dr + ROWS:
                am[at, tile(r)] = zero
                ae[at, tile(r)] = zero

    def select(cells, slot, tiles, base):
        k = lax.broadcasted_iota(jnp.int32, (cells, 1), 0)
        slot, row, j = slot(k // 16), (k % 16) // 2, k % 2
        row_to = jnp.where(slot < 2, row + 2, jnp.where(slot < 4, row + 10, row - 6))
        row_to = jnp.where((slot >= 2) & (slot < 4) & top, 17 - row, row_to)
        flipped = (slot >= 2) & (slot < 4) & top
        inner = (j + slot + jnp.where(flipped, 1, 0)) % 2 == 1
        lane_to = jnp.where(slot % 2 == 0, 0, LANES - 1)
        good = (slot < 2) | ((slot < 4) & (row_to < EXT)) | ((slot >= 4) & (row_to >= 0))
        tile_to = row_to - base + jnp.where(inner, 0, tiles)
        goal = jnp.where(good, tile_to * LANES + lane_to, -1)
        place = lax.broadcasted_iota(jnp.int32, (cells, 2 * tiles * LANES), 1)
        return (place == goal).astype(F32).astype(BF)

    loads[3].wait()
    loads[4].wait()
    gap = jnp.zeros((CH, KX - CIN), F32)
    k1 = [jnp.concatenate([w1_in[t].astype(F32), gap], axis=1) for t in range(9)]
    k2 = [w2_in[t].astype(F32) for t in range(9)]

    def square(k, pick):
        return jnp.concatenate(
            [jnp.concatenate([k[pick(a, b)] for b in range(3)], axis=1) for a in range(3)], axis=0
        )

    def plain(a, b):
        return 3 * a + b

    def turned(a, b):
        return 8 - 3 * a - b

    def swapped(a, b):
        return 3 * b + a

    def both(a, b):
        return 8 - 3 * b - a

    m = square(k1, plain)
    wa1[...] = m.astype(BF)
    wa1n[...] = jnp.where(top, square(k1, turned), m).astype(BF)
    wa2[...] = square(k2, plain).astype(BF)
    m = square(k2, both)
    tb2[...] = m.T.astype(BF)
    tb2n[...] = jnp.where(top, square(k2, swapped), m).T.astype(BF)
    m = square(k1, both)
    tb1[...] = m.T.astype(BF)
    tb1n[...] = jnp.where(top, square(k1, swapped), m).T.astype(BF)

    def landed(ref, slot):
        pltpu.make_async_copy(ref, ref, recv_sem.at[slot]).wait()

    lane = lax.broadcasted_iota(jnp.int32, (1, LANES), 1)

    def shifts(main, ghost):
        main, ghost = main.astype(F32), ghost.astype(F32)
        a = jnp.where(lane == 0, ghost, pltpu.roll(main, 1, 1)).astype(BF)
        b = jnp.where(lane == LANES - 1, ghost, pltpu.roll(main, LANES - 1, 1)).astype(BF)
        return a, b

    def spread(rows):
        for r in rows:
            t = tile(r)
            main, ghost, far = xm[:, t], xg[:, t], xo[:, t]
            a, b = shifts(main, ghost)
            ga = jnp.where(lane == LANES - 1, main, far)
            gb = jnp.where(lane == 0, main, far)
            for q, m, g in ((0, a, ga), (1, main, ghost), (2, b, gb)):
                d1m[q * KX : (q + 1) * KX, t] = m[:KX]
                d1g[q * KX : (q + 1) * KX, t] = g[:KX]
                d2m[q * CH : (q + 1) * CH, t] = m[KX:]
                d2g[q * CH : (q + 1) * CH, t] = g[KX:]

    def spread_results(h, g, base):
        for r in range(h[0].shape[1] // LANES):
            t, to = tile(r), tile(base + r)
            for ref, (main, ghost) in ((hd, h), (dad, g)):
                main = main[:, t]
                a, b = shifts(main, ghost[:, t])
                ref[0:CH, to] = a
                ref[CH : 2 * CH, to] = main
                ref[2 * CH :, to] = b

    def gated(a, grad, field, t):
        value, slope = gelu_parts(a)
        sea = field[CIN : CIN + 1, t].astype(F32)
        return (value * sea).astype(BF), (grad * (slope * sea)).astype(BF)

    inner = RIM - 2

    def lower(d1, d2, field):
        y = nn(wa1[...], d1[:, tile(0, RIM)])
        v = nn(tb2[...], d2[:, tile(0, RIM)])
        left = tuple(
            u[:CH, tile(inner)] + u[CH : 2 * CH, tile(inner + 1)] for u in (y, v)
        ) + (v[:CH, tile(inner + 1)],)
        h, g = gated(gather_rows(y, inner), gather_rows(v, inner), field, tile(1, inner))
        return h, g, left

    def upper(d1, d2, field, left):
        y = nn(wa1[...], d1[:, tile(RIM)])
        yn = nn(wa1n[...], d1[:, tile(RIM - 1, 3)])
        v = nn(tb2n[...], d2[:, tile(RIM, 2)])
        a = jnp.concatenate([left[0] + y[2 * CH :], gather_rows(yn, 1)], axis=1)
        grad = jnp.concatenate(
            [
                left[1] + v[2 * CH :, tile(0)],
                left[2] + v[CH : 2 * CH, tile(0)] + v[2 * CH :, tile(1)],
            ],
            axis=1,
        )
        return gated(a, grad, field, tile(RIM - 1, 2))

    pick_low = select(64, lambda s: jnp.where(s < 2, s, s + 2), RIM, 0)
    pick_high = select(32, lambda s: s + 2, 2, RIM)

    landed(packs.at[0], 0)
    landed(packs.at[1], 1)

    @pl.when(jnp.logical_not(bottom))
    def _():
        landed(below, 7)
        landed(packs.at[4], 4)
        landed(packs.at[5], 5)

    flat = jnp.concatenate([packs[s] for s in (0, 1, 4, 5)], axis=0)
    edge = tn(flat, pick_low).astype(BF)
    xg[:, tile(0, RIM)] = edge[:, tile(0, RIM)]
    xo[:, tile(0, RIM)] = edge[:, tile(RIM, RIM)]
    spread(range(RIM))
    hm, gm, left_m = lower(d1m, d2m, xm)
    hg, gg, left_g = lower(d1g, d2g, xg)
    for dr in range(3):
        am[dr * CH : (dr + 1) * CH, tile(dr, ROWS - 1)] = gm[:, tile(1, ROWS - 1)]
    spread_results((hm, hg), (gm, gg), 0)
    term2 = nt(ae[:, tile(0, inner)], hd[:, tile(0, inner)])
    term1 = nt(am[:, tile(0, inner - 1)], d1m[:, tile(1, inner - 1)])

    @pl.when(jnp.logical_not(top))
    def _():
        landed(above, 8)
        landed(packs.at[2], 2)
        landed(packs.at[3], 3)

    @pl.when(top)
    def _():
        landed(above, 6)

        @pl.when(fold_e != lon)
        def _():
            landed(packs.at[3], 9)

        @pl.when(fold_w != lon)
        def _():
            landed(packs.at[2], 10)

        back = lax.broadcasted_iota(jnp.int32, (LANES, LANES), 0)
        back = back + lax.broadcasted_iota(jnp.int32, (LANES, LANES), 1)
        back = (back == LANES - 1).astype(F32).astype(BF)
        first = nn(xm[:, tile(ROWS + 2)], back).astype(BF)
        second = nn(xm[:, tile(ROWS + 3)], back).astype(BF)
        xm[:, tile(ROWS + 2)] = second
        xm[:, tile(ROWS + 3)] = first

    flat = jnp.concatenate([packs[s] for s in (2, 3)], axis=0)
    edge = tn(flat, pick_high).astype(BF)
    xg[:, tile(RIM, 2)] = edge[:, tile(0, 2)]
    xo[:, tile(RIM, 2)] = edge[:, tile(2, 2)]
    spread((RIM, RIM + 1))
    hm, gm = upper(d1m, d2m, xm, left_m)
    hg, gg = upper(d1g, d2g, xg, left_g)
    for dr in range(3):
        am[dr * CH : (dr + 1) * CH, tile(dr + ROWS - 1)] = gm[:, tile(0)]
    spread_results((hm, hg), (gm, gg), inner)
    term2 = term2 + nt(ae[:, tile(inner, 2)], hd[:, tile(inner, 2)])
    term1 = term1 + nt(am[:, tile(inner - 1, 3)], d1m[:, tile(inner, 3)])
    terms = jnp.concatenate([term1, term2], axis=1).astype(BF)
    for t in range(TILES):
        a, b = t // 3, t % 3
        gbuf[chunk_of(t, group)] = terms[16 * a : 16 * a + 16, tile(b)]
    for t in range(TILES, CHUNKS * UNIT):
        gbuf[chunk_of(t, group)] = jnp.zeros((16, LANES), BF)

    def pass_on(src, dst, sems, p, a, b):
        pltpu.make_async_remote_copy(
            src_ref=src, dst_ref=dst, send_sem=sems[0].at[p], recv_sem=sems[1].at[p],
            device_id=(a, b), device_id_type=MESH,
        ).start()

    def done(ref, count, sem):
        some = ref.at[pl.ds(0, count)]
        pltpu.make_async_copy(some, some, sem).wait()

    def total(ref, p, count):
        acc = ref[p, 0].astype(F32)
        for i in range(1, count):
            acc = acc + ref[p, i].astype(F32)
        return acc.astype(BF)

    def only(test, always, f):
        if always:
            f()
        else:
            pl.when(test)(f)

    parts = -(-CHUNKS // group)
    count = [min(group, CHUNKS - p * group) for p in range(parts)]
    by_z = {j: at_z(j) for j in range(1, z_n)}
    by_y = {j: at_y(j) for j in range(1, y_n)}
    axes = ((z_n, z, by_z.get), (y_n, y, by_y.get))
    first = [axes[p % 2] for p in range(parts)]
    second = [axes[1 - p % 2] for p in range(parts)]

    by_x = {j: at_x(j) for j in range(1, group)}
    for p in range(parts):
        for j in range(1, group):
            to, a, b = by_x[j]
            only(
                to < count[p], count[p] == group,
                functools.partial(pass_on, gbuf.at[p, to], rbuf.at[p, me], sem_rs, p, a, b),
            )

    def hop(p, source, arrived, sem, held_as, axis, sems):
        length, at, peer = axis

        def go():
            done(source.at[p], arrived - 1, sem.at[p])
            held_as[p, at] = total(source, p, arrived)
            for j in far_first(length):
                pass_on(held_as.at[p, at], held_as.at[p, at], sems, p, *peer(j))

        only(me < count[p], count[p] == group, go)

    for p in range(parts):
        def own(p=p):
            rbuf[p, me] = gbuf[p, me]

        only(me < count[p], count[p] == group, own)
        hop(p, rbuf, group, sem_rs[1], ex1, first[p], sem_x1)
    sea = f_ref[CIN : CIN + 1, :].astype(F32)
    res = gather_rows(nn(wa2[...], hd[...]), ROWS) * sea
    for r in range(ROWS):
        flip[pl.ds(r, CH, stride=ROWS), :] = res[:, tile(r)]
    c_in[...] = flip[: CH * ROWS, :].reshape(CH, ROWS, LANES).astype(BF)
    stores = [pltpu.make_async_copy(c_in, out_ref, in_sem.at[0])]
    stores[0].start()

    for p in range(parts):
        hop(p, ex1, first[p][0], sem_x1[1], ex2, second[p], sem_x2)

    v = jnp.concatenate(
        [nn(tb1[...], dad[:, tile(0, RIM - 1)]), nn(tb1n[...], dad[:, tile(RIM - 1)])], axis=1
    )
    res = gather_rows(v, ROWS)
    for r in range(ROWS):
        flip[pl.ds(r, KX, stride=ROWS), :] = res[:, tile(r)]
    x_in[...] = flip[: CIN * ROWS, :].reshape(CIN, ROWS, LANES).astype(BF)
    stores.append(pltpu.make_async_copy(x_in, dx_ref, in_sem.at[1]))
    stores[1].start()

    everyone = (group, me, lambda j: by_x[j][1:])
    for p in range(parts):
        hop(p, ex2, second[p][0], sem_x2[1], obuf, everyone, sem_ag)
    for p in range(parts):
        if count[p] == group:
            done(obuf.at[p], group - 1, sem_ag[1].at[p])
        else:
            pl.when(me < count[p])(
                functools.partial(done, obuf.at[p], count[p] - 1, sem_ag[1].at[p])
            )
            pl.when(me >= count[p])(
                functools.partial(done, obuf.at[p], count[p], sem_ag[1].at[p])
            )
        n = count[p]
        move = pltpu.make_async_copy(obuf.at[p, pl.ds(0, n)], dw_ref.at[p, pl.ds(0, n)], out_sem.at[p])
        move.start()
        stores.append(move)

    def sent(ref, sem):
        pltpu.make_async_copy(ref, ref, sem).wait()

    sent(mine.at[0], send_sem.at[0])
    sent(mine.at[1], send_sem.at[1])

    @pl.when(jnp.logical_not(top))
    def _():
        sent(high, send_sem.at[7])
        sent(mine.at[0], send_sem.at[4])
        sent(mine.at[1], send_sem.at[5])

    @pl.when(top)
    def _():
        sent(high, send_sem.at[6])

        @pl.when(fold_e != lon)
        def _():
            sent(mine.at[0], send_sem.at[9])

        @pl.when(fold_w != lon)
        def _():
            sent(mine.at[1], send_sem.at[10])

    @pl.when(jnp.logical_not(bottom))
    def _():
        sent(low, send_sem.at[8])
        sent(mine.at[0], send_sem.at[2])
        sent(mine.at[1], send_sem.at[3])

    for p in range(parts):
        n = count[p]
        if n == group:
            done(gbuf.at[p], group - 1, sem_rs[0].at[p])
        else:
            pl.when(me < n)(functools.partial(done, gbuf.at[p], n - 1, sem_rs[0].at[p]))
            pl.when(me >= n)(functools.partial(done, gbuf.at[p], n, sem_rs[0].at[p]))

        def drain(p=p):
            done(ex1.at[p], first[p][0] - 1, sem_x1[0].at[p])
            done(ex2.at[p], second[p][0] - 1, sem_x2[0].at[p])
            done(rbuf.at[p], group - 1, sem_ag[0].at[p])

        only(me < n, n == group, drain)
    for store in stores:
        store.wait()


def finish(
    factor, parts, group,
    out_in, dx_in, dw_in, out_ref, dx_ref, dw1_ref, dw2_ref,
    tiles, dw1, dw2, get_sem, put_sem,
):
    get = pltpu.make_async_copy(dw_in, tiles, get_sem)
    puts = [
        pltpu.make_async_copy(src, dst, put_sem.at[i])
        for i, (src, dst) in enumerate(
            ((dw1, dw1_ref), (dw2, dw2_ref), (out_in, out_ref), (dx_in, dx_ref))
        )
    ]
    get.start()
    puts[2].start()
    puts[3].start()
    get.wait()
    for dr in range(3):
        grads = jnp.concatenate(
            [
                jnp.concatenate(
                    [tiles[chunk_of(t, group)] for t in range(3 * a, 3 * a + 3)], axis=1
                )
                for a in range(3 * dr, 3 * dr + 3)
            ],
            axis=0,
        ).astype(F32) * factor
        for dc in range(3):
            dw1[3 * dr + dc] = grads[:, dc * KX : dc * KX + CIN]
            dw2[3 * dr + dc] = grads[:, 3 * KX + dc * CH : 3 * KX + (dc + 1) * CH]
    puts[0].start()
    puts[1].start()
    for put in puts:
        put.wait()


def body(dims, *inputs):
    xl_n, z_n, xh_n, y_n, c_n = dims
    group = xl_n * xh_n * c_n
    parts = -(-CHUNKS // group)
    wide, slim, ring = EXT * LANES, RIM * LANES, max(y_n, z_n)
    anywhere = pl.BlockSpec(memory_space=pl.ANY)
    hbm = pl.BlockSpec(memory_space=pltpu.HBM)

    def held(*shape):
        return pltpu.VMEM(shape, BF)

    fields_like = (
        jax.ShapeDtypeStruct((CH, ROWS, LANES), BF),
        jax.ShapeDtypeStruct((CIN, ROWS, LANES), BF),
    )
    out, dx, dw = pl.pallas_call(
        functools.partial(kernel, dims),
        out_shape=fields_like + (jax.ShapeDtypeStruct((parts, group, TALL, LANES), BF),),
        in_specs=[hbm] * 5,
        out_specs=(anywhere,) * 3,
        scratch_shapes=[
            held(CIN, ROWS, LANES), pltpu.VMEM((ROWS, LANES), jnp.int32),
            held(9, CH, CIN), held(9, CH, CH), held(CH, ROWS, LANES),
            pltpu.VMEM(((KX + CH) * ROWS, LANES), F32), held(KX + CH, ROWS * LANES),
            held(3 * CH, 3 * KX), held(3 * CH, 3 * KX), held(3 * CH, 3 * CH),
            held(3 * CH, 3 * CH), held(3 * CH, 3 * CH), held(3 * KX, 3 * CH), held(3 * KX, 3 * CH),
            held(128, wide), held(128, wide), held(128, wide), held(6, 16, 128), held(2, 16, 128),
            held(3 * KX, wide), held(3 * KX, wide), held(3 * CH, wide), held(3 * CH, wide),
            held(3 * CH, slim), held(3 * CH, slim), held(3 * CH, slim), held(3 * CH, slim),
            held(parts, group, TALL, LANES), held(parts, group, TALL, LANES),
            held(parts, ring, TALL, LANES), held(parts, ring, TALL, LANES),
            held(parts, group, TALL, LANES),
            pltpu.SemaphoreType.DMA((5,)), pltpu.SemaphoreType.DMA((parts,)),
            pltpu.SemaphoreType.DMA((11,)), pltpu.SemaphoreType.DMA((11,)),
        ] + [pltpu.SemaphoreType.DMA((parts,))] * 8,
        compiler_params=pltpu.CompilerParams(
            collective_id=0, has_side_effects=True, vmem_limit_bytes=24 * 1024 * 1024
        ),
    )(*(pltpu.with_memory_space_constraint(v, pltpu.HBM) for v in inputs))
    factor = 1.0 / math.sqrt(ROWS * LANES * xl_n * z_n * xh_n * y_n * c_n)
    return pl.pallas_call(
        functools.partial(finish, factor, parts, group),
        out_shape=fields_like + (
            jax.ShapeDtypeStruct((9, CH, CIN), F32),
            jax.ShapeDtypeStruct((9, CH, CH), F32),
        ),
        in_specs=[anywhere] * 3,
        out_specs=(hbm,) * 4,
        scratch_shapes=[
            held(parts, group, TALL, LANES),
            pltpu.VMEM((9, CH, CIN), F32), pltpu.VMEM((9, CH, CH), F32),
            pltpu.SemaphoreType.DMA, pltpu.SemaphoreType.DMA((4,)),
        ],
        compiler_params=pltpu.CompilerParams(vmem_limit_bytes=8 * 1024 * 1024),
    )(out, dx, dw)


def solution(mesh):
    in_specs = (P(None, "lat", "lon"), P("lat", "lon"), P(), P(), P(None, "lat", "lon"))
    out_specs = (P(None, "lat", "lon"), P(None, "lat", "lon"), P(), P())
    nlat, nlon = mesh.shape["lat"], mesh.shape["lon"]
    x_hi = 2 if nlon > 4 else 1
    dims = (2, nlat // 2, x_hi, nlon // (2 * x_hi), 2)
    run = functools.partial(body, dims)
    return jax.shard_map(run, mesh=mesh, in_specs=in_specs, out_specs=out_specs, check_vma=False)
```

```python
import functools
import math

import jax
import jax.numpy as jnp
from jax import lax
from jax.experimental import pallas as pl
from jax.experimental.pallas import tpu as pltpu
from jax.sharding import PartitionSpec as P

MESH = pl.DeviceIdType.MESH
BF = jnp.bfloat16
F32 = jnp.float32
CIN, CH, KX = 75, 48, 80
ROWS, LANES = 8, 128
EXT = ROWS + 4
RIM = ROWS + 2
TILES = 27
UNIT = 2
CHUNKS = -(-TILES // UNIT)
TALL = 16 * UNIT


def nn(a, b):
    return lax.dot_general(a, b, (((1,), (0,)), ((), ())), preferred_element_type=F32)


def nt(a, b):
    return lax.dot_general(a, b, (((1,), (1,)), ((), ())), preferred_element_type=F32)


def tn(a, b):
    return lax.dot_general(a, b, (((0,), (0,)), ((), ())), preferred_element_type=F32)


def gelu_parts(a):
    coeff = 0.7978845608
    inner = coeff * (a + 0.044715 * a * a * a)
    tval = jnp.tanh(inner)
    value = 0.5 * a * (1.0 + tval)
    slope = 0.5 * (1.0 + tval) + 0.5 * a * (1.0 - tval * tval) * coeff * (1.0 + 0.134145 * a * a)
    return (value, slope)


def tile(r, count=1):
    return slice(r * LANES, (r + count) * LANES)


def gather_rows(y, rows):
    n = rows * LANES
    c = y.shape[0] // 3
    return y[:c, :n] + y[c : 2 * c, LANES : LANES + n] + y[2 * c :, 2 * LANES : 2 * LANES + n]


def chunk_of(t, group):
    c, row = t // UNIT, t % UNIT * 16
    return c // group, c % group, slice(row, row + 16)


def far_first(n):
    return sorted(range(1, n), key=lambda j: -min(j, n - j))


def kernel(
    dims,
    x_hbm, m_hbm, w1_hbm, w2_hbm, c_hbm,
    out_ref, dx_ref, dw_ref,
    x_in, m_in, w1_in, w2_in, c_in, flip, f_ref,
    wa1, wa1n, wa2, tb2, tb2n, tb1, tb1n,
    xm, xg, xo, packs, mine, d1m, d1g, d2m, d2g, hd, dad, am, ae,
    gbuf, rbuf, ex1, ex2, obuf,
    in_sem, out_sem, send_sem, recv_sem, *red,
):
    sem_rs, sem_x1, sem_x2, sem_ag = red[0:2], red[2:4], red[4:6], red[6:8]
    xl_n, z_n, xh_n, y_n, c_n = dims
    nlat, nlon, group = xl_n * z_n, xh_n * y_n * c_n, xl_n * xh_n * c_n
    lat, lon = lax.axis_index("lat"), lax.axis_index("lon")
    xl, z = lat // z_n, lat % z_n
    xh, y, core = lon // (y_n * c_n), (lon // c_n) % y_n, lon % c_n
    me = (xl * xh_n + xh) * c_n + core
    top, bottom = lat == nlat - 1, lat == 0
    east, west = lax.rem(lon + 1, nlon), lax.rem(lon + nlon - 1, nlon)
    mirror = nlon - 1 - lon
    fold_e = lax.rem(2 * nlon - 2 - lon, nlon)
    fold_w = lax.rem(nlon - lon, nlon)

    def at_z(j):
        to = lax.rem(z + j, z_n)
        return xl * z_n + to, lon

    def at_y(j):
        to = lax.rem(y + j, y_n)
        return lat, (xh * y_n + to) * c_n + core

    def at_x(j):
        to = lax.rem(me + j, group)
        a, b, c = to // (xh_n * c_n), (to // c_n) % xh_n, to % c_n
        return to, a * z_n + z, (b * y_n + y) * c_n + c

    loads = [
        pltpu.make_async_copy(src, dst, in_sem.at[i])
        for i, (src, dst) in enumerate(
            ((x_hbm, x_in), (m_hbm, m_in), (c_hbm, c_in), (w1_hbm, w1_in), (w2_hbm, w2_in))
        )
    ]
    for load in loads:
        load.start()

    barrier = pltpu.get_barrier_semaphore()

    def greet(a, b):
        pl.semaphore_signal(barrier, inc=1, device_id=(a, b), device_id_type=MESH)

    @pl.when(top)
    def _():
        greet(lat, mirror)

        @pl.when(fold_e != lon)
        def _():
            greet(lat, fold_e)

        @pl.when(fold_w != lon)
        def _():
            greet(lat, fold_w)

    @pl.when(jnp.logical_not(top))
    def _():
        greet(lat + 1, east)
        greet(lat + 1, west)
        greet(lat + 1, lon)

    @pl.when(jnp.logical_not(bottom))
    def _():
        greet(lat - 1, east)
        greet(lat - 1, west)
        greet(lat - 1, lon)

    greet(lat, east)
    greet(lat, west)

    for j in far_first(y_n):
        greet(*at_y(j))
    for j in far_first(z_n):
        greet(*at_z(j))
    for j in range(1, group):
        greet(*at_x(j)[1:])

    for load in loads[:3]:
        load.wait()
    sea8 = m_in[...].astype(F32)
    flip[: CIN * ROWS, :] = x_in[...].astype(F32).reshape(CIN * ROWS, LANES)
    flip[CIN * ROWS : (CIN + 1) * ROWS, :] = sea8
    flip[(CIN + 1) * ROWS : KX * ROWS, :] = jnp.zeros(((KX - CIN - 1) * ROWS, LANES), F32)
    flip[KX * ROWS :, :] = (c_in[...].astype(F32) * sea8[None]).reshape(CH * ROWS, LANES)
    for r in range(ROWS):
        f_ref[:, tile(r)] = flip[pl.ds(r, KX + CH, stride=ROWS), :].astype(BF)

    cell = lax.broadcasted_iota(jnp.int32, (32, ROWS * LANES), 0)
    place = lax.broadcasted_iota(jnp.int32, (32, ROWS * LANES), 1)
    want = ((cell % 16) // 2) * LANES + cell % 2 + jnp.where(cell < 16, LANES - 2, 0)
    picked = nt((place == want).astype(F32).astype(BF), f_ref[...]).astype(BF)
    mine[0] = picked[:16]
    mine[1] = picked[16:]

    folds = 1 + jnp.where(fold_e != lon, 1, 0) + jnp.where(fold_w != lon, 1, 0)
    pl.semaphore_wait(
        barrier,
        y_n + z_n + group - 3 + 2 + jnp.where(top, folds, 3) + jnp.where(bottom, 0, 3),
    )

    def send(src, dst, slot, a, b):
        return pltpu.make_async_remote_copy(
            src_ref=src, dst_ref=dst, send_sem=send_sem.at[slot], recv_sem=recv_sem.at[slot],
            device_id=(a, b), device_id_type=MESH,
        )

    low, high = f_ref.at[:, tile(0, 2)], f_ref.at[:, tile(ROWS - 2, 2)]
    above, below = xm.at[:, tile(ROWS + 2, 2)], xm.at[:, tile(0, 2)]

    @pl.when(top)
    def _():
        @pl.when(fold_e != lon)
        def _():
            send(mine.at[0], packs.at[3], 9, lat, fold_e).start()

        @pl.when(fold_w != lon)
        def _():
            send(mine.at[1], packs.at[2], 10, lat, fold_w).start()

        @pl.when(fold_e == lon)
        def _():
            packs[3] = mine[0]

        @pl.when(fold_w == lon)
        def _():
            packs[2] = mine[1]

    @pl.when(jnp.logical_not(bottom))
    def _():
        send(mine.at[0], packs.at[2], 2, lat - 1, east).start()
        send(mine.at[1], packs.at[3], 3, lat - 1, west).start()

    @pl.when(jnp.logical_not(top))
    def _():
        send(mine.at[0], packs.at[4], 4, lat + 1, east).start()
        send(mine.at[1], packs.at[5], 5, lat + 1, west).start()

    send(mine.at[0], packs.at[0], 0, lat, east).start()
    send(mine.at[1], packs.at[1], 1, lat, west).start()

    @pl.when(jnp.logical_not(top))
    def _():
        send(high, below, 7, lat + 1, lon).start()

    @pl.when(jnp.logical_not(bottom))
    def _():
        send(low, above, 8, lat - 1, lon).start()

    @pl.when(top)
    def _():
        send(high, above, 6, lat, mirror).start()

    @pl.when(bottom)
    def _():
        xm[:, tile(0, 2)] = jnp.zeros((128, 2 * LANES), BF)
        packs[4] = jnp.zeros((16, 128), BF)
        packs[5] = jnp.zeros((16, 128), BF)

    xm[:, tile(2, ROWS)] = f_ref[...]
    zero = jnp.zeros((CH, LANES), BF)
    for dr in range(3):
        at = slice(dr * CH, (dr + 1) * CH)
        ae[at, tile(dr, ROWS)] = f_ref[KX:, :]
        for r in range(RIM):
            if not dr <= r < dr + ROWS:
                am[at, tile(r)] = zero
                ae[at, tile(r)] = zero

    def select(cells, slot, tiles, base):
        k = lax.broadcasted_iota(jnp.int32, (cells, 1), 0)
        slot, row, j = slot(k // 16), (k % 16) // 2, k % 2
        row_to = jnp.where(slot < 2, row + 2, jnp.where(slot < 4, row + 10, row - 6))
        row_to = jnp.where((slot >= 2) & (slot < 4) & top, 17 - row, row_to)
        flipped = (slot >= 2) & (slot < 4) & top
        inner = (j + slot + jnp.where(flipped, 1, 0)) % 2 == 1
        lane_to = jnp.where(slot % 2 == 0, 0, LANES - 1)
        good = (slot < 2) | ((slot < 4) & (row_to < EXT)) | ((slot >= 4) & (row_to >= 0))
        tile_to = row_to - base + jnp.where(inner, 0, tiles)
        goal = jnp.where(good, tile_to * LANES + lane_to, -1)
        place = lax.broadcasted_iota(jnp.int32, (cells, 2 * tiles * LANES), 1)
        return (place == goal).astype(F32).astype(BF)

    loads[3].wait()
    loads[4].wait()
    gap = jnp.zeros((CH, KX - CIN), F32)
    k1 = [jnp.concatenate([w1_in[t].astype(F32), gap], axis=1) for t in range(9)]
    k2 = [w2_in[t].astype(F32) for t in range(9)]

    def square(k, pick):
        return jnp.concatenate(
            [jnp.concatenate([k[pick(a, b)] for b in range(3)], axis=1) for a in range(3)], axis=0
        )

    def plain(a, b):
        return 3 * a + b

    def turned(a, b):
        return 8 - 3 * a - b

    def swapped(a, b):
        return 3 * b + a

    def both(a, b):
        return 8 - 3 * b - a

    m = square(k1, plain)
    wa1[...] = m.astype(BF)
    wa1n[...] = jnp.where(top, square(k1, turned), m).astype(BF)
    wa2[...] = square(k2, plain).astype(BF)
    m = square(k2, both)
    tb2[...] = m.T.astype(BF)
    tb2n[...] = jnp.where(top, square(k2, swapped), m).T.astype(BF)
    m = square(k1, both)
    tb1[...] = m.T.astype(BF)
    tb1n[...] = jnp.where(top, square(k1, swapped), m).T.astype(BF)

    def landed(ref, slot):
        pltpu.make_async_copy(ref, ref, recv_sem.at[slot]).wait()

    lane = lax.broadcasted_iota(jnp.int32, (1, LANES), 1)

    def shifts(main, ghost):
        main, ghost = main.astype(F32), ghost.astype(F32)
        a = jnp.where(lane == 0, ghost, pltpu.roll(main, 1, 1)).astype(BF)
        b = jnp.where(lane == LANES - 1, ghost, pltpu.roll(main, LANES - 1, 1)).astype(BF)
        return a, b

    def spread(rows):
        for r in rows:
            t = tile(r)
            main, ghost, far = xm[:, t], xg[:, t], xo[:, t]
            a, b = shifts(main, ghost)
            ga = jnp.where(lane == LANES - 1, main, far)
            gb = jnp.where(lane == 0, main, far)
            for q, m, g in ((0, a, ga), (1, main, ghost), (2, b, gb)):
                d1m[q * KX : (q + 1) * KX, t] = m[:KX]
                d1g[q * KX : (q + 1) * KX, t] = g[:KX]
                d2m[q * CH : (q + 1) * CH, t] = m[KX:]
                d2g[q * CH : (q + 1) * CH, t] = g[KX:]

    def spread_results(h, g, base):
        for r in range(h[0].shape[1] // LANES):
            t, to = tile(r), tile(base + r)
            for ref, (main, ghost) in ((hd, h), (dad, g)):
                main = main[:, t]
                a, b = shifts(main, ghost[:, t])
                ref[0:CH, to] = a
                ref[CH : 2 * CH, to] = main
                ref[2 * CH :, to] = b

    def gated(a, grad, field, t):
        value, slope = gelu_parts(a)
        sea = field[CIN : CIN + 1, t].astype(F32)
        return (value * sea).astype(BF), (grad * (slope * sea)).astype(BF)

    inner = RIM - 2

    def lower(d1, d2, field):
        y = nn(wa1[...], d1[:, tile(0, RIM)])
        v = nn(tb2[...], d2[:, tile(0, RIM)])
        left = tuple(
            u[:CH, tile(inner)] + u[CH : 2 * CH, tile(inner + 1)] for u in (y, v)
        ) + (v[:CH, tile(inner + 1)],)
        h, g = gated(gather_rows(y, inner), gather_rows(v, inner), field, tile(1, inner))
        return h, g, left

    def upper(d1, d2, field, left):
        y = nn(wa1[...], d1[:, tile(RIM)])
        yn = nn(wa1n[...], d1[:, tile(RIM - 1, 3)])
        v = nn(tb2n[...], d2[:, tile(RIM, 2)])
        a = jnp.concatenate([left[0] + y[2 * CH :], gather_rows(yn, 1)], axis=1)
        grad = jnp.concatenate(
            [
                left[1] + v[2 * CH :, tile(0)],
                left[2] + v[CH : 2 * CH, tile(0)] + v[2 * CH :, tile(1)],
            ],
            axis=1,
        )
        return gated(a, grad, field, tile(RIM - 1, 2))

    pick_low = select(64, lambda s: jnp.where(s < 2, s, s + 2), RIM, 0)
    pick_high = select(32, lambda s: s + 2, 2, RIM)

    landed(packs.at[0], 0)
    landed(packs.at[1], 1)

    @pl.when(jnp.logical_not(bottom))
    def _():
        landed(below, 7)
        landed(packs.at[4], 4)
        landed(packs.at[5], 5)

    flat = jnp.concatenate([packs[s] for s in (0, 1, 4, 5)], axis=0)
    edge = tn(flat, pick_low).astype(BF)
    xg[:, tile(0, RIM)] = edge[:, tile(0, RIM)]
    xo[:, tile(0, RIM)] = edge[:, tile(RIM, RIM)]
    spread(range(RIM))
    hm, gm, left_m = lower(d1m, d2m, xm)
    hg, gg, left_g = lower(d1g, d2g, xg)
    for dr in range(3):
        am[dr * CH : (dr + 1) * CH, tile(dr, ROWS - 1)] = gm[:, tile(1, ROWS - 1)]
    spread_results((hm, hg), (gm, gg), 0)
    term2 = nt(ae[:, tile(0, inner)], hd[:, tile(0, inner)])
    term1 = nt(am[:, tile(0, inner - 1)], d1m[:, tile(1, inner - 1)])

    @pl.when(jnp.logical_not(top))
    def _():
        landed(above, 8)
        landed(packs.at[2], 2)
        landed(packs.at[3], 3)

    @pl.when(top)
    def _():
        landed(above, 6)

        @pl.when(fold_e != lon)
        def _():
            landed(packs.at[3], 9)

        @pl.when(fold_w != lon)
        def _():
            landed(packs.at[2], 10)

        back = lax.broadcasted_iota(jnp.int32, (LANES, LANES), 0)
        back = back + lax.broadcasted_iota(jnp.int32, (LANES, LANES), 1)
        back = (back == LANES - 1).astype(F32).astype(BF)
        first = nn(xm[:, tile(ROWS + 2)], back).astype(BF)
        second = nn(xm[:, tile(ROWS + 3)], back).astype(BF)
        xm[:, tile(ROWS + 2)] = second
        xm[:, tile(ROWS + 3)] = first

    flat = jnp.concatenate([packs[s] for s in (2, 3)], axis=0)
    edge = tn(flat, pick_high).astype(BF)
    xg[:, tile(RIM, 2)] = edge[:, tile(0, 2)]
    xo[:, tile(RIM, 2)] = edge[:, tile(2, 2)]
    spread((RIM, RIM + 1))
    hm, gm = upper(d1m, d2m, xm, left_m)
    hg, gg = upper(d1g, d2g, xg, left_g)
    for dr in range(3):
        am[dr * CH : (dr + 1) * CH, tile(dr + ROWS - 1)] = gm[:, tile(0)]
    spread_results((hm, hg), (gm, gg), inner)
    term2 = term2 + nt(ae[:, tile(inner, 2)], hd[:, tile(inner, 2)])
    term1 = term1 + nt(am[:, tile(inner - 1, 3)], d1m[:, tile(inner, 3)])
    terms = jnp.concatenate([term1, term2], axis=1).astype(BF)
    for t in range(TILES):
        a, b = t // 3, t % 3
        gbuf[chunk_of(t, group)] = terms[16 * a : 16 * a + 16, tile(b)]
    for t in range(TILES, CHUNKS * UNIT):
        gbuf[chunk_of(t, group)] = jnp.zeros((16, LANES), BF)

    def pass_on(src, dst, sems, p, a, b):
        pltpu.make_async_remote_copy(
            src_ref=src, dst_ref=dst, send_sem=sems[0].at[p], recv_sem=sems[1].at[p],
            device_id=(a, b), device_id_type=MESH,
        ).start()

    def done(ref, count, sem):
        some = ref.at[pl.ds(0, count)]
        pltpu.make_async_copy(some, some, sem).wait()

    def total(ref, p, count):
        acc = ref[p, 0].astype(F32)
        for i in range(1, count):
            acc = acc + ref[p, i].astype(F32)
        return acc.astype(BF)

    def only(test, always, f):
        if always:
            f()
        else:
            pl.when(test)(f)

    parts = -(-CHUNKS // group)
    count = [min(group, CHUNKS - p * group) for p in range(parts)]
    by_z = {j: at_z(j) for j in range(1, z_n)}
    by_y = {j: at_y(j) for j in range(1, y_n)}
    axes = ((z_n, z, by_z.get), (y_n, y, by_y.get))
    first = [axes[1 - p % 2] for p in range(parts)]
    second = [axes[p % 2] for p in range(parts)]

    by_x = {j: at_x(j) for j in range(1, group)}
    for p in range(parts):
        for j in range(1, group):
            to, a, b = by_x[j]
            only(
                to < count[p], count[p] == group,
                functools.partial(pass_on, gbuf.at[p, to], rbuf.at[p, me], sem_rs, p, a, b),
            )

    def hop(p, source, arrived, sem, held_as, axis, sems):
        length, at, peer = axis

        def go():
            done(source.at[p], arrived - 1, sem.at[p])
            held_as[p, at] = total(source, p, arrived)
            for j in far_first(length):
                pass_on(held_as.at[p, at], held_as.at[p, at], sems, p, *peer(j))

        only(me < count[p], count[p] == group, go)

    for p in range(parts):
        def own(p=p):
            rbuf[p, me] = gbuf[p, me]

        only(me < count[p], count[p] == group, own)
        hop(p, rbuf, group, sem_rs[1], ex1, first[p], sem_x1)
    sea = f_ref[CIN : CIN + 1, :].astype(F32)
    res = gather_rows(nn(wa2[...], hd[...]), ROWS) * sea
    for r in range(ROWS):
        flip[pl.ds(r, CH, stride=ROWS), :] = res[:, tile(r)]
    c_in[...] = flip[: CH * ROWS, :].reshape(CH, ROWS, LANES).astype(BF)
    stores = [pltpu.make_async_copy(c_in, out_ref, in_sem.at[0])]
    stores[0].start()

    for p in range(parts):
        hop(p, ex1, first[p][0], sem_x1[1], ex2, second[p], sem_x2)

    v = jnp.concatenate(
        [nn(tb1[...], dad[:, tile(0, RIM - 1)]), nn(tb1n[...], dad[:, tile(RIM - 1)])], axis=1
    )
    res = gather_rows(v, ROWS)
    for r in range(ROWS):
        flip[pl.ds(r, KX, stride=ROWS), :] = res[:, tile(r)]
    x_in[...] = flip[: CIN * ROWS, :].reshape(CIN, ROWS, LANES).astype(BF)
    stores.append(pltpu.make_async_copy(x_in, dx_ref, in_sem.at[1]))
    stores[1].start()

    everyone = (group, me, lambda j: by_x[j][1:])
    for p in range(parts):
        hop(p, ex2, second[p][0], sem_x2[1], obuf, everyone, sem_ag)
    for p in range(parts):
        if count[p] == group:
            done(obuf.at[p], group - 1, sem_ag[1].at[p])
        else:
            pl.when(me < count[p])(
                functools.partial(done, obuf.at[p], count[p] - 1, sem_ag[1].at[p])
            )
            pl.when(me >= count[p])(
                functools.partial(done, obuf.at[p], count[p], sem_ag[1].at[p])
            )
        n = count[p]
        move = pltpu.make_async_copy(obuf.at[p, pl.ds(0, n)], dw_ref.at[p, pl.ds(0, n)], out_sem.at[p])
        move.start()
        stores.append(move)

    def sent(ref, sem):
        pltpu.make_async_copy(ref, ref, sem).wait()

    sent(mine.at[0], send_sem.at[0])
    sent(mine.at[1], send_sem.at[1])

    @pl.when(jnp.logical_not(top))
    def _():
        sent(high, send_sem.at[7])
        sent(mine.at[0], send_sem.at[4])
        sent(mine.at[1], send_sem.at[5])

    @pl.when(top)
    def _():
        sent(high, send_sem.at[6])

        @pl.when(fold_e != lon)
        def _():
            sent(mine.at[0], send_sem.at[9])

        @pl.when(fold_w != lon)
        def _():
            sent(mine.at[1], send_sem.at[10])

    @pl.when(jnp.logical_not(bottom))
    def _():
        sent(low, send_sem.at[8])
        sent(mine.at[0], send_sem.at[2])
        sent(mine.at[1], send_sem.at[3])

    for p in range(parts):
        n = count[p]
        if n == group:
            done(gbuf.at[p], group - 1, sem_rs[0].at[p])
        else:
            pl.when(me < n)(functools.partial(done, gbuf.at[p], n - 1, sem_rs[0].at[p]))
            pl.when(me >= n)(functools.partial(done, gbuf.at[p], n, sem_rs[0].at[p]))

        def drain(p=p):
            done(ex1.at[p], first[p][0] - 1, sem_x1[0].at[p])
            done(ex2.at[p], second[p][0] - 1, sem_x2[0].at[p])
            done(rbuf.at[p], group - 1, sem_ag[0].at[p])

        only(me < n, n == group, drain)
    for store in stores:
        store.wait()


def finish(
    factor, parts, group,
    out_in, dx_in, dw_in, out_ref, dx_ref, dw1_ref, dw2_ref,
    tiles, dw1, dw2, get_sem, put_sem,
):
    get = pltpu.make_async_copy(dw_in, tiles, get_sem)
    puts = [
        pltpu.make_async_copy(src, dst, put_sem.at[i])
        for i, (src, dst) in enumerate(
            ((dw1, dw1_ref), (dw2, dw2_ref), (out_in, out_ref), (dx_in, dx_ref))
        )
    ]
    get.start()
    puts[2].start()
    puts[3].start()
    get.wait()
    for dr in range(3):
        grads = jnp.concatenate(
            [
                jnp.concatenate(
                    [tiles[chunk_of(t, group)] for t in range(3 * a, 3 * a + 3)], axis=1
                )
                for a in range(3 * dr, 3 * dr + 3)
            ],
            axis=0,
        ).astype(F32) * factor
        for dc in range(3):
            dw1[3 * dr + dc] = grads[:, dc * KX : dc * KX + CIN]
            dw2[3 * dr + dc] = grads[:, 3 * KX + dc * CH : 3 * KX + (dc + 1) * CH]
    puts[0].start()
    puts[1].start()
    for put in puts:
        put.wait()


def body(dims, *inputs):
    xl_n, z_n, xh_n, y_n, c_n = dims
    group = xl_n * xh_n * c_n
    parts = -(-CHUNKS // group)
    wide, slim, ring = EXT * LANES, RIM * LANES, max(y_n, z_n)
    anywhere = pl.BlockSpec(memory_space=pl.ANY)
    hbm = pl.BlockSpec(memory_space=pltpu.HBM)

    def held(*shape):
        return pltpu.VMEM(shape, BF)

    fields_like = (
        jax.ShapeDtypeStruct((CH, ROWS, LANES), BF),
        jax.ShapeDtypeStruct((CIN, ROWS, LANES), BF),
    )
    out, dx, dw = pl.pallas_call(
        functools.partial(kernel, dims),
        out_shape=fields_like + (jax.ShapeDtypeStruct((parts, group, TALL, LANES), BF),),
        in_specs=[hbm] * 5,
        out_specs=(anywhere,) * 3,
        scratch_shapes=[
            held(CIN, ROWS, LANES), pltpu.VMEM((ROWS, LANES), jnp.int32),
            held(9, CH, CIN), held(9, CH, CH), held(CH, ROWS, LANES),
            pltpu.VMEM(((KX + CH) * ROWS, LANES), F32), held(KX + CH, ROWS * LANES),
            held(3 * CH, 3 * KX), held(3 * CH, 3 * KX), held(3 * CH, 3 * CH),
            held(3 * CH, 3 * CH), held(3 * CH, 3 * CH), held(3 * KX, 3 * CH), held(3 * KX, 3 * CH),
            held(128, wide), held(128, wide), held(128, wide), held(6, 16, 128), held(2, 16, 128),
            held(3 * KX, wide), held(3 * KX, wide), held(3 * CH, wide), held(3 * CH, wide),
            held(3 * CH, slim), held(3 * CH, slim), held(3 * CH, slim), held(3 * CH, slim),
            held(parts, group, TALL, LANES), held(parts, group, TALL, LANES),
            held(parts, ring, TALL, LANES), held(parts, ring, TALL, LANES),
            held(parts, group, TALL, LANES),
            pltpu.SemaphoreType.DMA((5,)), pltpu.SemaphoreType.DMA((parts,)),
            pltpu.SemaphoreType.DMA((11,)), pltpu.SemaphoreType.DMA((11,)),
        ] + [pltpu.SemaphoreType.DMA((parts,))] * 8,
        compiler_params=pltpu.CompilerParams(
            collective_id=0, has_side_effects=True, vmem_limit_bytes=24 * 1024 * 1024
        ),
    )(*(pltpu.with_memory_space_constraint(v, pltpu.HBM) for v in inputs))
    factor = 1.0 / math.sqrt(ROWS * LANES * xl_n * z_n * xh_n * y_n * c_n)
    return pl.pallas_call(
        functools.partial(finish, factor, parts, group),
        out_shape=fields_like + (
            jax.ShapeDtypeStruct((9, CH, CIN), F32),
            jax.ShapeDtypeStruct((9, CH, CH), F32),
        ),
        in_specs=[anywhere] * 3,
        out_specs=(hbm,) * 4,
        scratch_shapes=[
            held(parts, group, TALL, LANES),
            pltpu.VMEM((9, CH, CIN), F32), pltpu.VMEM((9, CH, CH), F32),
            pltpu.SemaphoreType.DMA, pltpu.SemaphoreType.DMA((4,)),
        ],
        compiler_params=pltpu.CompilerParams(vmem_limit_bytes=8 * 1024 * 1024),
    )(out, dx, dw)


def solution(mesh):
    in_specs = (P(None, "lat", "lon"), P("lat", "lon"), P(), P(), P(None, "lat", "lon"))
    out_specs = (P(None, "lat", "lon"), P(None, "lat", "lon"), P(), P())
    nlat, nlon = mesh.shape["lat"], mesh.shape["lon"]
    x_hi = 2 if nlon > 4 else 1
    dims = (2, nlat // 2, x_hi, nlon // (2 * x_hi), 2)
    run = functools.partial(body, dims)
    return jax.shard_map(run, mesh=mesh, in_specs=in_specs, out_specs=out_specs, check_vma=False)
```
